128 devices in a mesh: rep: 4 (over y_lo, core), sp: 32 (over x, y_hi, z).
Axes of the slice: x: 4, y: 4 (y_hi: 2, y_lo: 2; y = y_hi * 2 + y_lo), z: 4, core: 2. Of those that a mesh axis runs over, the one named last changes fastest.
Arguments:
- field: bfloat16 [4, 2, 36, 256, 1024], P('rep', None, None, 'sp'), may hold values from -6 to 6
- cotangent: bfloat16 [4, 2, 36, 256, 1024], P('rep', None, None, 'sp'), may hold values from -6 to 6
- spec_weight: float32 [2, 36, 36, 288], P(None, None, None, 'sp'), may hold values from -24 to 24
- point_weight: bfloat16 [36, 36], replicated, may hold values from -1 to 1
- kernel_one: bfloat16 [3, 3, 36, 36], replicated, may hold values from -0.3125 to 0.3125
- kernel_two: bfloat16 [3, 3, 36, 36], replicated, may hold values from -0.3125 to 0.3125
Outputs:
- output: bfloat16 [4, 2, 36, 256, 1024], P('rep', None, None, 'sp')
- field_grad: bfloat16 [4, 2, 36, 256, 1024], P('rep', None, None, 'sp')
- spec_grad: float32 [2, 36, 36, 288], P(None, None, None, 'sp')
- point_grad: float32 [36, 36], replicated
- kernel_one_grad: float32 [3, 3, 36, 36], replicated
- kernel_two_grad: float32 [3, 3, 36, 36], replicated
The draws below stay inside these ranges and needn't reach their ends.
All inputs are finite; a program needn't handle non-finite values.
Results may differ from the reference program's by a relative error of at most 0.014.
Values may be sent and summed in bfloat16 or wider, within the bound.
No kernel may reach another device: no remote copies, remote signals or barrier semaphores. Data moves between devices by JAX's collectives and lax.ppermute only.
A program may use at most 192 MiB of HBM per device.

```python
import math
import jax
import jax.numpy as jnp
from jax import lax

C = 36
NC = 1024
M = 12
LEV = 2
MODES = 288
NR = 256
SAMPLES = 4


def level_of(rng, dims, shards, low, high):
    loudness, own = 1.0, jax.random.fold_in(rng, 6)
    for dim, shards_of in shards:
        draws = jnp.exp(jax.random.uniform(jax.random.fold_in(own, dim), (shards_of,), jnp.float32, low / len(shards), high / len(shards)))
        loudness = loudness * jnp.repeat(draws, dims[dim] // shards_of).reshape([-1 if axis == dim else 1 for axis in range(len(dims))])
    return loudness


def normal_values(own_key, extent, spread, limit, shards=(), kind=jnp.bfloat16):
    drawn = jax.random.normal(own_key, extent, jnp.float32) * spread
    if len(shards) > 0:
        drawn = level_of(own_key, extent, shards, -0.22, 0.18) * drawn
    return jnp.clip(drawn, min=-limit, max=limit).astype(kind)


def setup_inputs(seed: int = 0) -> dict:
    splits = jax.random.split(jax.random.key(seed), 7)
    return {
        "field": normal_values(splits[0], (SAMPLES, LEV, C, NR, NC), 1.0, 6.0, ((0, 4), (3, 32))),
        "cotangent": normal_values(splits[1], (SAMPLES, LEV, C, NR, NC), 1.0, 6.0, ((0, 4), (3, 32))),
        "spec_weight": normal_values(splits[2], (2, C, C, MODES), 4.0, 24.0, ((3, 32),), jnp.float32),
        "point_weight": normal_values(splits[3], (C, C), C ** -0.5, 1.0),
        "kernel_one": normal_values(splits[4], (3, 3, C, C), (9 * C) ** -0.5, 0.3125),
        "kernel_two": normal_values(splits[5], (3, 3, C, C), (9 * C) ** -0.5, 0.3125),
    }


HIGHEST = lax.Precision.HIGHEST
ROOT_HALF = 0.7071067811865476
INV_ROOT_TAU = 0.3989422804014327

def gelu_value(values):
    return 0.5 * values * (1.0 + jax.scipy.special.erf(values * ROOT_HALF))

def gelu_slope(values):
    return 0.5 * (1.0 + jax.scipy.special.erf(values * ROOT_HALF)) + values * jnp.exp(-0.5 * values * values) * INV_ROOT_TAU

def column_tables(col_count, mode_count):
    column = jnp.arange(col_count, dtype=jnp.int32)[:, None]
    frequency = jnp.arange(mode_count, dtype=jnp.int32)[None, :]
    phase = (column * frequency % col_count).astype(jnp.float32) * (2.0 * math.pi / col_count)
    forward = jnp.concatenate([jnp.cos(phase), -jnp.sin(phase)], axis=1)
    doubled = jnp.where(frequency == 0, 1.0, 2.0).astype(jnp.float32)
    return (forward, jnp.concatenate([doubled, doubled], axis=1))

def row_tables(row_index, row_count, mode_count):
    slots = jnp.arange(2 * mode_count, dtype=jnp.int32)
    frequency = jnp.where(slots < mode_count, slots, row_count - 2 * mode_count + slots)
    phase = (row_index[:, None] * frequency[None, :] % row_count).astype(jnp.float32) * (2.0 * math.pi / row_count)
    return (jnp.cos(phase), jnp.sin(phase))

def column_forward(values, table_half):
    return jnp.einsum('bcrn,nk->bcrk', values.astype(jnp.float32), table_half.astype(jnp.float32), precision=HIGHEST)

def column_inverse(expanded, matrix):
    return jnp.einsum('bork,kn->born', expanded, matrix, precision=HIGHEST)

def contract_rows(operand, matrix):
    return jnp.einsum('bcrk,rj->bcjk', operand, matrix, precision=HIGHEST)

def expand_rows(spectrum, matrix):
    return jnp.einsum('bojk,rj->bork', spectrum, matrix, precision=HIGHEST)

def row_forward(columns, cosine_table, sine_table, mode_count):
    real_part = columns[..., :mode_count]
    imag_part = columns[..., mode_count:]
    spec_real = contract_rows(real_part, cosine_table) + contract_rows(imag_part, sine_table)
    spec_imag = contract_rows(imag_part, cosine_table) - contract_rows(real_part, sine_table)
    stacked = jnp.stack([spec_real, spec_imag])
    return stacked.reshape(2, stacked.shape[1], stacked.shape[2], -1)

def row_inverse(spectrum, cosine_table, sine_table, mode_count):
    grid = spectrum.reshape(2, spectrum.shape[1], spectrum.shape[2], 2 * mode_count, mode_count)
    rows_real = expand_rows(grid[0], cosine_table) - expand_rows(grid[1], sine_table)
    rows_imag = expand_rows(grid[0], sine_table) + expand_rows(grid[1], cosine_table)
    return jnp.concatenate([rows_real, rows_imag], axis=3)

def spectral_mix(spectrum, weight):
    mixed_real = jnp.einsum('bcq,coq->boq', spectrum[0], weight[0], precision=HIGHEST) - jnp.einsum('bcq,coq->boq', spectrum[1], weight[1], precision=HIGHEST)
    mixed_imag = jnp.einsum('bcq,coq->boq', spectrum[0], weight[1], precision=HIGHEST) + jnp.einsum('bcq,coq->boq', spectrum[1], weight[0], precision=HIGHEST)
    return jnp.stack([mixed_real, mixed_imag])

def spectral_back(cospectrum, weight):
    back_real = jnp.einsum('boq,coq->bcq', cospectrum[0], weight[0], precision=HIGHEST) + jnp.einsum('boq,coq->bcq', cospectrum[1], weight[1], precision=HIGHEST)
    back_imag = jnp.einsum('boq,coq->bcq', cospectrum[1], weight[0], precision=HIGHEST) - jnp.einsum('boq,coq->bcq', cospectrum[0], weight[1], precision=HIGHEST)
    return jnp.stack([back_real, back_imag])

def spectral_grad(spectrum, cospectrum):
    grad_real = jnp.einsum('bcq,boq->coq', spectrum[0], cospectrum[0], precision=HIGHEST) + jnp.einsum('bcq,boq->coq', spectrum[1], cospectrum[1], precision=HIGHEST)
    grad_imag = jnp.einsum('bcq,boq->coq', spectrum[0], cospectrum[1], precision=HIGHEST) - jnp.einsum('bcq,boq->coq', spectrum[1], cospectrum[0], precision=HIGHEST)
    return jnp.stack([grad_real, grad_imag])

def correlate(padded, kernel):
    return lax.conv_general_dilated(padded.astype(jnp.float32), kernel.astype(jnp.float32), (1, 1), ((0, 0), (1, 1)), dimension_numbers=('NCHW', 'HWIO', 'NCHW'), precision=HIGHEST)

def transpose_conv(padded, kernel):
    flipped = jnp.transpose(kernel[::-1, ::-1], (0, 1, 3, 2))
    return correlate(padded, flipped)

def kernel_grad(padded, upstream):
    result = lax.conv_general_dilated(padded.astype(jnp.float32), upstream.astype(jnp.float32), (1, 1), ((0, 0), (1, 1)), dimension_numbers=('CNHW', 'IOHW', 'NCHW'), precision=HIGHEST)
    return jnp.transpose(result, (2, 3, 0, 1))

def pad_rows(values):
    return jnp.pad(values, ((0, 0), (0, 0), (1, 1), (0, 0)))

def reference(field, cotangent, spec_weight, point_weight, kernel_one, kernel_two):
    samples, levels, channels, row_count, col_count = field.shape
    inputs = field.reshape(samples * levels, channels, row_count, col_count)
    upstream_all = cotangent.reshape(samples * levels, channels, row_count, col_count)
    forward, doubled = column_tables(col_count, M)
    table_half = forward.astype(jnp.bfloat16)
    inverse_table = jnp.transpose(forward * doubled) / (row_count * col_count)
    cosine_table, sine_table = row_tables(jnp.arange(row_count, dtype=jnp.int32), row_count, M)
    cell_count = samples * levels * row_count * col_count
    point_float = point_weight.astype(jnp.float32)

    def one_field(totals, couple):
        single = couple[0][None]
        upstream = couple[1][None]
        single_float = single.astype(jnp.float32)
        partial_value = row_forward(column_forward(single, table_half), cosine_table, sine_table, M)
        mixed = spectral_mix(partial_value, spec_weight)
        spectral = column_inverse(row_inverse(mixed, cosine_table, sine_table, M), inverse_table)
        pointwise = jnp.einsum('bcrn,co->born', single_float, point_float, precision=HIGHEST)
        padded = pad_rows(single)
        hidden = correlate(padded, kernel_one)
        middle_pad = pad_rows(gelu_value(hidden).astype(jnp.bfloat16))
        branch = correlate(middle_pad, kernel_two)
        preact = spectral + pointwise + branch
        output = gelu_value(preact).astype(jnp.bfloat16)
        out_slope = (upstream.astype(jnp.float32) * gelu_slope(preact)).astype(jnp.bfloat16)
        slope_float = out_slope.astype(jnp.float32)
        slope_columns = column_forward(out_slope, table_half) * (doubled / (row_count * col_count))
        cospectrum = row_forward(slope_columns, cosine_table, sine_table, M)
        spec_delta = spectral_grad(partial_value, cospectrum)
        cofield = spectral_back(cospectrum, spec_weight)
        back_spec = column_inverse(row_inverse(cofield, cosine_table, sine_table, M), jnp.transpose(forward))
        back_point = jnp.einsum('born,co->bcrn', slope_float, point_float, precision=HIGHEST)
        point_delta = jnp.einsum('bcrn,born->co', single_float, slope_float, precision=HIGHEST)
        two_delta = kernel_grad(middle_pad, out_slope)
        pre_slope = (transpose_conv(pad_rows(out_slope), kernel_two) * gelu_slope(hidden)).astype(jnp.bfloat16)
        one_delta = kernel_grad(padded, pre_slope)
        back_conv = transpose_conv(pad_rows(pre_slope), kernel_one)
        field_grad = (back_spec + back_point + back_conv).astype(jnp.bfloat16)
        totals = (totals[0] + spec_delta, totals[1] + point_delta, totals[2] + one_delta, totals[3] + two_delta)
        return (totals, (output[0], field_grad[0]))
    start = (jnp.zeros((2, channels, channels, spec_weight.shape[3]), jnp.float32), jnp.zeros((channels, channels), jnp.float32), jnp.zeros((3, 3, channels, channels), jnp.float32), jnp.zeros((3, 3, channels, channels), jnp.float32))
    totals, stacked = lax.scan(one_field, start, (inputs, upstream_all))
    grad_scale = 1.0 / math.sqrt(cell_count)
    output = stacked[0].reshape(field.shape)
    field_grad = stacked[1].reshape(field.shape)
    return (output, field_grad, totals[0], totals[1] * grad_scale, totals[2] * grad_scale, totals[3] * grad_scale)
```

```python
import math

import jax
import jax.numpy as jnp
import numpy as np
import ml_dtypes
from jax import lax
from jax.experimental import pallas as pl
from jax.experimental.pallas import tpu as pltpu
from jax.sharding import PartitionSpec as P

M = 12
C = 36
CP = 48
CO = 40
LEV = 2
RL = 8
NC = 1024
NR = 256
SP = 32
QN = 9
GR = 3 * CP

ROOT_HALF = 0.7071067811865476
INV_ROOT_TAU = 0.3989422804014327
BF = jnp.bfloat16
F32 = jnp.float32
HIGHEST = lax.Precision.HIGHEST
VMEM = 56 * 1024 * 1024


def split_np(values):
    high = values.astype(np.float32).astype(ml_dtypes.bfloat16)
    low = (values - high.astype(np.float64)).astype(np.float32).astype(ml_dtypes.bfloat16)
    return high, low


def make_tables():
    n = np.arange(NC)[:, None]
    k = np.arange(M)[None, :]
    t = 2.0 * np.pi * ((n * k) % NC) / NC
    forward = np.concatenate([np.cos(t), -np.sin(t)], axis=1)
    doubled = np.where(np.arange(M) == 0, 1.0, 2.0)
    doubled = np.concatenate([doubled, doubled]) / (NR * NC)
    table = np.zeros((NC, 128), np.float32)
    table[:, :24] = forward
    table = table.astype(ml_dtypes.bfloat16)

    def inverse(matrix):
        high, low = split_np(matrix.T)
        out = np.zeros((128, NC), ml_dtypes.bfloat16)
        out[0:24], out[24:48], out[48:72] = high, low, high
        return out

    rows = np.zeros((SP, 2, 16, 256))
    freq = np.where(np.arange(24) < M, np.arange(24), NR - 24 + np.arange(24))
    phase = np.zeros((SP, SP, 2, 16, 2))
    for owner in range(SP):
        for q in range(QN):
            mode = owner * QN + q
            j, kk = mode // M, mode % M
            for r in range(RL):
                p = 2.0 * np.pi * ((freq[j] * r) % NR) / NR
                rows[owner, 0, q, r * 24 + kk] = np.cos(p)
                rows[owner, 0, q, r * 24 + 12 + kk] = np.sin(p)
                rows[owner, 1, q, r * 24 + kk] = -np.sin(p)
                rows[owner, 1, q, r * 24 + 12 + kk] = np.cos(p)
            for s in range(SP):
                p = 2.0 * np.pi * ((freq[j] * s) % SP) / SP
                phase[s, owner, :, q, 0] = np.cos(p)
                phase[s, owner, :, q, 1] = np.sin(p)
    high, low = split_np(rows.reshape(SP * 32, 256))
    scale = np.zeros((1, 256), np.float32)
    scale[0, :192] = np.tile(doubled, RL)
    return (
        table,
        inverse(forward * doubled[None, :]),
        inverse(forward),
        high,
        low,
        phase.reshape(SP, SP * 32, 2).astype(np.float32),
        scale,
    )


TABLE, INVERSE, BACK, ROW_HIGH, ROW_LOW, PHASE, SCALE = make_tables()


def dot(a, b, precision=None):
    return lax.dot_general(a, b, (((1,), (0,)), ((), ())), precision=precision, preferred_element_type=F32)


def dot_nt(a, b, precision=None):
    return lax.dot_general(a, b, (((1,), (1,)), ((), ())), precision=precision, preferred_element_type=F32)


def dot_tn(a, b, precision=None):
    return lax.dot_general(a, b, (((0,), (0,)), ((), ())), precision=precision, preferred_element_type=F32)


def split(values):
    high = values.astype(BF)
    return high, (values - high.astype(F32)).astype(BF)


def gelu_parts(v):
    cdf = 0.5 * (1.0 + lax.erf(v * ROOT_HALF))
    return v * cdf, cdf + v * jnp.exp(-0.5 * v * v) * INV_ROOT_TAU


def store_taps(taps, i, x):
    col = lax.broadcasted_iota(jnp.int32, (CP, NC), 1)
    taps[i, 0:CP] = jnp.where(col == 0, 0.0, pltpu.roll(x, 1, 1)).astype(BF)
    taps[i, CP : 2 * CP] = x.astype(BF)
    taps[i, 2 * CP : 3 * CP] = jnp.where(col == NC - 1, 0.0, pltpu.roll(x, NC - 1, 1)).astype(BF)


def three(ref, i, width):
    return ref[pl.ds(i, 3)].reshape(3 * width, NC)


def row_transform(cols, phase, high, low):
    c_high, c_low = split(cols)
    out = dot_nt(high, c_high) + dot_nt(high, c_low) + dot_nt(low, c_high)
    out = out.reshape(SP, 2, 16, 128)
    cosine = phase[:, 0:1].reshape(SP, 2, 16, 1)
    sine = phase[:, 1:2].reshape(SP, 2, 16, 1)
    re, im = out[:, 0], out[:, 1]
    c, s = cosine[:, 0], sine[:, 0]
    both = jnp.concatenate([(re * c + im * s)[:, None], (im * c - re * s)[:, None]], axis=1)
    return both.reshape(SP * 32, 128).astype(BF)


def row_expand(modes, phase, high, low):
    m = modes.astype(F32).reshape(SP, 2, 16, 128)
    cosine = phase[:, 0:1].reshape(SP, 2, 16, 1)
    sine = phase[:, 1:2].reshape(SP, 2, 16, 1)
    re, im = m[:, 0], m[:, 1]
    c, s = cosine[:, 0], sine[:, 0]
    both = jnp.concatenate([(re * c - im * s)[:, None], (re * s + im * c)[:, None]], axis=1)
    m_high, m_low = split(both.reshape(SP * 32, 128))
    return dot_tn(m_high, high) + dot_tn(m_high, low) + dot_tn(m_low, high)


def place_rows(rows, left):
    high, low = split(rows)
    high, low = high.astype(F32), low.astype(F32)
    left[...] = jnp.zeros_like(left)
    for lev in range(LEV):
        for r in range(RL):
            at = (lev * RL + r) * CO
            h = high[lev * 64 : lev * 64 + CO, r * 24 : r * 24 + 24]
            w = low[lev * 64 : lev * 64 + CO, r * 24 : r * 24 + 24]
            left[at : at + CO, 0:72] = jnp.concatenate([h, h, w], axis=1)


def kernel_a(field, table, high, low, phase, message, rows, top, bottom, wide, flat, cols):
    flat[...] = dot(field[...], table[...])
    cols[...] = jnp.zeros_like(cols)
    for lev in range(LEV):
        for r in range(RL):
            part = flat[pl.ds(lev * C * RL + r, C, stride=RL), :]
            cols[lev * 64 : lev * 64 + C, r * 24 : r * 24 + 24] = part[:, 0:24]
    message[...] = row_transform(cols[...], phase[...], high[...], low[...])
    for n in range(0, NC, 128):
        wide[n // 128, 0 : LEV * C * RL, :] = field[:, n : n + 128].astype(F32)
        wide[n // 128, LEV * C * RL :, :] = jnp.zeros((12 * RL, 128), F32)
    for lev in range(LEV):
        for r in range(RL):
            for n in range(0, NC, 128):
                x = wide[n // 128, pl.ds(lev * C * RL + r, CP, stride=RL), :].astype(BF)
                rows[lev, r, :, n : n + 128] = x
                if r < 2:
                    top[lev, r, :, n : n + 128] = x
                if r >= RL - 2:
                    bottom[lev, r - RL + 2, :, n : n + 128] = x


def kernel_b(place, rows, above, below, cot, w_one, w_two, middle, slope, pre, cot_rows, taps, taps_two, point, wide):
    index = place[0]
    for r in range(2):
        store_taps(taps, r, above[0, r].astype(F32))
        store_taps(taps, RL + 2 + r, below[0, r].astype(F32))

    def fill(r, carry):
        store_taps(taps, r + 2, rows[0, r].astype(F32))
        return carry

    lax.fori_loop(0, RL, fill, 0)
    for n in range(0, NC, 128):
        wide[n // 128, 0 : C * RL, :] = cot[0, :, n : n + 128].astype(F32)
        wide[n // 128, C * RL :, :] = jnp.zeros((12 * RL, 128), F32)
    for r in range(RL):
        for n in range(0, NC, 128):
            cot_rows[0, r, :, n : n + 128] = wide[n // 128, pl.ds(r, CP, stride=RL), :].astype(BF)

    def first(i, carry):
        d = dot(w_one[...], three(taps, i, GR))
        value, gradient = gelu_parts(d[0:CO])
        outside = ((i == 0) & (index == 0)) | ((i == RL + 1) & (index == SP - 1))
        keep = jnp.where(outside, 0.0, 1.0).astype(F32)
        value = jnp.concatenate([value * keep, jnp.zeros((CP - CO, NC), F32)], axis=0)
        slope[0, i] = gradient * keep
        middle[0, i] = value.astype(BF)
        store_taps(taps_two, i, value)
        point[i] = d[CP : CP + CO]
        return carry

    lax.fori_loop(0, RL + 2, first, 0)

    def second(r, carry):
        pre[0, r] = dot(w_two[...], three(taps_two, r, GR))[0:CO] + point[r + 1]
        return carry

    lax.fori_loop(0, RL, second, 0)


def own_modes(received):
    own = jnp.sum(received.astype(F32), axis=0)
    return own, jnp.concatenate([own[:, 0:64], own[:, 64:128]], axis=0)


def mode_products(stacked, weight):
    row = lax.broadcasted_iota(jnp.int32, (64, 128), 0) % 16
    total = jnp.zeros((64, 128), F32)
    for q in range(QN):
        total = total + jnp.where(row == q, dot(stacked, weight[q], HIGHEST), 0.0)
    return total


def kernel_mix(received, weight, message, kept):
    _, stacked = own_modes(received[...])
    kept[...] = stacked
    total = mode_products(stacked, weight)
    res, ims = [], []
    for lev in range(LEV):
        r, i = total[lev * 32 : lev * 32 + 16], total[lev * 32 + 16 : lev * 32 + 32]
        res.append(r[:, 0:64] - i[:, 64:128])
        ims.append(r[:, 64:128] + i[:, 0:64])
    mixed = jnp.concatenate([jnp.concatenate(res, axis=1), jnp.concatenate(ims, axis=1)], axis=0)
    message[...] = jnp.broadcast_to(mixed.astype(BF)[None], (SP, 32, 128))


def kernel_mix_back(received, weight, kept, message, grad):
    _, stacked = own_modes(received[...])
    total = mode_products(stacked, weight)
    res, ims = [], []
    for lev in range(LEV):
        r, i = total[lev * 32 : lev * 32 + 16], total[lev * 32 + 16 : lev * 32 + 32]
        res.append(r[:, 0:64] + i[:, 64:128])
        ims.append(i[:, 0:64] - r[:, 64:128])
    mixed = jnp.concatenate([jnp.concatenate(res, axis=1), jnp.concatenate(ims, axis=1)], axis=0)
    message[...] = jnp.broadcast_to(mixed.astype(BF)[None], (SP, 32, 128))
    swapped = jnp.concatenate(
        [stacked[16:32], -stacked[0:16], stacked[48:64], -stacked[32:48]], axis=0
    )
    right = jnp.concatenate([stacked, swapped], axis=1)
    row = lax.broadcasted_iota(jnp.int32, (64, 64), 0) % 16
    left = kept[...]
    for q in range(QN):
        grad[q] = dot_tn(jnp.where(row == q, left, 0.0), right, HIGHEST)[0:CP].astype(BF)


def kernel_d(received, phase, high, low, inverse, pre, cot, table, scale, out, slopes, top, bottom, message, left, spec, wide, flat, cols):
    place_rows(row_expand(received[...], phase[...], high[...], low[...]), left)
    spec[...] = dot(left[...].astype(BF), inverse[...])

    def one(t, carry):
        lev, r = t // RL, t % RL
        preact = pre[lev, r] + spec[pl.ds(pl.multiple_of(t * CO, 8), CO), :]
        value, gradient = gelu_parts(preact)
        for n in range(0, NC, 128):
            wide[n // 128, pl.ds(lev * C * RL + r, C, stride=RL), :] = value[0:C, n : n + 128]
        s = jnp.concatenate([gradient, jnp.zeros((CP - CO, NC), F32)], axis=0) * cot[lev, r].astype(F32)
        s = s.astype(BF)
        slopes[lev, r] = s
        return carry

    lax.fori_loop(0, LEV * RL, one, 0)
    for n in range(0, NC, 128):
        out[:, n : n + 128] = wide[n // 128].astype(BF)
    flat[...] = dot(slopes[...].reshape(LEV * RL * CP, NC), table[...])
    cols[...] = jnp.zeros_like(cols)
    for lev in range(LEV):
        top[lev] = slopes[lev, 0:2]
        bottom[lev] = slopes[lev, RL - 2 : RL]
        for r in range(RL):
            at = (lev * RL + r) * CP
            cols[lev * 64 : lev * 64 + CO, r * 24 : r * 24 + 24] = flat[at : at + CO, 0:24]
    message[...] = row_transform(cols[...] * scale[...], phase[...], high[...], low[...])


def kernel_e(place, slopes, above, below, middle, rows, f_above, f_below, slope, w_two, w_one, back, grad_two, grad_one, grad_point, taps, taps_two, field, point):
    index = place[0]
    lev = pl.program_id(0)
    for r in range(2):
        store_taps(taps, r, above[0, r].astype(F32))
        store_taps(taps, RL + 2 + r, below[0, r].astype(F32))
    field[0] = f_above[0, 1]
    field[RL + 1] = f_below[0, 0]

    def fill(r, carry):
        store_taps(taps, r + 2, slopes[0, r].astype(F32))
        field[r + 1] = rows[0, r]
        return carry

    lax.fori_loop(0, RL, fill, 0)

    @pl.when(lev == 0)
    def _():
        grad_two[...] = jnp.zeros_like(grad_two)
        grad_one[...] = jnp.zeros_like(grad_one)
        grad_point[...] = jnp.zeros_like(grad_point)

    def first(i, carry):
        d = dot(w_two[...], three(taps, i, GR))
        outside = ((i == 0) & (index == 0)) | ((i == RL + 1) & (index == SP - 1))
        keep = jnp.where(outside, 0.0, 1.0).astype(F32)
        value = jnp.concatenate([d[0:CO] * (slope[0, i] * keep), jnp.zeros((CP - CO, NC), F32)], axis=0)
        store_taps(taps_two, i, value)
        point[i] = d[CP : CP + CO]
        return carry

    lax.fori_loop(0, RL + 2, first, 0)

    def second(r, carry):
        back[0, r] = dot(w_one[...], three(taps_two, r, GR))[0:CO] + point[r + 1]
        grad_two[...] += dot_nt(three(middle.at[0], r, CP), taps[r + 2])
        grad_one[...] += dot_nt(three(field, r, CP), taps_two[r + 1])
        grad_point[...] += dot_nt(field[r + 1], taps[r + 2, CP : 2 * CP])
        return carry

    lax.fori_loop(0, RL, second, 0)


def kernel_f(received, phase, high, low, inverse, back, out, left, spec, wide):
    place_rows(row_expand(received[...], phase[...], high[...], low[...]), left)
    spec[...] = dot(left[...].astype(BF), inverse[...])

    def one(t, carry):
        lev, r = t // RL, t % RL
        value = back[lev, r] + spec[pl.ds(pl.multiple_of(t * CO, 8), CO), :]
        for n in range(0, NC, 128):
            wide[n // 128, pl.ds(lev * C * RL + r, C, stride=RL), :] = value[0:C, n : n + 128]
        return carry

    lax.fori_loop(0, LEV * RL, one, 0)
    for n in range(0, NC, 128):
        out[:, n : n + 128] = wide[n // 128].astype(BF)


def shape(dims, kind):
    return jax.ShapeDtypeStruct(dims, kind)


def params():
    return pltpu.CompilerParams(vmem_limit_bytes=VMEM)


def cost(us):
    return pl.CostEstimate(flops=int(us * 1e9), bytes_accessed=int(us * 3e6), transcendentals=0)


def level_spec(*dims):
    return pl.BlockSpec((1,) + dims, lambda lev: (lev,) + (0,) * len(dims))


def whole_spec(*dims):
    return pl.BlockSpec(dims, lambda lev: (0,) * len(dims))


def taps_weight(kernel):
    padded = jnp.pad(kernel, ((0, 0), (0, 0), (0, CP - C), (0, CP - C)))
    return jnp.transpose(padded, (3, 0, 1, 2)).reshape(CP, 9 * CP)


def centre_weight(matrix):
    padded = jnp.pad(matrix, ((0, CP - C), (0, CP - C)))
    return jnp.pad(jnp.transpose(padded), ((0, 0), (4 * CP, 4 * CP)))


def mode_weight(weight):
    moved = jnp.transpose(weight, (3, 1, 0, 2))
    return jnp.pad(moved, ((0, 0), (0, 64 - C), (0, 0), (0, 64 - C))).reshape(QN, 64, 128)


def from_above(x):
    return lax.ppermute(x, "sp", [(i, i + 1) for i in range(SP - 1)])


def from_below(x):
    return lax.ppermute(x, "sp", [(i + 1, i) for i in range(SP - 1)])


def exchange(x):
    return lax.all_to_all(x, "sp", 0, 0, tiled=True)


def local(field, cotangent, spec_weight, point_weight, kernel_one, kernel_two):
    index = lax.axis_index("sp")
    place = index.astype(jnp.int32).reshape(1)
    inputs = field.reshape(LEV * C * RL, NC)
    upstream = cotangent.reshape(LEV, C * RL, NC)
    phase = lax.dynamic_index_in_dim(jnp.asarray(PHASE), index, 0, keepdims=False)
    table, high, low = jnp.asarray(TABLE), jnp.asarray(ROW_HIGH), jnp.asarray(ROW_LOW)
    strip = shape((LEV, 2, CP, NC), BF)
    message, rows, top, bottom = pl.pallas_call(
        kernel_a,
        out_shape=[shape((SP * 32, 128), BF), shape((LEV, RL, CP, NC), BF), strip, strip],
        scratch_shapes=[
            pltpu.VMEM((NC // 128, (LEV * C + 12) * RL, 128), F32),
            pltpu.VMEM((LEV * C * RL, 128), F32),
            pltpu.VMEM((128, 256), F32),
        ],
        compiler_params=params(),
        cost_estimate=cost(8),
        name="field_modes",
    )(inputs, table, high, low, phase)
    f_above, f_below = from_above(bottom), from_below(top)
    arrived = exchange(message.reshape(SP, 32, 128))

    w_one = jnp.concatenate([taps_weight(kernel_one), centre_weight(point_weight)], axis=0)
    w_two = taps_weight(kernel_two)
    middle, slope, pre, cot_rows = pl.pallas_call(
        kernel_b,
        grid=(LEV,),
        in_specs=[
            pl.BlockSpec(memory_space=pltpu.SMEM),
            level_spec(RL, CP, NC),
            level_spec(2, CP, NC),
            level_spec(2, CP, NC),
            level_spec(C * RL, NC),
            whole_spec(2 * CP, 9 * CP),
            whole_spec(CP, 9 * CP),
        ],
        out_specs=[
            level_spec(RL + 2, CP, NC),
            level_spec(RL + 2, CO, NC),
            level_spec(RL, CO, NC),
            level_spec(RL, CP, NC),
        ],
        out_shape=[
            shape((LEV, RL + 2, CP, NC), BF),
            shape((LEV, RL + 2, CO, NC), F32),
            shape((LEV, RL, CO, NC), F32),
            shape((LEV, RL, CP, NC), BF),
        ],
        scratch_shapes=[
            pltpu.VMEM((RL + 4, GR, NC), BF),
            pltpu.VMEM((RL + 2, GR, NC), BF),
            pltpu.VMEM((RL + 2, CO, NC), F32),
            pltpu.VMEM((NC // 128, (C + 12) * RL, 128), F32),
        ],
        compiler_params=params(),
        cost_estimate=cost(25),
        name="two_convolutions",
    )(place, rows, f_above, f_below, upstream, w_one, w_two)

    mixed, kept = pl.pallas_call(
        kernel_mix,
        out_shape=[shape((SP, 32, 128), BF), shape((64, 64), F32)],
        compiler_params=params(),
        cost_estimate=cost(3),
        name="mode_mix",
    )(arrived, mode_weight(spec_weight))
    gathered = exchange(mixed).reshape(SP * 32, 128)

    out, slopes, s_top, s_bottom, message = pl.pallas_call(
        kernel_d,
        out_shape=[
            shape((LEV * C * RL, NC), BF),
            shape((LEV, RL, CP, NC), BF),
            strip,
            strip,
            shape((SP * 32, 128), BF),
        ],
        scratch_shapes=[
            pltpu.VMEM((LEV * RL * CO, 128), F32),
            pltpu.VMEM((LEV * RL * CO, NC), F32),
            pltpu.VMEM((NC // 128, LEV * C * RL, 128), F32),
            pltpu.VMEM((LEV * RL * CP, 128), F32),
            pltpu.VMEM((128, 256), F32),
        ],
        compiler_params=params(),
        cost_estimate=cost(15),
        name="output_and_slope",
    )(gathered, phase, high, low, jnp.asarray(INVERSE), pre, cot_rows, table, jnp.asarray(SCALE))
    s_above, s_below = from_above(s_bottom), from_below(s_top)
    arrived = exchange(message.reshape(SP, 32, 128))

    flip_two = jnp.transpose(kernel_two[::-1, ::-1], (0, 1, 3, 2))
    flip_one = jnp.transpose(kernel_one[::-1, ::-1], (0, 1, 3, 2))
    w_two_back = jnp.concatenate(
        [taps_weight(flip_two), centre_weight(jnp.transpose(point_weight))], axis=0
    )
    w_one_back = taps_weight(flip_one)
    back, grad_two, grad_one, grad_point = pl.pallas_call(
        kernel_e,
        grid=(LEV,),
        in_specs=[
            pl.BlockSpec(memory_space=pltpu.SMEM),
            level_spec(RL, CP, NC),
            level_spec(2, CP, NC),
            level_spec(2, CP, NC),
            level_spec(RL + 2, CP, NC),
            level_spec(RL, CP, NC),
            level_spec(2, CP, NC),
            level_spec(2, CP, NC),
            level_spec(RL + 2, CO, NC),
            whole_spec(2 * CP, 9 * CP),
            whole_spec(CP, 9 * CP),
        ],
        out_specs=[
            level_spec(RL, CO, NC),
            whole_spec(GR, GR),
            whole_spec(GR, GR),
            whole_spec(CP, CP),
        ],
        out_shape=[
            shape((LEV, RL, CO, NC), F32),
            shape((GR, GR), F32),
            shape((GR, GR), F32),
            shape((CP, CP), F32),
        ],
        scratch_shapes=[
            pltpu.VMEM((RL + 4, GR, NC), BF),
            pltpu.VMEM((RL + 2, GR, NC), BF),
            pltpu.VMEM((RL + 2, CP, NC), BF),
            pltpu.VMEM((RL + 2, CO, NC), F32),
        ],
        compiler_params=params(),
        cost_estimate=cost(30),
        name="backward_convolutions",
    )(place, slopes, s_above, s_below, middle, rows, f_above, f_below, slope, w_two_back, w_one_back)

    mixed, spec_part = pl.pallas_call(
        kernel_mix_back,
        out_shape=[shape((SP, 32, 128), BF), shape((QN, CP, 128), BF)],
        compiler_params=params(),
        cost_estimate=cost(4),
        name="mode_mix_back",
    )(arrived, mode_weight(jnp.transpose(spec_weight, (0, 2, 1, 3))), kept)
    gathered = exchange(mixed).reshape(SP * 32, 128)
    spec_all = lax.all_gather(spec_part, "rep", axis=0)

    field_grad = pl.pallas_call(
        kernel_f,
        out_shape=shape((LEV * C * RL, NC), BF),
        scratch_shapes=[
            pltpu.VMEM((LEV * RL * CO, 128), F32),
            pltpu.VMEM((LEV * RL * CO, NC), F32),
            pltpu.VMEM((NC // 128, LEV * C * RL, 128), F32),
        ],
        compiler_params=params(),
        cost_estimate=cost(8),
        name="field_gradient",
    )(gathered, phase, high, low, jnp.asarray(BACK), back)

    def wide_rows(x, count):
        return jnp.pad(x, ((0, count - x.shape[0]), (0, 256 - x.shape[1])))

    sums = jnp.concatenate([wide_rows(grad_two, 160), wide_rows(grad_one, 160), wide_rows(grad_point, 192)], axis=0)
    shares = jnp.sum(exchange(sums.reshape(SP, 16, 256)), axis=0)
    shares = jnp.sum(lax.all_gather(shares, "rep", axis=0), axis=0)
    sums = exchange(jnp.broadcast_to(shares[None], (SP, 16, 256))).reshape(SP * 16, 256)
    grad_scale = 1.0 / math.sqrt(NR * NC * LEV * lax.axis_size("rep"))
    sums = sums * grad_scale

    def kernel_shape(x):
        x = x[:GR, :GR].reshape(3, CP, 3, CP)[:, :C, ::-1, :C]
        return jnp.transpose(x, (0, 2, 1, 3))

    spec_sum = jnp.sum(spec_all.astype(F32), axis=0)
    spec_total = jnp.transpose(spec_sum.reshape(QN, CP, 2, 64)[:, :C, :, :C], (2, 1, 3, 0))
    return (
        out.reshape(field.shape),
        field_grad.reshape(field.shape),
        spec_total,
        sums[320 : 320 + C, :C],
        kernel_shape(sums[160:320]),
        kernel_shape(sums[:160]),
    )


def solution(mesh):
    specs = (
        P("rep", None, None, "sp", None),
        P("rep", None, None, "sp", None),
        P(None, None, None, "sp"),
        P(),
        P(),
        P(),
    )
    return jax.shard_map(local, mesh=mesh, in_specs=specs, out_specs=specs, check_vma=False)
```

```python
import math

import jax
import jax.numpy as jnp
import numpy as np
import ml_dtypes
from jax import lax
from jax.experimental import pallas as pl
from jax.experimental.pallas import tpu as pltpu
from jax.sharding import PartitionSpec as P

M = 12
C = 36
CP = 48
CO = 40
LEV = 2
RL = 8
NC = 1024
NR = 256
SP = 32
QN = 9
GR = 3 * CP

ROOT_HALF = 0.7071067811865476
INV_ROOT_TAU = 0.3989422804014327
BF = jnp.bfloat16
F32 = jnp.float32


def split_np(values):
    high = values.astype(np.float32).astype(ml_dtypes.bfloat16)
    low = (values - high.astype(np.float64)).astype(np.float32).astype(ml_dtypes.bfloat16)
    return high, low


def make_tables():
    n = np.arange(NC)[:, None]
    k = np.arange(M)[None, :]
    t = 2.0 * np.pi * ((n * k) % NC) / NC
    forward = np.concatenate([np.cos(t), -np.sin(t)], axis=1)
    doubled = np.where(np.arange(M) == 0, 1.0, 2.0)
    doubled = np.concatenate([doubled, doubled]) / (NR * NC)
    table = np.zeros((NC, 128), np.float32)
    table[:, :24] = forward
    table = table.astype(ml_dtypes.bfloat16)

    def inverse(matrix):
        high, low = split_np(matrix.T)
        out = np.zeros((128, NC), ml_dtypes.bfloat16)
        out[0:24], out[24:48], out[48:72] = high, low, high
        return out

    rows = np.zeros((SP, 2, 16, 256))
    freq = np.where(np.arange(24) < M, np.arange(24), NR - 24 + np.arange(24))
    mode_row = np.zeros((SP, 2, 16, 32))
    for owner in range(SP):
        for q in range(QN):
            mode = owner * QN + q
            j, kk = mode // M, mode % M
            for r in range(RL):
                p = 2.0 * np.pi * ((freq[j] * r) % NR) / NR
                rows[owner, 0, q, r * 24 + kk] = np.cos(p)
                rows[owner, 0, q, r * 24 + 12 + kk] = np.sin(p)
                rows[owner, 1, q, r * 24 + kk] = -np.sin(p)
                rows[owner, 1, q, r * 24 + 12 + kk] = np.cos(p)
            mode_row[owner, :, q, j] = 1.0
    high, low = split_np(rows.reshape(SP * 32, 256))
    scale = np.zeros((1, 256), np.float32)
    scale[0, :192] = np.tile(doubled, RL)
    return (
        table,
        inverse(forward * doubled[None, :]),
        inverse(forward),
        high,
        low,
        mode_row.reshape(SP * 32, 32).astype(ml_dtypes.bfloat16),
        scale,
    )


TABLE, INVERSE, BACK, ROW_HIGH, ROW_LOW, MODE_ROW, SCALE = make_tables()


def dot(a, b):
    return lax.dot_general(a, b, (((1,), (0,)), ((), ())), preferred_element_type=F32)


def dot_nt(a, b):
    return lax.dot_general(a, b, (((1,), (1,)), ((), ())), preferred_element_type=F32)


def dot_tn(a, b):
    return lax.dot_general(a, b, (((0,), (0,)), ((), ())), preferred_element_type=F32)


def split(values):
    high = values.astype(BF)
    return high, (values - high.astype(F32)).astype(BF)


def gelu_parts(v):
    cdf = 0.5 * (1.0 + lax.erf(v * ROOT_HALF))
    return v * cdf, cdf + v * jnp.exp(-0.5 * v * v) * INV_ROOT_TAU


def store_taps(taps, i, x):
    col = lax.broadcasted_iota(jnp.int32, (CP, NC), 1)
    taps[i, 0:CP] = jnp.where(col == 0, 0.0, pltpu.roll(x, 1, 1)).astype(BF)
    taps[i, CP : 2 * CP] = x.astype(BF)
    taps[i, 2 * CP : 3 * CP] = jnp.where(col == NC - 1, 0.0, pltpu.roll(x, NC - 1, 1)).astype(BF)


def row_transform(cols, high, low):
    c_high, c_low = split(cols)
    return (dot_nt(high, c_high) + dot_nt(high, c_low) + dot_nt(low, c_high)).astype(BF)


def row_expand(modes, high, low):
    return dot_tn(modes, high) + dot_tn(modes, low)


def place_rows(rows, left):
    high, low = split(rows)
    high, low = high.astype(F32), low.astype(F32)
    left[...] = jnp.zeros_like(left)
    for lev in range(LEV):
        for r in range(RL):
            at = (lev * RL + r) * CO
            h = high[lev * 64 : lev * 64 + CO, r * 24 : r * 24 + 24]
            w = low[lev * 64 : lev * 64 + CO, r * 24 : r * 24 + 24]
            left[at : at + CO, 0:72] = jnp.concatenate([h, h, w], axis=1)


def kernel_a(place, field, table, high, low, mode_row, message, own_high, own_low, flat, cols):
    j = lax.broadcasted_iota(jnp.int32, (32, 128), 0)
    turn = ((j + jnp.where(j < M, 0, NR - 24)) * place[0]) % SP
    angle = turn.astype(F32) * (2.0 * math.pi / SP)
    t_high, t_low = split(jnp.concatenate([jnp.cos(angle), jnp.sin(angle)], axis=1))
    phase = (dot(mode_row[...], t_high) + dot(mode_row[...], t_low)).reshape(SP, 2, 16, 256)[:, 0]
    cosine, sine = phase[:, :, 0:128], phase[:, :, 128:256]
    cosine, sine = jnp.concatenate([cosine, cosine], axis=2), jnp.concatenate([sine, sine], axis=2)
    first = (high[...].astype(F32) + low[...].astype(F32)).reshape(SP, 2, 16, 256)
    re, im = first[:, 0], first[:, 1]
    turned = jnp.concatenate([(re * cosine + im * sine)[:, None], (im * cosine - re * sine)[:, None]], axis=1)
    h, w = split(turned.reshape(SP * 32, 256))
    own_high[...], own_low[...] = h, w
    flat[...] = dot(field[...], table[...])
    cols[...] = jnp.zeros_like(cols)
    for lev in range(LEV):
        for r in range(RL):
            part = flat[pl.ds(lev * C * RL + r, C, stride=RL), :]
            cols[lev * 64 : lev * 64 + C, r * 24 : r * 24 + 24] = part[:, 0:24]
    message[...] = row_transform(cols[...], h, w)


def prepare(one, two, point, w_one, w_two, w_two_back, w_one_back, w_point, w_point_back, base, wide):
    def spread(target, rows):
        wide[...] = jnp.zeros_like(wide)
        for t in range(4):
            wide[t * CP : (t + 1) * CP, t * rows : t * rows + base.shape[1]] = base[...]
        target[...] = wide[:, 0 : target.shape[1]].astype(BF)

    for kernel, forward, backward in ((one, w_one, w_one_back), (two, w_two, w_two_back)):
        base[...] = jnp.zeros_like(base)
        for a in range(3):
            for b in range(3):
                at = (a * 3 + b) * CP
                base[0:C, at : at + C] = jnp.transpose(kernel[a, b].astype(F32))
        spread(forward, GR)
        for a in range(3):
            for b in range(3):
                at = ((2 - a) * 3 + 2 - b) * CP
                base[0:C, at : at + C] = kernel[a, b].astype(F32)
        spread(backward, GR)
    for target, matrix in ((w_point, jnp.transpose(point[...].astype(F32))), (w_point_back, point[...].astype(F32))):
        wide[...] = jnp.zeros_like(wide)
        for t in range(4):
            wide[t * CP : t * CP + C, t * CP : t * CP + C] = matrix
        target[...] = wide[:, 0 : 4 * CP].astype(BF)


def kernel_rows(field, cot, one, two, point, after, rows, top, bottom, cot_rows, w_one, w_two, w_two_back, w_one_back, w_point, w_point_back, wide, base, spread):
    prepare(one, two, point, w_one, w_two, w_two_back, w_one_back, w_point, w_point_back, base, spread)
    for source, target in ((field, rows), (cot, cot_rows)):
        for n in range(0, NC, 128):
            wide[n // 128, 0 : LEV * C * RL, :] = source[:, n : n + 128].astype(F32)
            wide[n // 128, LEV * C * RL :, :] = jnp.zeros((12 * RL, 128), F32)
        for lev in range(LEV):
            for r in range(RL):
                for n in range(0, NC, 128):
                    x = wide[n // 128, pl.ds(lev * C * RL + r, CP, stride=RL), :].astype(BF)
                    target[lev, r, :, n : n + 128] = x
                    if target is rows and r < 2:
                        top[lev, r, :, n : n + 128] = x
                    if target is rows and r >= RL - 2:
                        bottom[lev, r - RL + 2, :, n : n + 128] = x


def window(ref, i, count):
    return ref[i : i + count].reshape(count * GR, NC)


def kernel_b(place, rows, above, below, w_one, w_two, w_point, after, mid_taps, slope, pre, taps):
    index = place[0]
    source = [above.at[0, 0], above.at[0, 1]] + [rows.at[0, r] for r in range(RL)] + [below.at[0, 0], below.at[0, 1]]
    for i, x in enumerate(source):
        store_taps(taps, i, x[...].astype(F32))
    rest = jnp.zeros((CP - CO, NC), F32)
    for start, count in ((0, 4), (4, 3), (7, 3)):
        d = dot(w_one[0 : CP * count, 0 : GR * (count + 2)], window(taps, start, count + 2))
        for t in range(count):
            i = start + t
            value, gradient = gelu_parts(d[t * CP : t * CP + CO])
            if i in (0, RL + 1):
                keep = jnp.where(index == (0 if i == 0 else SP - 1), 0.0, 1.0).astype(F32)
                value, gradient = value * keep, gradient * keep
            slope[0, i] = gradient
            store_taps(mid_taps.at[0], i, jnp.concatenate([value, rest], axis=0))
    for r in (0, 4):
        d = dot(w_two[...], window(mid_taps.at[0], r, 6))
        d = d + dot(w_point[...], rows[0, r : r + 4].reshape(4 * CP, NC))
        for t in range(4):
            pre[0, r + t] = d[t * CP : t * CP + CO]


def own_modes(received):
    return jnp.sum(received.astype(F32), axis=0)


def by_channel(own, real, imag):
    rest = jnp.zeros((96, 128), F32)
    real[...] = jnp.transpose(jnp.concatenate([own, rest], axis=0))
    imag[...] = jnp.transpose(jnp.concatenate([own[16:32], own[0:16], rest], axis=0))


def weight_rows(weight, lines):
    lines[...] = jnp.zeros_like(lines)
    lines[:, 0:C] = weight[...]


def mode_line(lines, q, part):
    return lines[pl.ds(2 * q + part, C, stride=2 * QN), :]


def kernel_mix(received, weight, message, kept, real, imag, mixed, lines):
    own = own_modes(received[...])
    kept[...] = own
    by_channel(own, real, imag)
    weight_rows(weight, lines)
    mixed[...] = jnp.zeros_like(mixed)
    for q in range(QN):
        w_re, w_im = mode_line(lines, q, 0), mode_line(lines, q, 1)
        re, im = [], []
        for lev in range(LEV):
            s_re = real[lev * 64 : lev * 64 + C, q : q + 1]
            s_im = imag[lev * 64 : lev * 64 + C, q : q + 1]
            re.append(jnp.sum(w_re * s_re - w_im * s_im, axis=0, keepdims=True))
            im.append(jnp.sum(w_im * s_re + w_re * s_im, axis=0, keepdims=True))
        mixed[q : q + 1] = re[0] + pltpu.roll(re[1], 64, 1)
        mixed[16 + q : 17 + q] = im[0] + pltpu.roll(im[1], 64, 1)
    message[...] = jnp.broadcast_to(mixed[0:32].astype(BF)[None], (SP, 32, 128))


def mix_back(own, lines, mixed):
    other = pltpu.roll(own, 64, 1)
    mixed[...] = jnp.zeros_like(mixed)
    for q in range(QN):
        w_re, w_im = mode_line(lines, q, 0), mode_line(lines, q, 1)
        for lev, z in enumerate((own, other)):
            z_re, z_im = z[q : q + 1], z[16 + q : 17 + q]
            at = lev * 64
            mixed[at : at + C, q : q + 1] = jnp.sum(w_re * z_re + w_im * z_im, axis=1, keepdims=True)
            mixed[at : at + C, 16 + q : 17 + q] = jnp.sum(w_re * z_im - w_im * z_re, axis=1, keepdims=True)
    return jnp.transpose(mixed[...])[0:32].astype(BF)


def kernel_spec_grad(p0, p1, p2, p3, after, grad, s_re, s_im, lines):
    pairs = (p0, p1, p2, p3)
    co = []
    for i, pair in enumerate(pairs):
        by_channel(pair[0:32], s_re.at[i], s_im.at[i])
        co.append((pair[32:64], pltpu.roll(pair[32:64], 64, 1)))
    for q in range(QN):
        res, ims = [], []
        for i in range(4):
            re, im = jnp.zeros((C, 128), F32), jnp.zeros((C, 128), F32)
            for lev in range(LEV):
                at = lev * 64
                a, b = s_re[i, at : at + C, q : q + 1], s_im[i, at : at + C, q : q + 1]
                x, y = co[i][lev][q : q + 1], co[i][lev][16 + q : 17 + q]
                re = re + (a * x + b * y)
                im = im + (a * y - b * x)
            res.append(re)
            ims.append(im)
        lines[pl.ds(2 * q, C, stride=2 * QN), :] = (res[0] + res[1]) + (res[2] + res[3])
        lines[pl.ds(2 * q + 1, C, stride=2 * QN), :] = (ims[0] + ims[1]) + (ims[2] + ims[3])
    grad[...] = lines[:, 0:C]


def kernel_share(gathered, first, second, share):
    share[...] = jnp.sum(gathered[:, 32:48].astype(F32), axis=0)


def kernel_d(received, high, low, inverse, pre, cot, table, scale, values, slopes, top, bottom, message, left, spec, kept, cols):
    lev = pl.program_id(0)

    @pl.when(lev == 0)
    def _():
        place_rows(row_expand(received[...], high[...], low[...]), left)
        spec[...] = dot(left[...].astype(BF), inverse[...]).reshape(LEV * RL, CO, NC)
        cols[...] = jnp.zeros_like(cols)

    rest = jnp.zeros((CP - CO, NC), F32)
    for r in range(RL):
        value, gradient = gelu_parts(pre[0, r] + spec[lev * RL + r])
        values[0, r] = jnp.concatenate([value, rest], axis=0).astype(BF)
        s = jnp.concatenate([gradient, rest], axis=0) * cot[0, r].astype(F32)
        s = s.astype(BF)
        slopes[0, r] = s
        if r < 2:
            top[0, r] = s
        if r >= RL - 2:
            bottom[0, r - RL + 2] = s
    kept[lev] = dot(slopes[0].reshape(RL * CP, NC), table[...])

    @pl.when(lev == LEV - 1)
    def _():
        for at in range(LEV):
            for r in range(RL):
                cols[at * 64 : at * 64 + CO, r * 24 : r * 24 + 24] = kept[at, r * CP : r * CP + CO, 0:24]
        message[...] = row_transform(cols[...] * scale[...], high[...], low[...])


def kernel_out(values, after, out, wide):
    for lev in range(LEV):
        for r in range(RL):
            for n in range(0, NC, 128):
                x = values[lev, r, :, n : n + 128].astype(F32)
                wide[n // 128, pl.ds(lev * C * RL + r, C, stride=RL), :] = x[0:C]
    for n in range(0, NC, 128):
        out[:, n : n + 128] = wide[n // 128].astype(BF)


def kernel_mix_back(received, weight, kept, cofield, pair, mixed, lines):
    own = own_modes(received[...])
    pair[0:32] = kept[...]
    pair[32:64] = own
    weight_rows(weight, lines)
    cofield[...] = mix_back(own, lines, mixed)


def kernel_e_zero(slopes, mid_taps, rows, grad_two):
    none = jnp.zeros((CP, NC), BF)
    left, right = [], []
    for i in range(RL + 2):
        inside = 1 <= i <= RL
        left.append(jnp.concatenate([mid_taps[0, i], rows[0, i - 1] if inside else none], axis=0))
        right.append(jnp.concatenate([slopes[0, r] if 0 <= r < RL else none for r in (i, i - 1, i - 2)], axis=0))
    part = dot_nt(jnp.concatenate(left, axis=1), jnp.concatenate(right, axis=1))

    @pl.when(pl.program_id(0) == 0)
    def _():
        grad_two[...] = part

    @pl.when(pl.program_id(0) > 0)
    def _():
        grad_two[...] += part


def kernel_e(place, slopes, above, below, rows, f_above, f_below, slope, w_two, cofield, grad_two, pre_taps, message, taps, grad_one, sums):
    index = place[0]
    lev = pl.program_id(0)
    source = [above.at[0, 0], above.at[0, 1]] + [slopes.at[0, r] for r in range(RL)] + [below.at[0, 0], below.at[0, 1]]
    for i, x in enumerate(source):
        store_taps(taps, i, x[...].astype(F32))
    rest = jnp.zeros((CP - CO, NC), F32)
    for start, count in ((0, 4), (4, 3), (7, 3)):
        d = dot(w_two[0 : CP * count, 0 : GR * (count + 2)], window(taps, start, count + 2))
        for t in range(count):
            i = start + t
            value = d[t * CP : t * CP + CO] * slope[0, i]
            if i in (0, RL + 1):
                value = value * jnp.where(index == (0 if i == 0 else SP - 1), 0.0, 1.0).astype(F32)
            store_taps(pre_taps.at[0], i, jnp.concatenate([value, rest], axis=0))
    field = [f_above[0, 1]] + [rows[0, r] for r in range(RL)] + [f_below[0, 0]]
    left = jnp.concatenate([jnp.concatenate(field[r : r + 3], axis=0) for r in range(RL)], axis=1)
    right = jnp.concatenate([pre_taps[0, r + 1] for r in range(RL)], axis=1)
    part_one = dot_nt(left, right)

    @pl.when(lev == 0)
    def _():
        grad_one[...] = part_one

    @pl.when(lev == LEV - 1)
    def _():
        sums[...] = jnp.zeros_like(sums)
        two, one = grad_two[...], grad_one[...] + part_one
        for b in range(3):
            sums[b * GR : (b + 1) * GR, 0:CP] = two[0:GR, b * CP : (b + 1) * CP]
            sums[b * GR : (b + 1) * GR, 64 : 64 + CP] = one[:, b * CP : (b + 1) * CP]
        sums[3 * GR : 3 * GR + CP, 0:CP] = two[GR : GR + CP, CP : 2 * CP]
        message[:, 0:32] = jnp.broadcast_to(cofield[...][None], (SP, 32, 128))
        message[:, 32:48] = sums[...].reshape(SP, 16, 128).astype(BF)


def kernel_e_two(pre_taps, slopes, w_one, w_point, after, back):
    for r in (0, 4):
        d = dot(w_one[...], window(pre_taps.at[0], r, 6))
        d = d + dot(w_point[...], slopes[0, r : r + 4].reshape(4 * CP, NC))
        for t in range(4):
            back[0, r + t] = d[t * CP : t * CP + CO]


def kernel_f(received, high, low, inverse, back, out, left, spec, wide):
    modes = received[:, 0:32].reshape(SP * 32, 128)
    place_rows(row_expand(modes, high[...], low[...]), left)
    spec[...] = dot(left[...].astype(BF), inverse[...])
    for lev in range(LEV):
        for r in range(RL):
            at = (lev * RL + r) * CO
            value = back[lev, r] + spec[at : at + CO, :]
            for n in range(0, NC, 128):
                wide[n // 128, pl.ds(lev * C * RL + r, C, stride=RL), :] = value[0:C, n : n + 128]
    for n in range(0, NC, 128):
        out[:, n : n + 128] = wide[n // 128].astype(BF)


def kernel_last(sums, point, one, two):
    scaled = sums[...] * (1.0 / math.sqrt(NR * NC * LEV * 4))
    for a in range(3):
        for b in range(3):
            at = a * GR + b * CP
            two[a, b] = scaled[at : at + C, 0:C]
            at = (2 - b) * GR + a * CP
            one[a, b] = scaled[at : at + C, 64 : 64 + C]
    point[...] = scaled[3 * GR : 3 * GR + C, 0:C]


def shape(dims, kind):
    return jax.ShapeDtypeStruct(dims, kind)


def params(mib):
    return pltpu.CompilerParams(vmem_limit_bytes=56 * 1024 * 1024)


def estimate(us):
    if us is None:
        return None
    return pl.CostEstimate(flops=us * 10**9, bytes_accessed=us * 3 * 10**6, transcendentals=0)


def level_spec(*dims):
    return pl.BlockSpec((1,) + dims, lambda lev: (lev,) + (0,) * len(dims))


def whole_spec(*dims):
    return pl.BlockSpec(dims, lambda lev: (0,) * len(dims))


def from_above(x):
    return lax.ppermute(x, "sp", [(i, i + 1) for i in range(SP - 1)])


def from_below(x):
    return lax.ppermute(x, "sp", [(i + 1, i) for i in range(SP - 1)])


def exchange(x):
    return lax.all_to_all(x, "sp", 0, 0, tiled=True)


def anywhere():
    return pl.BlockSpec(memory_space=pl.ANY)


def plain_call(kernel, operands, after, outs, scratch, mib, name, place=(), cost=None):
    vmem = pl.BlockSpec(memory_space=pltpu.VMEM)
    return pl.pallas_call(
        kernel,
        in_specs=[pl.BlockSpec(memory_space=pltpu.SMEM)] * len(place) + [vmem] * len(operands) + [anywhere()] * len(after),
        out_specs=[vmem] * len(outs),
        out_shape=outs,
        scratch_shapes=scratch,
        compiler_params=params(mib),
        cost_estimate=estimate(cost),
        name=name,
    )(*place, *operands, *after)


def local(field, cotangent, spec_weight, point_weight, kernel_one, kernel_two):
    place = lax.axis_index("sp").astype(jnp.int32).reshape(1)
    inputs = field.reshape(LEV * C * RL, NC)
    upstream = cotangent.reshape(LEV * C * RL, NC)
    table = jnp.asarray(TABLE)
    weight = jnp.transpose(spec_weight, (1, 3, 0, 2)).reshape(C * QN * 2, C)
    strip = shape((LEV, 2, CP, NC), BF)
    grid_rows = shape((LEV, RL, CP, NC), BF)
    natural = shape((LEV * C * RL, NC), BF)
    relayout = pltpu.VMEM((NC // 128, (LEV * C + 12) * RL, 128), F32)
    flat, cols = pltpu.VMEM((LEV * C * RL, 128), F32), pltpu.VMEM((128, 256), F32)
    row_matrix = shape((SP * 32, 256), BF)
    message, high, low = plain_call(
        kernel_a,
        (inputs, table, jnp.asarray(ROW_HIGH), jnp.asarray(ROW_LOW), jnp.asarray(MODE_ROW)),
        (),
        [shape((SP * 32, 128), BF), row_matrix, row_matrix],
        [flat, cols],
        10,
        "field_modes",
        (place,),
    )
    arrived = exchange(message.reshape(SP, 32, 128))
    toeplitz, blocks = shape((4 * CP, 6 * GR), BF), shape((4 * CP, 4 * CP), BF)
    rows, top, bottom, cot_rows, w_one, w_two, w_two_back, w_one_back, w_point, w_point_back = plain_call(
        kernel_rows,
        (inputs, upstream, kernel_one, kernel_two, point_weight),
        (message,),
        [grid_rows, strip, strip, grid_rows] + [toeplitz] * 4 + [blocks] * 2,
        [relayout, pltpu.VMEM((CP, 9 * CP), F32), pltpu.VMEM((4 * CP, 6 * GR), F32)],
        12,
        "row_layout",
    )
    f_above, f_below = from_above(bottom), from_below(top)

    square, lines = pltpu.VMEM((128, 128), F32), pltpu.VMEM((C * QN * 2, 128), F32)
    mixed, kept = plain_call(
        kernel_mix,
        (arrived, weight),
        (),
        [shape((SP, 32, 128), BF), shape((32, 128), F32)],
        [square, square, square, lines],
        6,
        "mode_mix",
    )
    gathered = exchange(mixed).reshape(SP * 32, 128)

    mid_taps, slope, pre = pl.pallas_call(
        kernel_b,
        grid=(LEV,),
        in_specs=[
            pl.BlockSpec(memory_space=pltpu.SMEM),
            level_spec(RL, CP, NC),
            level_spec(2, CP, NC),
            level_spec(2, CP, NC),
            whole_spec(4 * CP, 6 * GR),
            whole_spec(4 * CP, 6 * GR),
            whole_spec(4 * CP, 4 * CP),
            anywhere(),
        ],
        out_specs=[
            level_spec(RL + 2, GR, NC),
            level_spec(RL + 2, CO, NC),
            level_spec(RL, CO, NC),
        ],
        out_shape=[
            shape((LEV, RL + 2, GR, NC), BF),
            shape((LEV, RL + 2, CO, NC), F32),
            shape((LEV, RL, CO, NC), F32),
        ],
        scratch_shapes=[pltpu.VMEM((RL + 4, GR, NC), BF)],
        compiler_params=params(28),
        name="two_convolutions",
    )(place, rows, f_above, f_below, w_one, w_two, w_point, mixed)

    left, spec = pltpu.VMEM((LEV * RL * CO, 128), F32), pltpu.VMEM((LEV * RL * CO, NC), F32)
    values, slopes, s_top, s_bottom, message = pl.pallas_call(
        kernel_d,
        grid=(LEV,),
        in_specs=[
            whole_spec(SP * 32, 128),
            whole_spec(SP * 32, 256),
            whole_spec(SP * 32, 256),
            whole_spec(128, NC),
            level_spec(RL, CO, NC),
            level_spec(RL, CP, NC),
            whole_spec(NC, 128),
            whole_spec(1, 256),
        ],
        out_specs=[level_spec(RL, CP, NC)] * 2 + [level_spec(2, CP, NC)] * 2 + [whole_spec(SP * 32, 128)],
        out_shape=[grid_rows, grid_rows, strip, strip, shape((SP * 32, 128), BF)],
        scratch_shapes=[
            left,
            pltpu.VMEM((LEV * RL, CO, NC), F32),
            pltpu.VMEM((LEV, RL * CP, 128), F32),
            cols,
        ],
        compiler_params=params(22),
        name="output_and_slope",
    )(gathered, high, low, jnp.asarray(INVERSE), pre, cot_rows, table, jnp.asarray(SCALE))
    arrived = exchange(message.reshape(SP, 32, 128))
    s_above, s_below = from_above(s_bottom), from_below(s_top)

    grad_two = pl.pallas_call(
        kernel_e_zero,
        grid=(LEV,),
        in_specs=[level_spec(RL, CP, NC), level_spec(RL + 2, GR, NC), level_spec(RL, CP, NC)],
        out_specs=whole_spec(GR + CP, GR),
        out_shape=shape((GR + CP, GR), F32),
        compiler_params=params(22),
        name="weight_gradients_two",
    )(slopes, mid_taps, rows)
    cofield, pair = plain_call(
        kernel_mix_back,
        (arrived, weight, kept),
        (),
        [shape((32, 128), BF), shape((64, 128), F32)],
        [square, lines],
        6,
        "mode_mix_back",
        cost=15,
    )
    pre_taps, message = pl.pallas_call(
        kernel_e,
        grid=(LEV,),
        in_specs=[
            pl.BlockSpec(memory_space=pltpu.SMEM),
            level_spec(RL, CP, NC),
            level_spec(2, CP, NC),
            level_spec(2, CP, NC),
            level_spec(RL, CP, NC),
            level_spec(2, CP, NC),
            level_spec(2, CP, NC),
            level_spec(RL + 2, CO, NC),
            whole_spec(4 * CP, 6 * GR),
            whole_spec(32, 128),
            whole_spec(GR + CP, GR),
        ],
        out_specs=[level_spec(RL + 2, GR, NC), whole_spec(SP, 48, 128)],
        out_shape=[shape((LEV, RL + 2, GR, NC), BF), shape((SP, 48, 128), BF)],
        scratch_shapes=[
            pltpu.VMEM((RL + 4, GR, NC), BF),
            pltpu.VMEM((GR, GR), F32),
            pltpu.VMEM((SP * 16, 128), F32),
        ],
        compiler_params=params(28),
        name="slope_and_weight_gradients",
    )(place, slopes, s_above, s_below, rows, f_above, f_below, slope, w_two_back, cofield, grad_two)
    gathered = exchange(message)
    others = [lax.ppermute(pair, "rep", [(i, i ^ k) for i in range(4)]) for k in (1, 2, 3)]
    (spec_grad,) = plain_call(
        kernel_spec_grad,
        (pair, *others),
        (message,),
        [shape(weight.shape, F32)],
        [pltpu.VMEM((4, 128, 128), F32)] * 2 + [lines],
        8,
        "spectral_gradient",
    )
    back = pl.pallas_call(
        kernel_e_two,
        grid=(LEV,),
        in_specs=[
            level_spec(RL + 2, GR, NC),
            level_spec(RL, CP, NC),
            whole_spec(4 * CP, 6 * GR),
            whole_spec(4 * CP, 4 * CP),
            anywhere(),
        ],
        out_specs=level_spec(RL, CO, NC),
        out_shape=shape((LEV, RL, CO, NC), F32),
        compiler_params=params(22),
        name="backward_convolution",
    )(pre_taps, slopes, w_one_back, w_point_back, message)

    (shares,) = plain_call(
        kernel_share, (gathered,), (back, spec_grad), [shape((16, 128), F32)], [], 4, "weight_gradient_shares"
    )
    shares = jnp.sum(lax.all_gather(shares, "rep", axis=0), axis=0)
    every = exchange(jnp.broadcast_to(shares[None], (SP, 16, 128)))
    (out,) = plain_call(
        kernel_out,
        (values,),
        (shares,),
        [natural],
        [pltpu.VMEM((NC // 128, LEV * C * RL, 128), F32)],
        10,
        "output_layout",
    )
    (field_grad,) = plain_call(
        kernel_f,
        (gathered, high, low, jnp.asarray(BACK), back),
        (),
        [natural],
        [left, spec, pltpu.VMEM((NC // 128, LEV * C * RL, 128), F32)],
        18,
        "field_gradient",
    )
    kernel_out_shape = shape((3, 3, C, C), F32)
    point_total, one_total, two_total = plain_call(
        kernel_last,
        (every.reshape(SP * 16, 128),),
        (),
        [shape((C, C), F32), kernel_out_shape, kernel_out_shape],
        [],
        4,
        "weight_gradients",
    )
    spec_total = jnp.transpose(spec_grad.reshape(C, QN, 2, C), (2, 0, 3, 1))
    return (
        out.reshape(field.shape),
        field_grad.reshape(field.shape),
        spec_total,
        point_total,
        one_total,
        two_total,
    )


def solution(mesh):
    specs = (
        P("rep", None, None, "sp", None),
        P("rep", None, None, "sp", None),
        P(None, None, None, "sp"),
        P(),
        P(),
        P(),
    )
    return jax.shard_map(local, mesh=mesh, in_specs=specs, out_specs=specs, check_vma=False)
```

```python
import math

import jax
import jax.numpy as jnp
import numpy as np
import ml_dtypes
from jax import lax
from jax.experimental import pallas as pl
from jax.experimental.pallas import tpu as pltpu
from jax.sharding import PartitionSpec as P

M = 12
C = 36
CP = 48
CO = 40
LEV = 2
RL = 8
NC = 1024
NR = 256
SP = 32
QN = 9
GR = 3 * CP

ROOT_HALF = 0.7071067811865476
INV_ROOT_TAU = 0.3989422804014327
BF = jnp.bfloat16
F32 = jnp.float32


def split_np(values):
    high = values.astype(np.float32).astype(ml_dtypes.bfloat16)
    low = (values - high.astype(np.float64)).astype(np.float32).astype(ml_dtypes.bfloat16)
    return high, low


def make_tables():
    n = np.arange(NC)[:, None]
    k = np.arange(M)[None, :]
    t = 2.0 * np.pi * ((n * k) % NC) / NC
    forward = np.concatenate([np.cos(t), -np.sin(t)], axis=1)
    doubled = np.where(np.arange(M) == 0, 1.0, 2.0)
    doubled = np.concatenate([doubled, doubled]) / (NR * NC)
    table = np.zeros((NC, 128), np.float32)
    table[:, :24] = forward
    table = table.astype(ml_dtypes.bfloat16)

    def inverse(matrix):
        high, low = split_np(matrix.T)
        out = np.zeros((128, NC), ml_dtypes.bfloat16)
        out[0:24], out[24:48], out[48:72] = high, low, high
        return out

    rows = np.zeros((SP, 2, 16, 256))
    freq = np.where(np.arange(24) < M, np.arange(24), NR - 24 + np.arange(24))
    mode_row = np.zeros((SP, 2, 16, 32))
    for owner in range(SP):
        for q in range(QN):
            mode = owner * QN + q
            j, kk = mode // M, mode % M
            for r in range(RL):
                p = 2.0 * np.pi * ((freq[j] * r) % NR) / NR
                rows[owner, 0, q, r * 24 + kk] = np.cos(p)
                rows[owner, 0, q, r * 24 + 12 + kk] = np.sin(p)
                rows[owner, 1, q, r * 24 + kk] = -np.sin(p)
                rows[owner, 1, q, r * 24 + 12 + kk] = np.cos(p)
            mode_row[owner, :, q, j] = 1.0
    high, low = split_np(rows.reshape(SP * 32, 256))
    scale = np.zeros((1, 256), np.float32)
    scale[0, :192] = np.tile(doubled, RL)
    return (
        table,
        inverse(forward * doubled[None, :]),
        inverse(forward),
        high,
        low,
        mode_row.reshape(SP * 32, 32).astype(ml_dtypes.bfloat16),
        scale,
    )


TABLE, INVERSE, BACK, ROW_HIGH, ROW_LOW, MODE_ROW, SCALE = make_tables()


def dot(a, b):
    return lax.dot_general(a, b, (((1,), (0,)), ((), ())), preferred_element_type=F32)


def dot_nt(a, b):
    return lax.dot_general(a, b, (((1,), (1,)), ((), ())), preferred_element_type=F32)


def dot_tn(a, b):
    return lax.dot_general(a, b, (((0,), (0,)), ((), ())), preferred_element_type=F32)


def split(values):
    high = values.astype(BF)
    return high, (values - high.astype(F32)).astype(BF)


def gelu_parts(v):
    cdf = 0.5 * (1.0 + lax.erf(v * ROOT_HALF))
    return v * cdf, cdf + v * jnp.exp(-0.5 * v * v) * INV_ROOT_TAU


def store_taps(taps, i, x):
    col = lax.broadcasted_iota(jnp.int32, (CP, NC), 1)
    taps[i, 0:CP] = jnp.where(col == 0, 0.0, pltpu.roll(x, 1, 1)).astype(BF)
    taps[i, CP : 2 * CP] = x.astype(BF)
    taps[i, 2 * CP : 3 * CP] = jnp.where(col == NC - 1, 0.0, pltpu.roll(x, NC - 1, 1)).astype(BF)


def row_transform(cols, high, low):
    c_high, c_low = split(cols)
    return (dot_nt(high, c_high) + dot_nt(high, c_low) + dot_nt(low, c_high)).astype(BF)


def row_expand(modes, high, low):
    return dot_tn(modes, high) + dot_tn(modes, low)


def place_rows(rows, left):
    high, low = split(rows)
    high, low = high.astype(F32), low.astype(F32)
    left[...] = jnp.zeros_like(left)
    for lev in range(LEV):
        for r in range(RL):
            at = (lev * RL + r) * CO
            h = high[lev * 64 : lev * 64 + CO, r * 24 : r * 24 + 24]
            w = low[lev * 64 : lev * 64 + CO, r * 24 : r * 24 + 24]
            left[at : at + CO, 0:72] = jnp.concatenate([h, h, w], axis=1)


def kernel_a(place, field, table, high, low, mode_row, message, own_high, own_low, flat, cols):
    j = lax.broadcasted_iota(jnp.int32, (32, 128), 0)
    turn = ((j + jnp.where(j < M, 0, NR - 24)) * place[0]) % SP
    angle = turn.astype(F32) * (2.0 * math.pi / SP)
    t_high, t_low = split(jnp.concatenate([jnp.cos(angle), jnp.sin(angle)], axis=1))
    phase = (dot(mode_row[...], t_high) + dot(mode_row[...], t_low)).reshape(SP, 2, 16, 256)[:, 0]
    cosine, sine = phase[:, :, 0:128], phase[:, :, 128:256]
    cosine, sine = jnp.concatenate([cosine, cosine], axis=2), jnp.concatenate([sine, sine], axis=2)
    first = (high[...].astype(F32) + low[...].astype(F32)).reshape(SP, 2, 16, 256)
    re, im = first[:, 0], first[:, 1]
    turned = jnp.concatenate([(re * cosine + im * sine)[:, None], (im * cosine - re * sine)[:, None]], axis=1)
    h, w = split(turned.reshape(SP * 32, 256))
    own_high[...], own_low[...] = h, w
    flat[...] = dot(field[...], table[...])
    cols[...] = jnp.zeros_like(cols)
    for lev in range(LEV):
        for r in range(RL):
            part = flat[pl.ds(lev * C * RL + r, C, stride=RL), :]
            cols[lev * 64 : lev * 64 + C, r * 24 : r * 24 + 24] = part[:, 0:24]
    message[...] = row_transform(cols[...], h, w)


def prepare(one, two, point, w_one, w_two, w_two_back, w_one_back, w_point, w_point_back, base, wide):
    def spread(target, rows):
        wide[...] = jnp.zeros_like(wide)
        for t in range(4):
            wide[t * CP : (t + 1) * CP, t * rows : t * rows + base.shape[1]] = base[...]
        target[...] = wide[:, 0 : target.shape[1]].astype(BF)

    for kernel, forward, backward in ((one, w_one, w_one_back), (two, w_two, w_two_back)):
        base[...] = jnp.zeros_like(base)
        for a in range(3):
            for b in range(3):
                at = (a * 3 + b) * CP
                base[0:C, at : at + C] = jnp.transpose(kernel[a, b].astype(F32))
        spread(forward, GR)
        for a in range(3):
            for b in range(3):
                at = ((2 - a) * 3 + 2 - b) * CP
                base[0:C, at : at + C] = kernel[a, b].astype(F32)
        spread(backward, GR)
    for target, matrix in ((w_point, jnp.transpose(point[...].astype(F32))), (w_point_back, point[...].astype(F32))):
        wide[...] = jnp.zeros_like(wide)
        for t in range(4):
            wide[t * CP : t * CP + C, t * CP : t * CP + C] = matrix
        target[...] = wide[:, 0 : 4 * CP].astype(BF)


def kernel_rows(field, cot, one, two, point, after, rows, top, bottom, cot_rows, w_one, w_two, w_two_back, w_one_back, w_point, w_point_back, wide, base, spread):
    @pl.when(pl.program_id(0) == 0)
    def _():
        prepare(one, two, point, w_one, w_two, w_two_back, w_one_back, w_point, w_point_back, base, spread)

    for k, (source, target) in enumerate(((field, rows), (cot, cot_rows))):
        for n in range(0, NC, 128):
            wide[k, n // 128, 0 : C * RL, :] = source[0, :, n : n + 128].astype(F32)
            wide[k, n // 128, C * RL :, :] = jnp.zeros((12 * RL, 128), F32)
        for r in range(RL):
            for n in range(0, NC, 128):
                x = wide[k, n // 128, pl.ds(r, CP, stride=RL), :].astype(BF)
                target[0, r, :, n : n + 128] = x
                if k == 0 and r < 2:
                    top[0, r, :, n : n + 128] = x
                if k == 0 and r >= RL - 2:
                    bottom[0, r - RL + 2, :, n : n + 128] = x


def window(ref, i, count):
    return ref[i : i + count].reshape(count * GR, NC)


def kernel_b(place, rows, above, below, w_one, w_two, w_point, after, middle, slope, pre, taps, mid_taps):
    index = place[0]
    source = [above.at[0, 0], above.at[0, 1]] + [rows.at[0, r] for r in range(RL)] + [below.at[0, 0], below.at[0, 1]]
    for i, x in enumerate(source):
        store_taps(taps, i, x[...].astype(F32))
    rest = jnp.zeros((CP - CO, NC), F32)
    for start, count in ((0, 4), (4, 3), (7, 3)):
        d = dot(w_one[0 : CP * count, 0 : GR * (count + 2)], window(taps, start, count + 2))
        for t in range(count):
            i = start + t
            value, gradient = gelu_parts(d[t * CP : t * CP + CO])
            if i in (0, RL + 1):
                keep = jnp.where(index == (0 if i == 0 else SP - 1), 0.0, 1.0).astype(F32)
                value, gradient = value * keep, gradient * keep
            slope[0, i] = gradient
            value = jnp.concatenate([value, rest], axis=0)
            middle[0, i] = value.astype(BF)
            store_taps(mid_taps, i, value)
    for r in (0, 4):
        d = dot(w_two[...], window(mid_taps, r, 6))
        d = d + dot(w_point[...], rows[0, r : r + 4].reshape(4 * CP, NC))
        for t in range(4):
            pre[0, r + t] = d[t * CP : t * CP + CO]


def own_modes(received):
    return jnp.sum(received.astype(F32), axis=0)


def by_channel(own, real, imag):
    rest = jnp.zeros((96, 128), F32)
    real[...] = jnp.transpose(jnp.concatenate([own, rest], axis=0))
    imag[...] = jnp.transpose(jnp.concatenate([own[16:32], own[0:16], rest], axis=0))


def weight_rows(weight, lines):
    lines[...] = jnp.zeros_like(lines)
    lines[:, 0:C] = weight[...]


def mode_line(lines, q, part):
    return lines[pl.ds(2 * q + part, C, stride=2 * QN), :]


def kernel_mix(received, weight, message, kept, real, imag, mixed, lines):
    own = own_modes(received[...])
    kept[...] = own
    by_channel(own, real, imag)
    weight_rows(weight, lines)
    mixed[...] = jnp.zeros_like(mixed)
    for q in range(QN):
        w_re, w_im = mode_line(lines, q, 0), mode_line(lines, q, 1)
        re, im = [], []
        for lev in range(LEV):
            s_re = real[lev * 64 : lev * 64 + C, q : q + 1]
            s_im = imag[lev * 64 : lev * 64 + C, q : q + 1]
            re.append(jnp.sum(w_re * s_re - w_im * s_im, axis=0, keepdims=True))
            im.append(jnp.sum(w_im * s_re + w_re * s_im, axis=0, keepdims=True))
        mixed[q : q + 1] = re[0] + pltpu.roll(re[1], 64, 1)
        mixed[16 + q : 17 + q] = im[0] + pltpu.roll(im[1], 64, 1)
    message[...] = jnp.broadcast_to(mixed[0:32].astype(BF)[None], (SP, 32, 128))


def mix_back(own, lines, mixed):
    other = pltpu.roll(own, 64, 1)
    mixed[...] = jnp.zeros_like(mixed)
    for q in range(QN):
        w_re, w_im = mode_line(lines, q, 0), mode_line(lines, q, 1)
        for lev, z in enumerate((own, other)):
            z_re, z_im = z[q : q + 1], z[16 + q : 17 + q]
            at = lev * 64
            mixed[at : at + C, q : q + 1] = jnp.sum(w_re * z_re + w_im * z_im, axis=1, keepdims=True)
            mixed[at : at + C, 16 + q : 17 + q] = jnp.sum(w_re * z_im - w_im * z_re, axis=1, keepdims=True)
    return jnp.transpose(mixed[...])[0:32].astype(BF)


def kernel_spec_grad(p0, p1, p2, p3, after, grad, s_re, s_im, lines):
    pairs = (p0, p1, p2, p3)
    co = []
    for i, pair in enumerate(pairs):
        by_channel(pair[0:32], s_re.at[i], s_im.at[i])
        co.append((pair[32:64], pltpu.roll(pair[32:64], 64, 1)))
    for q in range(QN):
        res, ims = [], []
        for i in range(4):
            re, im = jnp.zeros((C, 128), F32), jnp.zeros((C, 128), F32)
            for lev in range(LEV):
                at = lev * 64
                a, b = s_re[i, at : at + C, q : q + 1], s_im[i, at : at + C, q : q + 1]
                x, y = co[i][lev][q : q + 1], co[i][lev][16 + q : 17 + q]
                re = re + (a * x + b * y)
                im = im + (a * y - b * x)
            res.append(re)
            ims.append(im)
        lines[pl.ds(2 * q, C, stride=2 * QN), :] = (res[0] + res[1]) + (res[2] + res[3])
        lines[pl.ds(2 * q + 1, C, stride=2 * QN), :] = (ims[0] + ims[1]) + (ims[2] + ims[3])
    grad[...] = lines[:, 0:C]


def kernel_d(received, high, low, inverse, pre, cot, table, scale, values, slopes, top, bottom, message, left, spec, kept, cols):
    lev = pl.program_id(0)

    @pl.when(lev == 0)
    def _():
        place_rows(row_expand(received[...], high[...], low[...]), left)
        spec[...] = dot(left[...].astype(BF), inverse[...]).reshape(LEV * RL, CO, NC)
        cols[...] = jnp.zeros_like(cols)

    rest = jnp.zeros((CP - CO, NC), F32)
    for r in range(RL):
        value, gradient = gelu_parts(pre[0, r] + spec[lev * RL + r])
        values[0, r] = jnp.concatenate([value, rest], axis=0).astype(BF)
        s = jnp.concatenate([gradient, rest], axis=0) * cot[0, r].astype(F32)
        s = s.astype(BF)
        slopes[0, r] = s
        if r < 2:
            top[0, r] = s
        if r >= RL - 2:
            bottom[0, r - RL + 2] = s
    kept[lev] = dot(slopes[0].reshape(RL * CP, NC), table[...])

    @pl.when(lev == LEV - 1)
    def _():
        for at in range(LEV):
            for r in range(RL):
                cols[at * 64 : at * 64 + CO, r * 24 : r * 24 + 24] = kept[at, r * CP : r * CP + CO, 0:24]
        message[...] = row_transform(cols[...] * scale[...], high[...], low[...])


def kernel_out(values, after, out, wide):
    for lev in range(LEV):
        for r in range(RL):
            for n in range(0, NC, 128):
                x = values[lev, r, :, n : n + 128].astype(F32)
                wide[n // 128, pl.ds(lev * C * RL + r, C, stride=RL), :] = x[0:C]
    for n in range(0, NC, 128):
        for lev in range(LEV):
            out[lev, :, n : n + 128] = wide[n // 128, lev * C * RL : (lev + 1) * C * RL].astype(BF)


def kernel_own(received, kept, first, second, sums):
    sums[0:32] = kept[...]
    sums[32:64] = own_modes(received[:, 0:32])
    sums[64:80] = own_modes(received[:, 32:48])


def kernel_mix_back(sums, weight, cofield, mixed, lines):
    weight_rows(weight, lines)
    cofield[...] = mix_back(sums[32:64], lines, mixed)


def kernel_send_back(cofield, p0, p1, p2, p3, message):
    total = (p0[64:80] + p1[64:80]) + (p2[64:80] + p3[64:80])
    high, low = split(total)
    message[...] = jnp.broadcast_to(jnp.concatenate([cofield[...], high, low], axis=0)[None], (SP, 64, 128))


def kernel_e_zero(slopes, middle, rows, grad_two, taps):
    left, right = [], []
    for r in range(RL):
        store_taps(taps, r, slopes[0, r].astype(F32))
        left.append(jnp.concatenate([middle[0, r], middle[0, r + 1], middle[0, r + 2], rows[0, r]], axis=0))
        right.append(taps[r])
    part = dot_nt(jnp.concatenate(left, axis=1), jnp.concatenate(right, axis=1))

    @pl.when(pl.program_id(0) == 0)
    def _():
        grad_two[...] = part

    @pl.when(pl.program_id(0) > 0)
    def _():
        grad_two[...] += part


def kernel_e(place, slopes, above, below, rows, f_above, f_below, slope, w_two, modes, grad_two, pre_slope, message, taps, pre_taps, grad_one, sums):
    index = place[0]
    lev = pl.program_id(0)
    source = [above.at[0, 0], above.at[0, 1]] + [slopes.at[0, r] for r in range(RL)] + [below.at[0, 0], below.at[0, 1]]
    for i, x in enumerate(source):
        store_taps(taps, i, x[...].astype(F32))
    rest = jnp.zeros((CP - CO, NC), F32)
    for start, count in ((0, 4), (4, 3), (7, 3)):
        d = dot(w_two[0 : CP * count, 0 : GR * (count + 2)], window(taps, start, count + 2))
        for t in range(count):
            i = start + t
            value = d[t * CP : t * CP + CO] * slope[0, i]
            if i in (0, RL + 1):
                value = value * jnp.where(index == (0 if i == 0 else SP - 1), 0.0, 1.0).astype(F32)
            value = jnp.concatenate([value, rest], axis=0)
            pre_slope[0, i] = value.astype(BF)
            store_taps(pre_taps, i, value)
    field = [f_above[0, 1]] + [rows[0, r] for r in range(RL)] + [f_below[0, 0]]
    left = jnp.concatenate([jnp.concatenate(field[r : r + 3], axis=0) for r in range(RL)], axis=1)
    right = jnp.concatenate([pre_taps[r + 1] for r in range(RL)], axis=1)
    part_one = dot_nt(left, right)

    @pl.when(lev == 0)
    def _():
        grad_one[...] = part_one

    @pl.when(lev == LEV - 1)
    def _():
        sums[...] = jnp.zeros_like(sums)
        two, one = grad_two[...], grad_one[...] + part_one
        for b in range(3):
            sums[b * GR : (b + 1) * GR, 0:CP] = two[0:GR, b * CP : (b + 1) * CP]
            sums[b * GR : (b + 1) * GR, 64 : 64 + CP] = one[:, b * CP : (b + 1) * CP]
        sums[3 * GR : 3 * GR + CP, 0:CP] = two[GR : GR + CP, CP : 2 * CP]
        message[:, 0:32] = modes[...]
        message[:, 32:48] = sums[...].reshape(SP, 16, 128).astype(BF)


def kernel_e_two(pre_slope, slopes, w_one, w_point, after, back, taps, wide):
    for i in range(RL + 2):
        store_taps(taps, i, pre_slope[0, i].astype(F32))
    for r in (0, 4):
        d = dot(w_one[...], window(taps, r, 6))
        d = d + dot(w_point[...], slopes[0, r : r + 4].reshape(4 * CP, NC))
        for t in range(4):
            for n in range(0, NC, 128):
                wide[n // 128, pl.ds(r + t, C, stride=RL), :] = d[t * CP : t * CP + C, n : n + 128]
    for n in range(0, NC, 128):
        back[0, :, n : n + 128] = wide[n // 128]


def kernel_f(received, high, low, inverse, back, out, point, one, two, left):
    lev = pl.program_id(0)

    @pl.when(lev == 0)
    def _():
        modes = received[:, 0:32].reshape(SP * 32, 128)
        r_high, r_low = split(row_expand(modes, high[...], low[...]))
        r_high, r_low = r_high.astype(F32), r_low.astype(F32)
        rest = jnp.zeros((C, 56), F32)
        for at in range(LEV):
            for r in range(RL):
                h = r_high[at * 64 : at * 64 + C, r * 24 : r * 24 + 24]
                w = r_low[at * 64 : at * 64 + C, r * 24 : r * 24 + 24]
                left[at, pl.ds(r, C, stride=RL), :] = jnp.concatenate([h, h, w, rest], axis=1)
        total = (received[:, 32:48].astype(F32) + received[:, 48:64].astype(F32)).reshape(SP * 16, 128)
        scaled = total * (1.0 / math.sqrt(NR * NC * LEV * 4))
        for a in range(3):
            for b in range(3):
                at = (2 - b) * GR + a * CP
                two[a, b] = scaled[at : at + C, 0:C]
                one[a, b] = scaled[at : at + C, 64 : 64 + C]
        point[...] = scaled[3 * GR : 3 * GR + C, 0:C]

    out[0] = (back[0] + dot(left[lev].astype(BF), inverse[...])).astype(BF)


def shape(dims, kind):
    return jax.ShapeDtypeStruct(dims, kind)


def params(mib):
    return pltpu.CompilerParams(vmem_limit_bytes=56 * 1024 * 1024)


def estimate(us):
    if us is None:
        return None
    return pl.CostEstimate(flops=us * 10**9, bytes_accessed=us * 3 * 10**6, transcendentals=0)


def level_spec(*dims):
    return pl.BlockSpec((1,) + dims, lambda lev: (lev,) + (0,) * len(dims))


def whole_spec(*dims):
    return pl.BlockSpec(dims, lambda lev: (0,) * len(dims))


def from_above(x):
    return lax.ppermute(x, "sp", [(i, i + 1) for i in range(SP - 1)])


def from_below(x):
    return lax.ppermute(x, "sp", [(i + 1, i) for i in range(SP - 1)])


def exchange(x):
    return lax.all_to_all(x, "sp", 0, 0, tiled=True)


def anywhere():
    return pl.BlockSpec(memory_space=pl.ANY)


def plain_call(kernel, operands, after, outs, scratch, mib, name, place=(), cost=None):
    vmem = pl.BlockSpec(memory_space=pltpu.VMEM)
    return pl.pallas_call(
        kernel,
        in_specs=[pl.BlockSpec(memory_space=pltpu.SMEM)] * len(place) + [vmem] * len(operands) + [anywhere()] * len(after),
        out_specs=[vmem] * len(outs),
        out_shape=outs,
        scratch_shapes=scratch,
        compiler_params=params(mib),
        cost_estimate=estimate(cost),
        name=name,
    )(*place, *operands, *after)


def local(field, cotangent, spec_weight, point_weight, kernel_one, kernel_two):
    place = lax.axis_index("sp").astype(jnp.int32).reshape(1)
    inputs = field.reshape(LEV * C * RL, NC)
    table = jnp.asarray(TABLE)
    weight = jnp.transpose(spec_weight, (1, 3, 0, 2)).reshape(C * QN * 2, C)
    strip = shape((LEV, 2, CP, NC), BF)
    grid_rows = shape((LEV, RL, CP, NC), BF)
    natural = shape((LEV, C * RL, NC), BF)
    flat, cols = pltpu.VMEM((LEV * C * RL, 128), F32), pltpu.VMEM((128, 256), F32)
    row_matrix = shape((SP * 32, 256), BF)
    message, high, low = plain_call(
        kernel_a,
        (inputs, table, jnp.asarray(ROW_HIGH), jnp.asarray(ROW_LOW), jnp.asarray(MODE_ROW)),
        (),
        [shape((SP * 32, 128), BF), row_matrix, row_matrix],
        [flat, cols],
        10,
        "field_modes",
        (place,),
    )
    arrived = exchange(message.reshape(SP, 32, 128))
    toeplitz, blocks = shape((4 * CP, 6 * GR), BF), shape((4 * CP, 4 * CP), BF)
    weights_out = [toeplitz] * 4 + [blocks] * 2
    rows, top, bottom, cot_rows, w_one, w_two, w_two_back, w_one_back, w_point, w_point_back = pl.pallas_call(
        kernel_rows,
        grid=(LEV,),
        in_specs=[
            level_spec(C * RL, NC),
            level_spec(C * RL, NC),
            whole_spec(3, 3, C, C),
            whole_spec(3, 3, C, C),
            whole_spec(C, C),
            anywhere(),
        ],
        out_specs=[level_spec(RL, CP, NC), level_spec(2, CP, NC), level_spec(2, CP, NC), level_spec(RL, CP, NC)]
        + [whole_spec(*x.shape) for x in weights_out],
        out_shape=[grid_rows, strip, strip, grid_rows] + weights_out,
        scratch_shapes=[
            pltpu.VMEM((2, NC // 128, (C + 12) * RL, 128), F32),
            pltpu.VMEM((CP, 9 * CP), F32),
            pltpu.VMEM((4 * CP, 6 * GR), F32),
        ],
        compiler_params=params(12),
        name="row_layout",
    )(field.reshape(natural.shape), cotangent.reshape(natural.shape), kernel_one, kernel_two, point_weight, message)
    f_above, f_below = from_above(bottom), from_below(top)

    square, lines = pltpu.VMEM((128, 128), F32), pltpu.VMEM((C * QN * 2, 128), F32)
    mixed, kept = plain_call(
        kernel_mix,
        (arrived, weight),
        (),
        [shape((SP, 32, 128), BF), shape((32, 128), F32)],
        [square, square, square, lines],
        6,
        "mode_mix",
    )
    gathered = exchange(mixed).reshape(SP * 32, 128)

    middle, slope, pre = pl.pallas_call(
        kernel_b,
        grid=(LEV,),
        in_specs=[
            pl.BlockSpec(memory_space=pltpu.SMEM),
            level_spec(RL, CP, NC),
            level_spec(2, CP, NC),
            level_spec(2, CP, NC),
            whole_spec(4 * CP, 6 * GR),
            whole_spec(4 * CP, 6 * GR),
            whole_spec(4 * CP, 4 * CP),
            anywhere(),
        ],
        out_specs=[
            level_spec(RL + 2, CP, NC),
            level_spec(RL + 2, CO, NC),
            level_spec(RL, CO, NC),
        ],
        out_shape=[
            shape((LEV, RL + 2, CP, NC), BF),
            shape((LEV, RL + 2, CO, NC), F32),
            shape((LEV, RL, CO, NC), F32),
        ],
        scratch_shapes=[pltpu.VMEM((RL + 4, GR, NC), BF), pltpu.VMEM((RL + 2, GR, NC), BF)],
        compiler_params=params(28),
        name="two_convolutions",
    )(place, rows, f_above, f_below, w_one, w_two, w_point, mixed)

    left, spec = pltpu.VMEM((LEV * RL * CO, 128), F32), pltpu.VMEM((LEV * RL * CO, NC), F32)
    values, slopes, s_top, s_bottom, message = pl.pallas_call(
        kernel_d,
        grid=(LEV,),
        in_specs=[
            whole_spec(SP * 32, 128),
            whole_spec(SP * 32, 256),
            whole_spec(SP * 32, 256),
            whole_spec(128, NC),
            level_spec(RL, CO, NC),
            level_spec(RL, CP, NC),
            whole_spec(NC, 128),
            whole_spec(1, 256),
        ],
        out_specs=[level_spec(RL, CP, NC)] * 2 + [level_spec(2, CP, NC)] * 2 + [whole_spec(SP * 32, 128)],
        out_shape=[grid_rows, grid_rows, strip, strip, shape((SP * 32, 128), BF)],
        scratch_shapes=[
            left,
            pltpu.VMEM((LEV * RL, CO, NC), F32),
            pltpu.VMEM((LEV, RL * CP, 128), F32),
            cols,
        ],
        compiler_params=params(22),
        name="output_and_slope",
    )(gathered, high, low, jnp.asarray(INVERSE), pre, cot_rows, table, jnp.asarray(SCALE))
    s_above, s_below = from_above(s_bottom), from_below(s_top)

    grad_two = pl.pallas_call(
        kernel_e_zero,
        grid=(LEV,),
        in_specs=[level_spec(RL, CP, NC), level_spec(RL + 2, CP, NC), level_spec(RL, CP, NC)],
        scratch_shapes=[pltpu.VMEM((RL, GR, NC), BF)],
        out_specs=whole_spec(GR + CP, GR),
        out_shape=shape((GR + CP, GR), F32),
        compiler_params=params(22),
        name="weight_gradients_two",
    )(slopes, middle, rows)
    pre_slope, message = pl.pallas_call(
        kernel_e,
        grid=(LEV,),
        in_specs=[
            pl.BlockSpec(memory_space=pltpu.SMEM),
            level_spec(RL, CP, NC),
            level_spec(2, CP, NC),
            level_spec(2, CP, NC),
            level_spec(RL, CP, NC),
            level_spec(2, CP, NC),
            level_spec(2, CP, NC),
            level_spec(RL + 2, CO, NC),
            whole_spec(4 * CP, 6 * GR),
            whole_spec(SP, 32, 128),
            whole_spec(GR + CP, GR),
        ],
        out_specs=[level_spec(RL + 2, CP, NC), whole_spec(SP, 48, 128)],
        out_shape=[shape((LEV, RL + 2, CP, NC), BF), shape((SP, 48, 128), BF)],
        scratch_shapes=[
            pltpu.VMEM((RL + 4, GR, NC), BF),
            pltpu.VMEM((RL + 2, GR, NC), BF),
            pltpu.VMEM((GR, GR), F32),
            pltpu.VMEM((SP * 16, 128), F32),
        ],
        compiler_params=params(28),
        name="slope_and_weight_gradients",
    )(place, slopes, s_above, s_below, rows, f_above, f_below, slope, w_two_back, message.reshape(SP, 32, 128), grad_two)
    arrived = exchange(message)
    back = pl.pallas_call(
        kernel_e_two,
        grid=(LEV,),
        in_specs=[
            level_spec(RL + 2, CP, NC),
            level_spec(RL, CP, NC),
            whole_spec(4 * CP, 6 * GR),
            whole_spec(4 * CP, 4 * CP),
            anywhere(),
        ],
        out_specs=level_spec(C * RL, NC),
        out_shape=shape(natural.shape, F32),
        scratch_shapes=[pltpu.VMEM((RL + 2, GR, NC), BF), pltpu.VMEM((NC // 128, C * RL, 128), F32)],
        compiler_params=params(22),
        name="backward_convolution",
    )(pre_slope, slopes, w_one_back, w_point_back, message)
    (out,) = plain_call(
        kernel_out,
        (values,),
        (message,),
        [natural],
        [pltpu.VMEM((NC // 128, LEV * C * RL, 128), F32)],
        10,
        "output_layout",
    )
    (sums,) = plain_call(
        kernel_own, (arrived, kept), (back, out), [shape((80, 128), F32)], [], 4, "own_sums"
    )
    others = [lax.ppermute(sums, "rep", [(i, i ^ k) for i in range(4)]) for k in (1, 2, 3)]
    (cofield,) = plain_call(
        kernel_mix_back, (sums, weight), (), [shape((32, 128), BF)], [square, lines], 6, "mode_mix_back"
    )
    (message,) = plain_call(
        kernel_send_back, (cofield, sums, *others), (), [shape((SP, 64, 128), BF)], [], 4, "gradient_modes"
    )
    gathered = exchange(message)
    (spec_grad,) = plain_call(
        kernel_spec_grad,
        (sums, *others),
        (message,),
        [shape(weight.shape, F32)],
        [pltpu.VMEM((4, 128, 128), F32)] * 2 + [lines],
        8,
        "spectral_gradient",
    )
    kernel_out_shape = shape((3, 3, C, C), F32)
    field_grad, point_total, one_total, two_total = pl.pallas_call(
        kernel_f,
        grid=(LEV,),
        in_specs=[
            whole_spec(SP, 64, 128),
            whole_spec(SP * 32, 256),
            whole_spec(SP * 32, 256),
            whole_spec(128, NC),
            level_spec(C * RL, NC),
        ],
        out_specs=[level_spec(C * RL, NC), whole_spec(C, C), whole_spec(3, 3, C, C), whole_spec(3, 3, C, C)],
        out_shape=[natural, shape((C, C), F32), kernel_out_shape, kernel_out_shape],
        scratch_shapes=[pltpu.VMEM((LEV, C * RL, 128), F32)],
        compiler_params=params(18),
        name="field_gradient",
    )(gathered, high, low, jnp.asarray(BACK), back)
    spec_total = jnp.transpose(spec_grad.reshape(C, QN, 2, C), (2, 0, 3, 1))
    return (
        out.reshape(field.shape),
        field_grad.reshape(field.shape),
        spec_total,
        point_total,
        one_total,
        two_total,
    )


def solution(mesh):
    specs = (
        P("rep", None, None, "sp", None),
        P("rep", None, None, "sp", None),
        P(None, None, None, "sp"),
        P(),
        P(),
        P(),
    )
    return jax.shard_map(local, mesh=mesh, in_specs=specs, out_specs=specs, check_vma=False)
```

```python
import math

import jax
import jax.numpy as jnp
import numpy as np
import ml_dtypes
from jax import lax
from jax.experimental import pallas as pl
from jax.experimental.pallas import tpu as pltpu
from jax.sharding import PartitionSpec as P

M = 12
C = 36
CP = 48
CO = 40
LEV = 2
RL = 8
NC = 1024
NR = 256
SP = 32
QN = 9
GR = 3 * CP

ROOT_HALF = 0.7071067811865476
INV_ROOT_TAU = 0.3989422804014327
BF = jnp.bfloat16
F32 = jnp.float32


def split_np(values):
    high = values.astype(np.float32).astype(ml_dtypes.bfloat16)
    low = (values - high.astype(np.float64)).astype(np.float32).astype(ml_dtypes.bfloat16)
    return high, low


def make_tables():
    n = np.arange(NC)[:, None]
    k = np.arange(M)[None, :]
    t = 2.0 * np.pi * ((n * k) % NC) / NC
    forward = np.concatenate([np.cos(t), -np.sin(t)], axis=1)
    doubled = np.where(np.arange(M) == 0, 1.0, 2.0)
    doubled = np.concatenate([doubled, doubled]) / (NR * NC)
    table = np.zeros((NC, 128), np.float32)
    table[:, :24] = forward
    table = table.astype(ml_dtypes.bfloat16)

    def inverse(matrix):
        high, low = split_np(matrix.T)
        out = np.zeros((128, NC), ml_dtypes.bfloat16)
        out[0:24], out[24:48], out[48:72] = high, low, high
        return out

    rows = np.zeros((SP, 2, 16, 256))
    freq = np.where(np.arange(24) < M, np.arange(24), NR - 24 + np.arange(24))
    mode_row = np.zeros((SP, 2, 16, 32))
    for owner in range(SP):
        for q in range(QN):
            mode = owner * QN + q
            j, kk = mode // M, mode % M
            for r in range(RL):
                p = 2.0 * np.pi * ((freq[j] * r) % NR) / NR
                rows[owner, 0, q, r * 24 + kk] = np.cos(p)
                rows[owner, 0, q, r * 24 + 12 + kk] = np.sin(p)
                rows[owner, 1, q, r * 24 + kk] = -np.sin(p)
                rows[owner, 1, q, r * 24 + 12 + kk] = np.cos(p)
            mode_row[owner, :, q, j] = 1.0
    high, low = split_np(rows.reshape(SP * 32, 256))
    scale = np.zeros((1, 256), np.float32)
    scale[0, :192] = np.tile(doubled, RL)
    return (
        table,
        inverse(forward * doubled[None, :]),
        inverse(forward),
        high,
        low,
        mode_row.reshape(SP * 32, 32).astype(ml_dtypes.bfloat16),
        scale,
    )


TABLE, INVERSE, BACK, ROW_HIGH, ROW_LOW, MODE_ROW, SCALE = make_tables()


def dot(a, b):
    return lax.dot_general(a, b, (((1,), (0,)), ((), ())), preferred_element_type=F32)


def dot_nt(a, b):
    return lax.dot_general(a, b, (((1,), (1,)), ((), ())), preferred_element_type=F32)


def dot_tn(a, b):
    return lax.dot_general(a, b, (((0,), (0,)), ((), ())), preferred_element_type=F32)


def split(values):
    high = values.astype(BF)
    return high, (values - high.astype(F32)).astype(BF)


def gelu_parts(v):
    cdf = 0.5 * (1.0 + lax.erf(v * ROOT_HALF))
    return v * cdf, cdf + v * jnp.exp(-0.5 * v * v) * INV_ROOT_TAU


def store_taps(taps, i, x):
    col = lax.broadcasted_iota(jnp.int32, (CP, NC), 1)
    taps[i, 0:CP] = jnp.where(col == 0, 0.0, pltpu.roll(x, 1, 1)).astype(BF)
    taps[i, CP : 2 * CP] = x.astype(BF)
    taps[i, 2 * CP : 3 * CP] = jnp.where(col == NC - 1, 0.0, pltpu.roll(x, NC - 1, 1)).astype(BF)


def row_transform(cols, high, low):
    c_high, c_low = split(cols)
    both = dot_nt(high, jnp.concatenate([c_high, c_low], axis=0))
    return (both[:, 0:128] + both[:, 128:256] + dot_nt(low, c_high)).astype(BF)


def row_expand(modes, high, low):
    both = dot_tn(modes, jnp.concatenate([high, low], axis=1))
    return both[:, 0:256] + both[:, 256:512]


def strip_pair(even, top, bottom):
    top, bottom = [jnp.concatenate([x[0:CO].astype(F32) for x in rows], axis=0) for rows in (top, bottom)]
    return jnp.where(even, bottom, top).astype(BF), jnp.where(even, top, bottom).astype(BF)


def halo_rows(even, first, second):
    first, second = first[0].astype(F32), second[0].astype(F32)
    above, below = jnp.where(even, second, first), jnp.where(even, first, second)
    rest = jnp.zeros((CP - CO, NC), F32)
    return [jnp.concatenate([x[i * CO : (i + 1) * CO], rest], axis=0) for x in (above, below) for i in range(2)]


def place_rows(rows, left):
    high, low = split(rows)
    high, low = high.astype(F32), low.astype(F32)
    left[...] = jnp.zeros_like(left)
    for lev in range(LEV):
        for r in range(RL):
            at = (lev * RL + r) * CO
            h = high[lev * 64 : lev * 64 + CO, r * 24 : r * 24 + 24]
            w = low[lev * 64 : lev * 64 + CO, r * 24 : r * 24 + 24]
            left[at : at + CO, 0:72] = jnp.concatenate([h, h, w], axis=1)


def kernel_a(place, field, table, high, low, mode_row, message, own_high, own_low, flat, cols):
    j = lax.broadcasted_iota(jnp.int32, (32, 128), 0)
    turn = ((j + jnp.where(j < M, 0, NR - 24)) * place[0]) % SP
    angle = turn.astype(F32) * (2.0 * math.pi / SP)
    t_high, t_low = split(jnp.concatenate([jnp.cos(angle), jnp.sin(angle)], axis=1))
    phase = (dot(mode_row[...], t_high) + dot(mode_row[...], t_low)).reshape(SP, 2, 16, 256)[:, 0]
    cosine, sine = phase[:, :, 0:128], phase[:, :, 128:256]
    cosine, sine = jnp.concatenate([cosine, cosine], axis=2), jnp.concatenate([sine, sine], axis=2)
    first = (high[...].astype(F32) + low[...].astype(F32)).reshape(SP, 2, 16, 256)
    re, im = first[:, 0], first[:, 1]
    turned = jnp.concatenate([(re * cosine + im * sine)[:, None], (im * cosine - re * sine)[:, None]], axis=1)
    h, w = split(turned.reshape(SP * 32, 256))
    own_high[...], own_low[...] = h, w
    flat[...] = dot(field[...], table[...])
    cols[...] = jnp.zeros_like(cols)
    for lev in range(LEV):
        for r in range(RL):
            part = flat[pl.ds(lev * C * RL + r, C, stride=RL), :]
            cols[lev * 64 : lev * 64 + C, r * 24 : r * 24 + 24] = part[:, 0:24]
    message[...] = row_transform(cols[...], h, w)


def prepare(one, two, point, w_one, w_two, w_two_back, w_one_back, w_point, w_point_back, base, wide):
    def spread(target, rows):
        wide[...] = jnp.zeros_like(wide)
        for t in range(4):
            wide[t * CP : (t + 1) * CP, t * rows : t * rows + base.shape[1]] = base[...]
        target[...] = wide[:, 0 : target.shape[1]].astype(BF)

    for kernel, forward, backward in ((one, w_one, w_one_back), (two, w_two, w_two_back)):
        base[...] = jnp.zeros_like(base)
        for a in range(3):
            for b in range(3):
                at = (a * 3 + b) * CP
                base[0:C, at : at + C] = jnp.transpose(kernel[a, b].astype(F32))
        spread(forward, GR)
        for a in range(3):
            for b in range(3):
                at = ((2 - a) * 3 + 2 - b) * CP
                base[0:C, at : at + C] = kernel[a, b].astype(F32)
        spread(backward, GR)
    for target, matrix in ((w_point, jnp.transpose(point[...].astype(F32))), (w_point_back, point[...].astype(F32))):
        wide[...] = jnp.zeros_like(wide)
        for t in range(4):
            wide[t * CP : t * CP + C, t * CP : t * CP + C] = matrix
        target[...] = wide[:, 0 : 4 * CP].astype(BF)


def kernel_rows(place, field, cot, one, two, point, after, rows, strip_one, strip_two, cot_rows, w_one, w_two, w_two_back, w_one_back, w_point, w_point_back, wide, base, spread):
    even = place[0] % 2 == 0

    @pl.when(pl.program_id(0) == 0)
    def _():
        prepare(one, two, point, w_one, w_two, w_two_back, w_one_back, w_point, w_point_back, base, spread)

    for k, (source, target) in enumerate(((field, rows), (cot, cot_rows))):
        for n in range(0, NC, 128):
            wide[k, n // 128, 0 : C * RL, :] = source[0, :, n : n + 128].astype(F32)
            wide[k, n // 128, C * RL :, :] = jnp.zeros((12 * RL, 128), F32)
        for n in range(0, NC, 128):
            found = [wide[k, n // 128, pl.ds(r, CP, stride=RL), :] for r in range(RL)]
            for r in range(RL):
                target[0, r, :, n : n + 128] = found[r].astype(BF)
            if k == 0:
                x, y = strip_pair(even, found[0:2], found[RL - 2 :])
                strip_one[0, :, n : n + 128], strip_two[0, :, n : n + 128] = x, y


def window(ref, i, count):
    return ref[i : i + count].reshape(count * GR, NC)


def kernel_b(place, rows, first, second, w_one, w_two, w_point, after, middle, slope, pre, taps, mid_taps):
    index = place[0]
    halo = halo_rows(index % 2 == 0, first, second)
    for i, x in enumerate(halo[0:2] + [rows[0, r].astype(F32) for r in range(RL)] + halo[2:4]):
        store_taps(taps, i, x)
    rest = jnp.zeros((CP - CO, NC), F32)
    for start, count in ((0, 4), (4, 3), (7, 3)):
        d = dot(w_one[0 : CP * count, 0 : GR * (count + 2)], window(taps, start, count + 2))
        for t in range(count):
            i = start + t
            value, gradient = gelu_parts(d[t * CP : t * CP + CO])
            if i in (0, RL + 1):
                keep = jnp.where(index == (0 if i == 0 else SP - 1), 0.0, 1.0).astype(F32)
                value, gradient = value * keep, gradient * keep
            slope[0, i] = jnp.concatenate([gradient, rest], axis=0).astype(BF)
            value = jnp.concatenate([value, rest], axis=0)
            middle[0, i] = value.astype(BF)
            store_taps(mid_taps, i, value)
    for r in (0, 4):
        d = dot(w_two[...], window(mid_taps, r, 6))
        d = d + dot(w_point[...], rows[0, r : r + 4].reshape(4 * CP, NC))
        for t in range(4):
            pre[0, r + t] = d[t * CP : t * CP + CO]


def own_modes(received):
    return jnp.sum(received.astype(F32), axis=0)


def by_channel(own, real, imag):
    rest = jnp.zeros((96, 128), F32)
    real[...] = jnp.transpose(jnp.concatenate([own, rest], axis=0))
    imag[...] = jnp.transpose(jnp.concatenate([own[16:32], own[0:16], rest], axis=0))


def weight_rows(weight, lines):
    lines[...] = jnp.zeros_like(lines)
    lines[:, 0:C] = weight[...]


def mode_line(lines, q, part):
    return lines[pl.ds(2 * q + part, C, stride=2 * QN), :]


def kernel_mix(received, weight, message, kept, real, imag, mixed, lines):
    own = own_modes(received[...])
    kept[...] = own
    by_channel(own, real, imag)
    weight_rows(weight, lines)
    mixed[...] = jnp.zeros_like(mixed)
    for q in range(QN):
        w_re, w_im = mode_line(lines, q, 0), mode_line(lines, q, 1)
        re, im = [], []
        for lev in range(LEV):
            s_re = real[lev * 64 : lev * 64 + C, q : q + 1]
            s_im = imag[lev * 64 : lev * 64 + C, q : q + 1]
            re.append(jnp.sum(w_re * s_re - w_im * s_im, axis=0, keepdims=True))
            im.append(jnp.sum(w_im * s_re + w_re * s_im, axis=0, keepdims=True))
        mixed[q : q + 1] = re[0] + pltpu.roll(re[1], 64, 1)
        mixed[16 + q : 17 + q] = im[0] + pltpu.roll(im[1], 64, 1)
    message[...] = jnp.broadcast_to(mixed[0:32].astype(BF)[None], (SP, 32, 128))


def mix_back(own, lines, mixed):
    other = pltpu.roll(own, 64, 1)
    mixed[...] = jnp.zeros_like(mixed)
    for q in range(QN):
        w_re, w_im = mode_line(lines, q, 0), mode_line(lines, q, 1)
        for lev, z in enumerate((own, other)):
            z_re, z_im = z[q : q + 1], z[16 + q : 17 + q]
            at = lev * 64
            mixed[at : at + C, q : q + 1] = jnp.sum(w_re * z_re + w_im * z_im, axis=1, keepdims=True)
            mixed[at : at + C, 16 + q : 17 + q] = jnp.sum(w_re * z_im - w_im * z_re, axis=1, keepdims=True)
    return jnp.transpose(mixed[...])[0:32].astype(BF)


def kernel_spec_grad(p0, p1, p2, p3, after, grad, s_re, s_im, lines):
    pairs = (p0, p1, p2, p3)
    co = []
    for i, pair in enumerate(pairs):
        by_channel(pair[0:32], s_re.at[i], s_im.at[i])
        co.append((pair[32:64], pltpu.roll(pair[32:64], 64, 1)))
    for q in range(QN):
        res, ims = [], []
        for i in range(4):
            re, im = jnp.zeros((C, 128), F32), jnp.zeros((C, 128), F32)
            for lev in range(LEV):
                at = lev * 64
                a, b = s_re[i, at : at + C, q : q + 1], s_im[i, at : at + C, q : q + 1]
                x, y = co[i][lev][q : q + 1], co[i][lev][16 + q : 17 + q]
                re = re + (a * x + b * y)
                im = im + (a * y - b * x)
            res.append(re)
            ims.append(im)
        lines[pl.ds(2 * q, C, stride=2 * QN), :] = (res[0] + res[1]) + (res[2] + res[3])
        lines[pl.ds(2 * q + 1, C, stride=2 * QN), :] = (ims[0] + ims[1]) + (ims[2] + ims[3])
    grad[...] = lines[:, 0:C]


def kernel_d(place, received, high, low, inverse, pre, cot, table, scale, values, slopes, strip_one, strip_two, message, left, spec, kept, cols):
    lev = pl.program_id(0)

    @pl.when(lev == 0)
    def _():
        place_rows(row_expand(received[...], high[...], low[...]), left)
        spec[...] = dot(left[...].astype(BF), inverse[...]).reshape(LEV * RL, CO, NC)
        cols[...] = jnp.zeros_like(cols)

    rest = jnp.zeros((CP - CO, NC), F32)
    edges = {}
    for r in range(RL):
        value, gradient = gelu_parts(pre[0, r] + spec[lev * RL + r])
        values[0, r] = jnp.concatenate([value, rest], axis=0).astype(BF)
        s = jnp.concatenate([gradient, rest], axis=0) * cot[0, r].astype(F32)
        slopes[0, r] = s.astype(BF)
        edges[r] = s
    x, y = strip_pair(place[0] % 2 == 0, [edges[0], edges[1]], [edges[RL - 2], edges[RL - 1]])
    strip_one[0], strip_two[0] = x, y
    kept[lev] = dot(slopes[0].reshape(RL * CP, NC), table[...])

    @pl.when(lev == LEV - 1)
    def _():
        for at in range(LEV):
            for r in range(RL):
                cols[at * 64 : at * 64 + CO, r * 24 : r * 24 + 24] = kept[at, r * CP : r * CP + CO, 0:24]
        message[...] = row_transform(cols[...] * scale[...], high[...], low[...])


def kernel_out(values, after, out, wide):
    for lev in range(LEV):
        for r in range(RL):
            for n in range(0, NC, 128):
                x = values[lev, r, :, n : n + 128].astype(F32)
                wide[n // 128, pl.ds(lev * C * RL + r, C, stride=RL), :] = x[0:C]
    for n in range(0, NC, 128):
        for lev in range(LEV):
            out[lev, :, n : n + 128] = wide[n // 128, lev * C * RL : (lev + 1) * C * RL].astype(BF)


def kernel_own(received, kept, first, second, sums):
    sums[0:32] = kept[...]
    sums[32:64] = own_modes(received[:, 0:32])
    sums[64:80] = own_modes(received[:, 32:48])


def kernel_mix_back(sums, weight, cofield, mixed, lines):
    weight_rows(weight, lines)
    cofield[...] = mix_back(sums[32:64], lines, mixed)


def kernel_send_back(cofield, p0, p1, p2, p3, message):
    total = (p0[64:80] + p1[64:80]) + (p2[64:80] + p3[64:80])
    high, low = split(total)
    message[...] = jnp.broadcast_to(jnp.concatenate([cofield[...], high, low], axis=0)[None], (SP, 64, 128))


def kernel_e_zero(slopes, middle, rows, grad_two, taps):
    left, right = [], []
    for r in range(RL):
        store_taps(taps, r, slopes[0, r].astype(F32))
        left.append(jnp.concatenate([middle[0, r], middle[0, r + 1], middle[0, r + 2], rows[0, r]], axis=0))
        right.append(taps[r])
    part = dot_nt(jnp.concatenate(left, axis=1), jnp.concatenate(right, axis=1))

    @pl.when(pl.program_id(0) == 0)
    def _():
        grad_two[...] = part

    @pl.when(pl.program_id(0) > 0)
    def _():
        grad_two[...] += part


def kernel_e(place, slopes, first, second, rows, f_first, f_second, slope, w_two, modes, grad_two, pre_slope, message, taps, pre_taps, grad_one, sums):
    index = place[0]
    lev = pl.program_id(0)
    even = index % 2 == 0
    halo = halo_rows(even, first, second)
    for i, x in enumerate(halo[0:2] + [slopes[0, r].astype(F32) for r in range(RL)] + halo[2:4]):
        store_taps(taps, i, x)
    rest = jnp.zeros((CP - CO, NC), F32)
    for start, count in ((0, 4), (4, 3), (7, 3)):
        d = dot(w_two[0 : CP * count, 0 : GR * (count + 2)], window(taps, start, count + 2))
        for t in range(count):
            i = start + t
            value = d[t * CP : t * CP + CO] * slope[0, i].astype(F32)[0:CO]
            if i in (0, RL + 1):
                value = value * jnp.where(index == (0 if i == 0 else SP - 1), 0.0, 1.0).astype(F32)
            value = jnp.concatenate([value, rest], axis=0)
            pre_slope[0, i] = value.astype(BF)
            store_taps(pre_taps, i, value)
    halo = halo_rows(even, f_first, f_second)
    field = [halo[1].astype(BF)] + [rows[0, r] for r in range(RL)] + [halo[2].astype(BF)]
    left = jnp.concatenate([jnp.concatenate(field[r : r + 3], axis=0) for r in range(RL)], axis=1)
    right = jnp.concatenate([pre_taps[r + 1] for r in range(RL)], axis=1)
    part_one = dot_nt(left, right)

    @pl.when(lev == 0)
    def _():
        grad_one[...] = part_one

    @pl.when(lev == LEV - 1)
    def _():
        sums[...] = jnp.zeros_like(sums)
        two, one = grad_two[...], grad_one[...] + part_one
        for b in range(3):
            sums[b * GR : (b + 1) * GR, 0:CP] = two[0:GR, b * CP : (b + 1) * CP]
            sums[b * GR : (b + 1) * GR, 64 : 64 + CP] = one[:, b * CP : (b + 1) * CP]
        sums[3 * GR : 3 * GR + CP, 0:CP] = two[GR : GR + CP, CP : 2 * CP]
        message[:, 0:32] = modes[...]
        message[:, 32:48] = sums[...].reshape(SP, 16, 128).astype(BF)


def kernel_e_two(pre_slope, slopes, w_one, w_point, after, back, taps, wide):
    for i in range(RL + 2):
        store_taps(taps, i, pre_slope[0, i].astype(F32))
    for r in (0, 4):
        d = dot(w_one[...], window(taps, r, 6))
        d = d + dot(w_point[...], slopes[0, r : r + 4].reshape(4 * CP, NC))
        for t in range(4):
            for n in range(0, NC, 128):
                wide[n // 128, pl.ds(r + t, C, stride=RL), :] = d[t * CP : t * CP + C, n : n + 128]
    for n in range(0, NC, 128):
        back[0, :, n : n + 128] = wide[n // 128]


def kernel_f(received, high, low, inverse, back, out, point, one, two, left):
    lev = pl.program_id(0)

    @pl.when(lev == 0)
    def _():
        modes = received[:, 0:32].reshape(SP * 32, 128)
        r_high, r_low = split(row_expand(modes, high[...], low[...]))
        r_high, r_low = r_high.astype(F32), r_low.astype(F32)
        rest = jnp.zeros((C, 56), F32)
        for at in range(LEV):
            for r in range(RL):
                h = r_high[at * 64 : at * 64 + C, r * 24 : r * 24 + 24]
                w = r_low[at * 64 : at * 64 + C, r * 24 : r * 24 + 24]
                left[at, pl.ds(r, C, stride=RL), :] = jnp.concatenate([h, h, w, rest], axis=1)
        total = (received[:, 32:48].astype(F32) + received[:, 48:64].astype(F32)).reshape(SP * 16, 128)
        scaled = total * (1.0 / math.sqrt(NR * NC * LEV * 4))
        for a in range(3):
            for b in range(3):
                at = (2 - b) * GR + a * CP
                two[a, b] = scaled[at : at + C, 0:C]
                one[a, b] = scaled[at : at + C, 64 : 64 + C]
        point[...] = scaled[3 * GR : 3 * GR + C, 0:C]

    out[0] = (back[0] + dot(left[lev].astype(BF), inverse[...])).astype(BF)


def shape(dims, kind):
    return jax.ShapeDtypeStruct(dims, kind)


def params(mib):
    return pltpu.CompilerParams(vmem_limit_bytes=mib * 1024 * 1024)


def estimate(us):
    if us is None:
        return None
    return pl.CostEstimate(flops=us * 10**9, bytes_accessed=us * 3 * 10**6, transcendentals=0)


def level_spec(*dims):
    return pl.BlockSpec((1,) + dims, lambda lev: (lev,) + (0,) * len(dims))


def whole_spec(*dims):
    return pl.BlockSpec(dims, lambda lev: (0,) * len(dims))


def partners(first, second):
    pairs = [(i, i ^ 1) for i in range(SP)]
    others = [(i, i + 1) for i in range(1, SP - 1, 2)] + [(i + 1, i) for i in range(1, SP - 1, 2)]
    return lax.ppermute(first, "sp", pairs), lax.ppermute(second, "sp", others)


def exchange(x):
    return lax.all_to_all(x, "sp", 0, 0, tiled=True)


def anywhere():
    return pl.BlockSpec(memory_space=pl.ANY)


def plain_call(kernel, operands, after, outs, scratch, mib, name, place=(), cost=None):
    vmem = pl.BlockSpec(memory_space=pltpu.VMEM)
    return pl.pallas_call(
        kernel,
        in_specs=[pl.BlockSpec(memory_space=pltpu.SMEM)] * len(place) + [vmem] * len(operands) + [anywhere()] * len(after),
        out_specs=[vmem] * len(outs),
        out_shape=outs,
        scratch_shapes=scratch,
        compiler_params=params(mib),
        cost_estimate=estimate(cost),
        name=name,
    )(*place, *operands, *after)


def local(field, cotangent, spec_weight, point_weight, kernel_one, kernel_two):
    place = lax.axis_index("sp").astype(jnp.int32).reshape(1)
    inputs = field.reshape(LEV * C * RL, NC)
    table = jnp.asarray(TABLE)
    weight = jnp.transpose(spec_weight, (1, 3, 0, 2)).reshape(C * QN * 2, C)
    strip = shape((LEV, 2 * CO, NC), BF)
    grid_rows = shape((LEV, RL, CP, NC), BF)
    natural = shape((LEV, C * RL, NC), BF)
    flat, cols = pltpu.VMEM((LEV * C * RL, 128), F32), pltpu.VMEM((128, 256), F32)
    row_matrix = shape((SP * 32, 256), BF)
    message, high, low = plain_call(
        kernel_a,
        (inputs, table, jnp.asarray(ROW_HIGH), jnp.asarray(ROW_LOW), jnp.asarray(MODE_ROW)),
        (),
        [shape((SP * 32, 128), BF), row_matrix, row_matrix],
        [flat, cols],
        56,
        "field_modes",
        (place,),
    )
    arrived = exchange(message.reshape(SP, 32, 128))
    toeplitz, blocks = shape((4 * CP, 6 * GR), BF), shape((4 * CP, 4 * CP), BF)
    weights_out = [toeplitz] * 4 + [blocks] * 2
    rows, f_first, f_second, cot_rows, w_one, w_two, w_two_back, w_one_back, w_point, w_point_back = pl.pallas_call(
        kernel_rows,
        grid=(LEV,),
        in_specs=[
            pl.BlockSpec(memory_space=pltpu.SMEM),
            level_spec(C * RL, NC),
            level_spec(C * RL, NC),
            whole_spec(3, 3, C, C),
            whole_spec(3, 3, C, C),
            whole_spec(C, C),
            anywhere(),
        ],
        out_specs=[level_spec(RL, CP, NC), level_spec(2 * CO, NC), level_spec(2 * CO, NC), level_spec(RL, CP, NC)]
        + [whole_spec(*x.shape) for x in weights_out],
        out_shape=[grid_rows, strip, strip, grid_rows] + weights_out,
        scratch_shapes=[
            pltpu.VMEM((2, NC // 128, (C + 12) * RL, 128), F32),
            pltpu.VMEM((CP, 9 * CP), F32),
            pltpu.VMEM((4 * CP, 6 * GR), F32),
        ],
        compiler_params=params(56),
        name="row_layout",
    )(place, field.reshape(natural.shape), cotangent.reshape(natural.shape), kernel_one, kernel_two, point_weight, message)
    f_first, f_second = partners(f_first, f_second)

    square, lines = pltpu.VMEM((128, 128), F32), pltpu.VMEM((C * QN * 2, 128), F32)
    mixed, kept = plain_call(
        kernel_mix,
        (arrived, weight),
        (),
        [shape((SP, 32, 128), BF), shape((32, 128), F32)],
        [square, square, square, lines],
        8,
        "mode_mix",
    )
    gathered = exchange(mixed).reshape(SP * 32, 128)

    middle, slope, pre = pl.pallas_call(
        kernel_b,
        grid=(LEV,),
        in_specs=[
            pl.BlockSpec(memory_space=pltpu.SMEM),
            level_spec(RL, CP, NC),
            level_spec(2 * CO, NC),
            level_spec(2 * CO, NC),
            whole_spec(4 * CP, 6 * GR),
            whole_spec(4 * CP, 6 * GR),
            whole_spec(4 * CP, 4 * CP),
            anywhere(),
        ],
        out_specs=[
            level_spec(RL + 2, CP, NC),
            level_spec(RL + 2, CP, NC),
            level_spec(RL, CO, NC),
        ],
        out_shape=[
            shape((LEV, RL + 2, CP, NC), BF),
            shape((LEV, RL + 2, CP, NC), BF),
            shape((LEV, RL, CO, NC), F32),
        ],
        scratch_shapes=[pltpu.VMEM((RL + 4, GR, NC), BF), pltpu.VMEM((RL + 2, GR, NC), BF)],
        compiler_params=params(56),
        name="two_convolutions",
    )(place, rows, f_first, f_second, w_one, w_two, w_point, mixed)

    left, spec = pltpu.VMEM((LEV * RL * CO, 128), F32), pltpu.VMEM((LEV * RL * CO, NC), F32)
    values, slopes, s_first, s_second, message = pl.pallas_call(
        kernel_d,
        grid=(LEV,),
        in_specs=[
            pl.BlockSpec(memory_space=pltpu.SMEM),
            whole_spec(SP * 32, 128),
            whole_spec(SP * 32, 256),
            whole_spec(SP * 32, 256),
            whole_spec(128, NC),
            level_spec(RL, CO, NC),
            level_spec(RL, CP, NC),
            whole_spec(NC, 128),
            whole_spec(1, 256),
        ],
        out_specs=[level_spec(RL, CP, NC)] * 2 + [level_spec(2 * CO, NC)] * 2 + [whole_spec(SP * 32, 128)],
        out_shape=[grid_rows, grid_rows, strip, strip, shape((SP * 32, 128), BF)],
        scratch_shapes=[
            left,
            pltpu.VMEM((LEV * RL, CO, NC), F32),
            pltpu.VMEM((LEV, RL * CP, 128), F32),
            cols,
        ],
        compiler_params=params(56),
        name="output_and_slope",
    )(place, gathered, high, low, jnp.asarray(INVERSE), pre, cot_rows, table, jnp.asarray(SCALE))
    s_first, s_second = partners(s_first, s_second)

    grad_two = pl.pallas_call(
        kernel_e_zero,
        grid=(LEV,),
        in_specs=[level_spec(RL, CP, NC), level_spec(RL + 2, CP, NC), level_spec(RL, CP, NC)],
        scratch_shapes=[pltpu.VMEM((RL, GR, NC), BF)],
        out_specs=whole_spec(GR + CP, GR),
        out_shape=shape((GR + CP, GR), F32),
        compiler_params=params(56),
        name="weight_gradients_two",
    )(slopes, middle, rows)
    pre_slope, message = pl.pallas_call(
        kernel_e,
        grid=(LEV,),
        in_specs=[
            pl.BlockSpec(memory_space=pltpu.SMEM),
            level_spec(RL, CP, NC),
            level_spec(2 * CO, NC),
            level_spec(2 * CO, NC),
            level_spec(RL, CP, NC),
            level_spec(2 * CO, NC),
            level_spec(2 * CO, NC),
            level_spec(RL + 2, CP, NC),
            whole_spec(4 * CP, 6 * GR),
            whole_spec(SP, 32, 128),
            whole_spec(GR + CP, GR),
        ],
        out_specs=[level_spec(RL + 2, CP, NC), whole_spec(SP, 48, 128)],
        out_shape=[shape((LEV, RL + 2, CP, NC), BF), shape((SP, 48, 128), BF)],
        scratch_shapes=[
            pltpu.VMEM((RL + 4, GR, NC), BF),
            pltpu.VMEM((RL + 2, GR, NC), BF),
            pltpu.VMEM((GR, GR), F32),
            pltpu.VMEM((SP * 16, 128), F32),
        ],
        compiler_params=params(56),
        name="slope_and_weight_gradients",
    )(place, slopes, s_first, s_second, rows, f_first, f_second, slope, w_two_back, message.reshape(SP, 32, 128), grad_two)
    arrived = exchange(message)
    back = pl.pallas_call(
        kernel_e_two,
        grid=(LEV,),
        in_specs=[
            level_spec(RL + 2, CP, NC),
            level_spec(RL, CP, NC),
            whole_spec(4 * CP, 6 * GR),
            whole_spec(4 * CP, 4 * CP),
            anywhere(),
        ],
        out_specs=level_spec(C * RL, NC),
        out_shape=shape(natural.shape, F32),
        scratch_shapes=[pltpu.VMEM((RL + 2, GR, NC), BF), pltpu.VMEM((NC // 128, C * RL, 128), F32)],
        compiler_params=params(56),
        name="backward_convolution",
    )(pre_slope, slopes, w_one_back, w_point_back, message)
    (out,) = plain_call(
        kernel_out,
        (values,),
        (message,),
        [natural],
        [pltpu.VMEM((NC // 128, LEV * C * RL, 128), F32)],
        56,
        "output_layout",
    )
    (sums,) = plain_call(
        kernel_own, (arrived, kept), (back, out), [shape((80, 128), F32)], [], 56, "own_sums"
    )
    others = [lax.ppermute(sums, "rep", [(i, i ^ k) for i in range(4)]) for k in (1, 2, 3)]
    (cofield,) = plain_call(
        kernel_mix_back, (sums, weight), (), [shape((32, 128), BF)], [square, lines], 56, "mode_mix_back"
    )
    (message,) = plain_call(
        kernel_send_back, (cofield, sums, *others), (), [shape((SP, 64, 128), BF)], [], 56, "gradient_modes"
    )
    gathered = exchange(message)
    (spec_grad,) = plain_call(
        kernel_spec_grad,
        (sums, *others),
        (message,),
        [shape(weight.shape, F32)],
        [pltpu.VMEM((4, 128, 128), F32)] * 2 + [lines],
        56,
        "spectral_gradient",
    )
    kernel_out_shape = shape((3, 3, C, C), F32)
    field_grad, point_total, one_total, two_total = pl.pallas_call(
        kernel_f,
        grid=(LEV,),
        in_specs=[
            whole_spec(SP, 64, 128),
            whole_spec(SP * 32, 256),
            whole_spec(SP * 32, 256),
            whole_spec(128, NC),
            level_spec(C * RL, NC),
        ],
        out_specs=[level_spec(C * RL, NC), whole_spec(C, C), whole_spec(3, 3, C, C), whole_spec(3, 3, C, C)],
        out_shape=[natural, shape((C, C), F32), kernel_out_shape, kernel_out_shape],
        scratch_shapes=[pltpu.VMEM((LEV, C * RL, 128), F32)],
        compiler_params=params(56),
        name="field_gradient",
    )(gathered, high, low, jnp.asarray(BACK), back)
    spec_total = jnp.transpose(spec_grad.reshape(C, QN, 2, C), (2, 0, 3, 1))
    return (
        out.reshape(field.shape),
        field_grad.reshape(field.shape),
        spec_total,
        point_total,
        one_total,
        two_total,
    )


def solution(mesh):
    specs = (
        P("rep", None, None, "sp", None),
        P("rep", None, None, "sp", None),
        P(None, None, None, "sp"),
        P(),
        P(),
        P(),
    )
    return jax.shard_map(local, mesh=mesh, in_specs=specs, out_specs=specs, check_vma=False)
```

```python
import math

import jax
import jax.numpy as jnp
import numpy as np
import ml_dtypes
from jax import lax
from jax.experimental import pallas as pl
from jax.experimental.pallas import tpu as pltpu
from jax.sharding import PartitionSpec as P

M = 12
C = 36
CP = 48
CO = 40
LEV = 2
RL = 8
NC = 1024
NR = 256
SP = 32
QN = 9
GR = 3 * CP
SHARE = 14

ROOT_HALF = 0.7071067811865476
INV_ROOT_TAU = 0.3989422804014327
BF = jnp.bfloat16
F32 = jnp.float32


def split_np(values):
    high = values.astype(np.float32).astype(ml_dtypes.bfloat16)
    low = (values - high.astype(np.float64)).astype(np.float32).astype(ml_dtypes.bfloat16)
    return high, low


def make_tables():
    n = np.arange(NC)[:, None]
    k = np.arange(M)[None, :]
    t = 2.0 * np.pi * ((n * k) % NC) / NC
    forward = np.concatenate([np.cos(t), -np.sin(t)], axis=1)
    doubled = np.where(np.arange(M) == 0, 1.0, 2.0)
    doubled = np.concatenate([doubled, doubled]) / (NR * NC)
    table = np.zeros((NC, 128), np.float32)
    table[:, :24] = forward
    table = table.astype(ml_dtypes.bfloat16)

    def inverse(matrix):
        high, low = split_np(matrix.T)
        out = np.zeros((128, NC), ml_dtypes.bfloat16)
        out[0:24], out[24:48], out[48:72] = high, low, high
        return out

    rows, turned = np.zeros((SP, 32, 256)), np.zeros((SP, 32, 256))
    freq = np.where(np.arange(24) < M, np.arange(24), NR - 24 + np.arange(24))
    mode_row = np.zeros((SP, 32, 32))
    for owner in range(SP):
        for q in range(QN):
            mode = owner * QN + q
            j, kk = mode // M, mode % M
            for r in range(RL):
                p = 2.0 * np.pi * ((freq[j] * r) % NR) / NR
                for x, line, sign in ((rows, q, 1.0), (turned, QN + q, -1.0)):
                    x[owner, line, r * 24 + kk] = sign * np.cos(p)
                    x[owner, line, r * 24 + 12 + kk] = sign * np.sin(p)
                for x, line in ((rows, QN + q), (turned, q)):
                    x[owner, line, r * 24 + kk] = -np.sin(p)
                    x[owner, line, r * 24 + 12 + kk] = np.cos(p)
            mode_row[owner, q, j] = mode_row[owner, QN + q, j] = 1.0
    rows, turned = split_np(rows.reshape(SP * 32, 256)), split_np(turned.reshape(SP * 32, 256))
    scale = np.zeros((1, 256), np.float32)
    scale[0, :192] = np.tile(doubled, RL)
    return (
        table,
        inverse(forward * doubled[None, :]),
        inverse(forward),
        rows,
        turned,
        mode_row.reshape(SP * 32, 32).astype(ml_dtypes.bfloat16),
        scale,
    )


TABLE, INVERSE, BACK, ROWS, ROWS_TURNED, MODE_ROW, SCALE = make_tables()


def dot(a, b):
    return lax.dot_general(a, b, (((1,), (0,)), ((), ())), preferred_element_type=F32)


def dot_nt(a, b):
    return lax.dot_general(a, b, (((1,), (1,)), ((), ())), preferred_element_type=F32)


def dot_tn(a, b):
    return lax.dot_general(a, b, (((0,), (0,)), ((), ())), preferred_element_type=F32)


def split(values):
    high = values.astype(BF)
    return high, (values - high.astype(F32)).astype(BF)


def gelu_parts(v):
    cdf = 0.5 * (1.0 + lax.erf(v * ROOT_HALF))
    return v * cdf, cdf + v * jnp.exp(-0.5 * v * v) * INV_ROOT_TAU


def store_taps(taps, i, x):
    col = lax.broadcasted_iota(jnp.int32, (CP, NC), 1)
    taps[i, 0:CP] = jnp.where(col == 0, 0.0, pltpu.roll(x, 1, 1)).astype(BF)
    taps[i, CP : 2 * CP] = x.astype(BF)
    taps[i, 2 * CP : 3 * CP] = jnp.where(col == NC - 1, 0.0, pltpu.roll(x, NC - 1, 1)).astype(BF)


def row_transform(cols, high, low):
    c_high, c_low = split(cols)
    both = dot_nt(high, jnp.concatenate([c_high, c_low], axis=0))
    return (both[:, 0:128] + both[:, 128:256] + dot_nt(low, c_high)).astype(BF)


def row_expand(modes, high, low):
    both = dot_tn(modes, jnp.concatenate([high, low], axis=1))
    return both[:, 0:256] + both[:, 256:512]


def strip_pair(even, top, bottom):
    top, bottom = [jnp.concatenate([x[0:CO].astype(F32) for x in rows], axis=0) for rows in (top, bottom)]
    return jnp.where(even, bottom, top).astype(BF), jnp.where(even, top, bottom).astype(BF)


def halo_rows(even, first, second):
    first, second = first[0].astype(F32), second[0].astype(F32)
    above, below = jnp.where(even, second, first), jnp.where(even, first, second)
    rest = jnp.zeros((CP - CO, NC), F32)
    return [jnp.concatenate([x[i * CO : (i + 1) * CO], rest], axis=0) for x in (above, below) for i in range(2)]


def place_rows(rows, left):
    high, low = split(rows)
    high, low = high.astype(F32), low.astype(F32)
    left[...] = jnp.zeros_like(left)
    for lev in range(LEV):
        for r in range(RL):
            at = (lev * RL + r) * CO
            h = high[lev * 64 : lev * 64 + CO, r * 24 : r * 24 + 24]
            w = low[lev * 64 : lev * 64 + CO, r * 24 : r * 24 + 24]
            left[at : at + CO, 0:72] = jnp.concatenate([h, h, w], axis=1)


def kernel_a(place, field, table, high, low, turned_high, turned_low, mode_row, message, own_high, own_low, flat, cols):
    j = lax.broadcasted_iota(jnp.int32, (32, 128), 0)
    turn = ((j + jnp.where(j < M, 0, NR - 24)) * place[0]) % SP
    angle = turn.astype(F32) * (2.0 * math.pi / SP)
    t_high, t_low = split(jnp.concatenate([jnp.cos(angle), jnp.sin(angle)], axis=1))
    phase = dot(mode_row[...], t_high) + dot(mode_row[...], t_low)
    cosine, sine = phase[:, 0:128], phase[:, 128:256]
    cosine, sine = jnp.concatenate([cosine, cosine], axis=1), jnp.concatenate([sine, sine], axis=1)
    first = high[...].astype(F32) + low[...].astype(F32)
    turned = turned_high[...].astype(F32) + turned_low[...].astype(F32)
    turned = first * cosine + turned * sine
    h, w = split(turned)
    own_high[...], own_low[...] = h, w
    flat[...] = dot(field[...], table[...])
    cols[...] = jnp.zeros_like(cols)
    for lev in range(LEV):
        for r in range(RL):
            part = flat[pl.ds(lev * C * RL + r, C, stride=RL), :]
            cols[lev * 64 : lev * 64 + C, r * 24 : r * 24 + 24] = part[:, 0:24]
    message[...] = row_transform(cols[...], h, w)


def prepare(one, two, point, w_one, w_two, w_two_back, w_one_back, w_point, w_point_back, base, wide):
    def spread(target, rows):
        wide[...] = jnp.zeros_like(wide)
        for t in range(4):
            wide[t * CP : (t + 1) * CP, t * rows : t * rows + base.shape[1]] = base[...]
        target[...] = wide[:, 0 : target.shape[1]].astype(BF)

    for kernel, forward, backward in ((one, w_one, w_one_back), (two, w_two, w_two_back)):
        base[...] = jnp.zeros_like(base)
        for a in range(3):
            for b in range(3):
                at = (a * 3 + b) * CP
                base[0:C, at : at + C] = jnp.transpose(kernel[a, b].astype(F32))
        spread(forward, GR)
        for a in range(3):
            for b in range(3):
                at = ((2 - a) * 3 + 2 - b) * CP
                base[0:C, at : at + C] = kernel[a, b].astype(F32)
        spread(backward, GR)
    for target, matrix in ((w_point, jnp.transpose(point[...].astype(F32))), (w_point_back, point[...].astype(F32))):
        wide[...] = jnp.zeros_like(wide)
        for t in range(4):
            wide[t * CP : t * CP + C, t * CP : t * CP + C] = matrix
        target[...] = wide[:, 0 : 4 * CP].astype(BF)


def kernel_rows(place, field, cot, one, two, point, after, rows, strip_one, strip_two, cot_rows, w_one, w_two, w_two_back, w_one_back, w_point, w_point_back, wide, base, spread):
    even = place[0] % 2 == 0

    @pl.when(pl.program_id(0) == 0)
    def _():
        prepare(one, two, point, w_one, w_two, w_two_back, w_one_back, w_point, w_point_back, base, spread)

    for k, (source, target) in enumerate(((field, rows), (cot, cot_rows))):
        for n in range(0, NC, 128):
            wide[k, n // 128, 0 : C * RL, :] = source[0, :, n : n + 128].astype(F32)
            wide[k, n // 128, C * RL :, :] = jnp.zeros((12 * RL, 128), F32)
        for n in range(0, NC, 128):
            found = [wide[k, n // 128, pl.ds(r, CP, stride=RL), :] for r in range(RL)]
            for r in range(RL):
                target[0, r, :, n : n + 128] = found[r].astype(BF)
            if k == 0:
                x, y = strip_pair(even, found[0:2], found[RL - 2 :])
                strip_one[0, :, n : n + 128], strip_two[0, :, n : n + 128] = x, y


def window(ref, i, count):
    return ref[i : i + count].reshape(count * GR, NC)


def kernel_b(place, rows, first, second, w_one, w_two, w_point, middle, slope, pre, taps, mid_taps):
    index = place[0]
    halo = halo_rows(index % 2 == 0, first, second)
    for i, x in enumerate(halo[0:2] + [rows[0, r].astype(F32) for r in range(RL)] + halo[2:4]):
        store_taps(taps, i, x)
    rest = jnp.zeros((CP - CO, NC), F32)
    for start, count in ((0, 4), (4, 3), (7, 3)):
        d = dot(w_one[0 : CP * count, 0 : GR * (count + 2)], window(taps, start, count + 2))
        for t in range(count):
            i = start + t
            value, gradient = gelu_parts(d[t * CP : t * CP + CO])
            if i in (0, RL + 1):
                keep = jnp.where(index == (0 if i == 0 else SP - 1), 0.0, 1.0).astype(F32)
                value, gradient = value * keep, gradient * keep
            slope[0, i] = jnp.concatenate([gradient, rest], axis=0).astype(BF)
            value = jnp.concatenate([value, rest], axis=0)
            middle[0, i] = value.astype(BF)
            store_taps(mid_taps, i, value)
    for r in (0, 4):
        d = dot(w_two[...], window(mid_taps, r, 6))
        d = d + dot(w_point[...], rows[0, r : r + 4].reshape(4 * CP, NC))
        for t in range(4):
            pre[0, r + t] = d[t * CP : t * CP + CO]


def own_modes(received):
    return jnp.sum(received.astype(F32), axis=0)


def by_channel(own, real, imag):
    rest = jnp.zeros((96, 128), F32)
    real[...] = jnp.transpose(jnp.concatenate([own, rest], axis=0))
    imag[...] = jnp.transpose(jnp.concatenate([pltpu.roll(own, 32 - QN, 0), rest], axis=0))


def weight_rows(weight, lines):
    lines[...] = jnp.zeros_like(lines)
    lines[:, 0:C] = weight[...]


def mode_line(lines, q, part):
    return lines[pl.ds(2 * q + part, C, stride=2 * QN), :]


def kernel_mix(received, weight, message, kept, real, imag, mixed, lines):
    own = own_modes(received[...])
    kept[...] = own
    by_channel(own, real, imag)
    weight_rows(weight, lines)
    mixed[...] = jnp.zeros_like(mixed)
    for q in range(QN):
        w_re, w_im = mode_line(lines, q, 0), mode_line(lines, q, 1)
        re, im = [], []
        for lev in range(LEV):
            s_re = real[lev * 64 : lev * 64 + C, q : q + 1]
            s_im = imag[lev * 64 : lev * 64 + C, q : q + 1]
            re.append(jnp.sum(w_re * s_re - w_im * s_im, axis=0, keepdims=True))
            im.append(jnp.sum(w_im * s_re + w_re * s_im, axis=0, keepdims=True))
        mixed[q : q + 1] = re[0] + pltpu.roll(re[1], 64, 1)
        mixed[QN + q : QN + q + 1] = im[0] + pltpu.roll(im[1], 64, 1)
    message[...] = jnp.broadcast_to(mixed[0:32].astype(BF)[None], (SP, 32, 128))


def mix_back(own, lines, mixed):
    other = pltpu.roll(own, 64, 1)
    mixed[...] = jnp.zeros_like(mixed)
    for q in range(QN):
        w_re, w_im = mode_line(lines, q, 0), mode_line(lines, q, 1)
        for lev, z in enumerate((own, other)):
            z_re, z_im = z[q : q + 1], z[QN + q : QN + q + 1]
            at = lev * 64
            mixed[at : at + C, q : q + 1] = jnp.sum(w_re * z_re + w_im * z_im, axis=1, keepdims=True)
            mixed[at : at + C, QN + q : QN + q + 1] = jnp.sum(w_re * z_im - w_im * z_re, axis=1, keepdims=True)
    return jnp.transpose(mixed[...])[0:32].astype(BF)


def kernel_spec_grad(p0, p1, p2, p3, grad, s_re, s_im, lines):
    pairs = (p0, p1, p2, p3)
    co = []
    for i, pair in enumerate(pairs):
        by_channel(pair[0:32], s_re.at[i], s_im.at[i])
        co.append((pair[32:64], pltpu.roll(pair[32:64], 64, 1)))
    for q in range(QN):
        res, ims = [], []
        for i in range(4):
            re, im = jnp.zeros((C, 128), F32), jnp.zeros((C, 128), F32)
            for lev in range(LEV):
                at = lev * 64
                a, b = s_re[i, at : at + C, q : q + 1], s_im[i, at : at + C, q : q + 1]
                x, y = co[i][lev][q : q + 1], co[i][lev][QN + q : QN + q + 1]
                re = re + (a * x + b * y)
                im = im + (a * y - b * x)
            res.append(re)
            ims.append(im)
        lines[pl.ds(2 * q, C, stride=2 * QN), :] = (res[0] + res[1]) + (res[2] + res[3])
        lines[pl.ds(2 * q + 1, C, stride=2 * QN), :] = (ims[0] + ims[1]) + (ims[2] + ims[3])
    grad[...] = lines[:, 0:C]


def kernel_d(place, received, high, low, inverse, pre, cot, table, scale, values, slopes, strip_one, strip_two, message, left, spec, kept, cols):
    lev = pl.program_id(0)

    @pl.when(lev == 0)
    def _():
        place_rows(row_expand(received[...], high[...], low[...]), left)
        spec[...] = dot(left[...].astype(BF), inverse[...]).reshape(LEV * RL, CO, NC)
        cols[...] = jnp.zeros_like(cols)

    rest = jnp.zeros((CP - CO, NC), F32)
    edges = {}
    for r in range(RL):
        value, gradient = gelu_parts(pre[0, r] + spec[lev * RL + r])
        values[0, r] = jnp.concatenate([value, rest], axis=0).astype(BF)
        s = jnp.concatenate([gradient, rest], axis=0) * cot[0, r].astype(F32)
        slopes[0, r] = s.astype(BF)
        edges[r] = s
    x, y = strip_pair(place[0] % 2 == 0, [edges[0], edges[1]], [edges[RL - 2], edges[RL - 1]])
    strip_one[0], strip_two[0] = x, y
    kept[lev] = dot(slopes[0].reshape(RL * CP, NC), table[...])

    @pl.when(lev == LEV - 1)
    def _():
        for at in range(LEV):
            for r in range(RL):
                cols[at * 64 : at * 64 + CO, r * 24 : r * 24 + 24] = kept[at, r * CP : r * CP + CO, 0:24]
        message[...] = row_transform(cols[...] * scale[...], high[...], low[...])


def kernel_out(values, after, out, wide):
    for lev in range(LEV):
        for r in range(RL):
            for n in range(0, NC, 128):
                x = values[lev, r, :, n : n + 128].astype(F32)
                wide[n // 128, pl.ds(lev * C * RL + r, C, stride=RL), :] = x[0:C]
    for n in range(0, NC, 128):
        for lev in range(LEV):
            out[lev, :, n : n + 128] = wide[n // 128, lev * C * RL : (lev + 1) * C * RL].astype(BF)


def kernel_own(received, kept, sums):
    sums[0:32] = kept[...]
    sums[32:64] = own_modes(received[...])


def kernel_mix_back(sums, weight, cofield, mixed, lines):
    weight_rows(weight, lines)
    cofield[...] = mix_back(sums[32:64], lines, mixed)


def kernel_send_back(cofield, p0, p1, p2, p3, message):
    total = (p0[32:64] + p1[32:64]) + (p2[32:64] + p3[32:64])
    row = lax.broadcasted_iota(jnp.int32, (32, 128), 0)
    total = jnp.where(row < 2 * QN, cofield[...].astype(F32), total).astype(BF)
    message[...] = jnp.broadcast_to(total[None], (SP, 32, 128))


def kernel_e_zero(slopes, middle, rows, grad_two, taps):
    left, right = [], []
    for r in range(RL):
        store_taps(taps, r, slopes[0, r].astype(F32))
        left.append(jnp.concatenate([middle[0, r], middle[0, r + 1], middle[0, r + 2], rows[0, r]], axis=0))
        right.append(taps[r])
    part = dot_nt(jnp.concatenate(left, axis=1), jnp.concatenate(right, axis=1))

    @pl.when(pl.program_id(0) == 0)
    def _():
        grad_two[...] = part

    @pl.when(pl.program_id(0) > 0)
    def _():
        grad_two[...] += part


def kernel_e(place, slopes, first, second, rows, f_first, f_second, slope, w_two, modes, grad_two, pre_slope, message, taps, pre_taps, grad_one, sums, packed):
    index = place[0]
    lev = pl.program_id(0)
    even = index % 2 == 0
    halo = halo_rows(even, first, second)
    for i, x in enumerate(halo[0:2] + [slopes[0, r].astype(F32) for r in range(RL)] + halo[2:4]):
        store_taps(taps, i, x)
    rest = jnp.zeros((CP - CO, NC), F32)
    for start, count in ((0, 4), (4, 3), (7, 3)):
        d = dot(w_two[0 : CP * count, 0 : GR * (count + 2)], window(taps, start, count + 2))
        for t in range(count):
            i = start + t
            value = d[t * CP : t * CP + CO] * slope[0, i].astype(F32)[0:CO]
            if i in (0, RL + 1):
                value = value * jnp.where(index == (0 if i == 0 else SP - 1), 0.0, 1.0).astype(F32)
            value = jnp.concatenate([value, rest], axis=0)
            pre_slope[0, i] = value.astype(BF)
            store_taps(pre_taps, i, value)
    halo = halo_rows(even, f_first, f_second)
    field = [halo[1].astype(BF)] + [rows[0, r] for r in range(RL)] + [halo[2].astype(BF)]
    left = jnp.concatenate([jnp.concatenate(field[r : r + 3], axis=0) for r in range(RL)], axis=1)
    right = jnp.concatenate([pre_taps[r + 1] for r in range(RL)], axis=1)
    part_one = dot_nt(left, right)

    @pl.when(lev == 0)
    def _():
        grad_one[...] = part_one

    @pl.when(lev == LEV - 1)
    def _():
        sums[...] = jnp.zeros_like(sums)
        two, one = grad_two[...], grad_one[...] + part_one
        for b in range(3):
            at = b * CP
            sums[b * GR : (b + 1) * GR, 0:C] = two[0:GR, at : at + C]
            sums[b * GR : (b + 1) * GR, C : 2 * C] = one[:, at : at + C]
        sums[0:CP, 2 * C : 3 * C] = two[GR : GR + CP, CP : CP + C]
        packed[...] = modes[...].astype(F32)
        for owner in range(SP):
            packed[owner, 2 * QN : 32] = sums[owner * SHARE : (owner + 1) * SHARE]
        message[...] = packed[...].astype(BF)


def kernel_e_two(pre_slope, slopes, w_one, w_point, after, back, taps, wide):
    for i in range(RL + 2):
        store_taps(taps, i, pre_slope[0, i].astype(F32))
    for r in (0, 4):
        d = dot(w_one[...], window(taps, r, 6))
        d = d + dot(w_point[...], slopes[0, r : r + 4].reshape(4 * CP, NC))
        for t in range(4):
            for n in range(0, NC, 128):
                wide[n // 128, pl.ds(r + t, C, stride=RL), :] = d[t * CP : t * CP + C, n : n + 128]
    for n in range(0, NC, 128):
        back[0, :, n : n + 128] = wide[n // 128]


def kernel_f(received, high, low, inverse, back, out, point, one, two, left, packed, sums):
    lev = pl.program_id(0)

    @pl.when(lev == 0)
    def _():
        modes = received[...].reshape(SP * 32, 128)
        r_high, r_low = split(row_expand(modes, high[...], low[...]))
        r_high, r_low = r_high.astype(F32), r_low.astype(F32)
        rest = jnp.zeros((C, 56), F32)
        for at in range(LEV):
            for r in range(RL):
                h = r_high[at * 64 : at * 64 + C, r * 24 : r * 24 + 24]
                w = r_low[at * 64 : at * 64 + C, r * 24 : r * 24 + 24]
                left[at, pl.ds(r, C, stride=RL), :] = jnp.concatenate([h, h, w, rest], axis=1)
        packed[...] = received[...].astype(F32)
        for owner in range(SP):
            sums[owner * SHARE : (owner + 1) * SHARE] = packed[owner, 2 * QN : 32]
        scaled = sums[...] * (1.0 / math.sqrt(NR * NC * LEV * 4))
        for a in range(3):
            for b in range(3):
                at = (2 - b) * GR + a * CP
                two[a, b] = scaled[at : at + C, 0:C]
                one[a, b] = scaled[at : at + C, C : 2 * C]
        point[...] = scaled[0:C, 2 * C : 3 * C]

    out[0] = (back[0] + dot(left[lev].astype(BF), inverse[...])).astype(BF)


def shape(dims, kind):
    return jax.ShapeDtypeStruct(dims, kind)


def params(mib):
    return pltpu.CompilerParams(vmem_limit_bytes=mib * 1024 * 1024)


def estimate(us):
    if us is None:
        return None
    return pl.CostEstimate(flops=us * 10**9, bytes_accessed=us * 3 * 10**6, transcendentals=0)


def level_spec(*dims):
    return pl.BlockSpec((1,) + dims, lambda lev: (lev,) + (0,) * len(dims))


def whole_spec(*dims):
    return pl.BlockSpec(dims, lambda lev: (0,) * len(dims))


def partners(first, second):
    pairs = [(i, i ^ 1) for i in range(SP)]
    others = [(i, i + 1) for i in range(1, SP - 1, 2)] + [(i + 1, i) for i in range(1, SP - 1, 2)]
    return lax.ppermute(first, "sp", pairs), lax.ppermute(second, "sp", others)


def exchange(x):
    return lax.all_to_all(x, "sp", 0, 0, tiled=True)


def anywhere():
    return pl.BlockSpec(memory_space=pl.ANY)


def plain_call(kernel, operands, after, outs, scratch, mib, name, place=(), cost=None):
    vmem = pl.BlockSpec(memory_space=pltpu.VMEM)
    return pl.pallas_call(
        kernel,
        in_specs=[pl.BlockSpec(memory_space=pltpu.SMEM)] * len(place) + [vmem] * len(operands) + [anywhere()] * len(after),
        out_specs=[vmem] * len(outs),
        out_shape=outs,
        scratch_shapes=scratch,
        compiler_params=params(mib),
        cost_estimate=estimate(cost),
        name=name,
    )(*place, *operands, *after)


def local(field, cotangent, spec_weight, point_weight, kernel_one, kernel_two):
    place = lax.axis_index("sp").astype(jnp.int32).reshape(1)
    inputs = field.reshape(LEV * C * RL, NC)
    table = jnp.asarray(TABLE)
    weight = jnp.transpose(spec_weight, (1, 3, 0, 2)).reshape(C * QN * 2, C)
    strip = shape((LEV, 2 * CO, NC), BF)
    grid_rows = shape((LEV, RL, CP, NC), BF)
    natural = shape((LEV, C * RL, NC), BF)
    flat, cols = pltpu.VMEM((LEV * C * RL, 128), F32), pltpu.VMEM((128, 256), F32)
    row_matrix = shape((SP * 32, 256), BF)
    message, high, low = plain_call(
        kernel_a,
        (inputs, table, *map(jnp.asarray, ROWS + ROWS_TURNED), jnp.asarray(MODE_ROW)),
        (),
        [shape((SP * 32, 128), BF), row_matrix, row_matrix],
        [flat, cols],
        56,
        "field_modes",
        (place,),
    )
    arrived = exchange(message.reshape(SP, 32, 128))
    toeplitz, blocks = shape((4 * CP, 6 * GR), BF), shape((4 * CP, 4 * CP), BF)
    weights_out = [toeplitz] * 4 + [blocks] * 2
    rows, f_first, f_second, cot_rows, w_one, w_two, w_two_back, w_one_back, w_point, w_point_back = pl.pallas_call(
        kernel_rows,
        grid=(LEV,),
        in_specs=[
            pl.BlockSpec(memory_space=pltpu.SMEM),
            level_spec(C * RL, NC),
            level_spec(C * RL, NC),
            whole_spec(3, 3, C, C),
            whole_spec(3, 3, C, C),
            whole_spec(C, C),
            anywhere(),
        ],
        out_specs=[level_spec(RL, CP, NC), level_spec(2 * CO, NC), level_spec(2 * CO, NC), level_spec(RL, CP, NC)]
        + [whole_spec(*x.shape) for x in weights_out],
        out_shape=[grid_rows, strip, strip, grid_rows] + weights_out,
        scratch_shapes=[
            pltpu.VMEM((2, NC // 128, (C + 12) * RL, 128), F32),
            pltpu.VMEM((CP, 9 * CP), F32),
            pltpu.VMEM((4 * CP, 6 * GR), F32),
        ],
        compiler_params=params(56),
        name="row_layout",
    )(place, field.reshape(natural.shape), cotangent.reshape(natural.shape), kernel_one, kernel_two, point_weight, message)
    f_first, f_second = partners(f_first, f_second)

    square, lines = pltpu.VMEM((128, 128), F32), pltpu.VMEM((C * QN * 2, 128), F32)
    mixed, kept = plain_call(
        kernel_mix,
        (arrived, weight),
        (),
        [shape((SP, 32, 128), BF), shape((32, 128), F32)],
        [square, square, square, lines],
        8,
        "mode_mix",
    )
    gathered = exchange(mixed).reshape(SP * 32, 128)

    middle, slope, pre = pl.pallas_call(
        kernel_b,
        grid=(LEV,),
        in_specs=[
            pl.BlockSpec(memory_space=pltpu.SMEM),
            level_spec(RL, CP, NC),
            level_spec(2 * CO, NC),
            level_spec(2 * CO, NC),
            whole_spec(4 * CP, 6 * GR),
            whole_spec(4 * CP, 6 * GR),
            whole_spec(4 * CP, 4 * CP),
        ],
        out_specs=[
            level_spec(RL + 2, CP, NC),
            level_spec(RL + 2, CP, NC),
            level_spec(RL, CO, NC),
        ],
        out_shape=[
            shape((LEV, RL + 2, CP, NC), BF),
            shape((LEV, RL + 2, CP, NC), BF),
            shape((LEV, RL, CO, NC), F32),
        ],
        scratch_shapes=[pltpu.VMEM((RL + 4, GR, NC), BF), pltpu.VMEM((RL + 2, GR, NC), BF)],
        compiler_params=params(56),
        name="two_convolutions",
    )(place, rows, f_first, f_second, w_one, w_two, w_point)

    left, spec = pltpu.VMEM((LEV * RL * CO, 128), F32), pltpu.VMEM((LEV * RL * CO, NC), F32)
    values, slopes, s_first, s_second, message = pl.pallas_call(
        kernel_d,
        grid=(LEV,),
        in_specs=[
            pl.BlockSpec(memory_space=pltpu.SMEM),
            whole_spec(SP * 32, 128),
            whole_spec(SP * 32, 256),
            whole_spec(SP * 32, 256),
            whole_spec(128, NC),
            level_spec(RL, CO, NC),
            level_spec(RL, CP, NC),
            whole_spec(NC, 128),
            whole_spec(1, 256),
        ],
        out_specs=[level_spec(RL, CP, NC)] * 2 + [level_spec(2 * CO, NC)] * 2 + [whole_spec(SP * 32, 128)],
        out_shape=[grid_rows, grid_rows, strip, strip, shape((SP * 32, 128), BF)],
        scratch_shapes=[
            left,
            pltpu.VMEM((LEV * RL, CO, NC), F32),
            pltpu.VMEM((LEV, RL * CP, 128), F32),
            cols,
        ],
        compiler_params=params(56),
        name="output_and_slope",
    )(place, gathered, high, low, jnp.asarray(INVERSE), pre, cot_rows, table, jnp.asarray(SCALE))
    s_first, s_second = partners(s_first, s_second)

    grad_two = pl.pallas_call(
        kernel_e_zero,
        grid=(LEV,),
        in_specs=[level_spec(RL, CP, NC), level_spec(RL + 2, CP, NC), level_spec(RL, CP, NC)],
        scratch_shapes=[pltpu.VMEM((RL, GR, NC), BF)],
        out_specs=whole_spec(GR + CP, GR),
        out_shape=shape((GR + CP, GR), F32),
        compiler_params=params(56),
        name="weight_gradients_two",
    )(slopes, middle, rows)
    pre_slope, message = pl.pallas_call(
        kernel_e,
        grid=(LEV,),
        in_specs=[
            pl.BlockSpec(memory_space=pltpu.SMEM),
            level_spec(RL, CP, NC),
            level_spec(2 * CO, NC),
            level_spec(2 * CO, NC),
            level_spec(RL, CP, NC),
            level_spec(2 * CO, NC),
            level_spec(2 * CO, NC),
            level_spec(RL + 2, CP, NC),
            whole_spec(4 * CP, 6 * GR),
            whole_spec(SP, 32, 128),
            whole_spec(GR + CP, GR),
        ],
        out_specs=[level_spec(RL + 2, CP, NC), whole_spec(SP, 32, 128)],
        out_shape=[shape((LEV, RL + 2, CP, NC), BF), shape((SP, 32, 128), BF)],
        scratch_shapes=[
            pltpu.VMEM((RL + 4, GR, NC), BF),
            pltpu.VMEM((RL + 2, GR, NC), BF),
            pltpu.VMEM((GR, GR), F32),
            pltpu.VMEM((SP * SHARE, 128), F32),
            pltpu.VMEM((SP, 32, 128), F32),
        ],
        compiler_params=params(56),
        name="slope_and_weight_gradients",
    )(place, slopes, s_first, s_second, rows, f_first, f_second, slope, w_two_back, message.reshape(SP, 32, 128), grad_two)
    arrived = exchange(message)
    back = pl.pallas_call(
        kernel_e_two,
        grid=(LEV,),
        in_specs=[
            level_spec(RL + 2, CP, NC),
            level_spec(RL, CP, NC),
            whole_spec(4 * CP, 6 * GR),
            whole_spec(4 * CP, 4 * CP),
            anywhere(),
        ],
        out_specs=level_spec(C * RL, NC),
        out_shape=shape(natural.shape, F32),
        scratch_shapes=[pltpu.VMEM((RL + 2, GR, NC), BF), pltpu.VMEM((NC // 128, C * RL, 128), F32)],
        compiler_params=params(56),
        name="backward_convolution",
    )(pre_slope, slopes, w_one_back, w_point_back, message)
    (out,) = plain_call(
        kernel_out,
        (values,),
        (message,),
        [natural],
        [pltpu.VMEM((NC // 128, LEV * C * RL, 128), F32)],
        56,
        "output_layout",
    )
    (sums,) = plain_call(
        kernel_own, (arrived, kept), (), [shape((64, 128), F32)], [], 8, "own_sums"
    )
    others = [lax.ppermute(sums, "rep", [(i, i ^ k) for i in range(4)]) for k in (1, 2, 3)]
    (cofield,) = plain_call(
        kernel_mix_back, (sums, weight), (), [shape((32, 128), BF)], [square, lines], 8, "mode_mix_back"
    )
    (message,) = plain_call(
        kernel_send_back, (cofield, sums, *others), (), [shape((SP, 32, 128), BF)], [], 8, "gradient_modes"
    )
    gathered = exchange(message)
    (spec_grad,) = plain_call(
        kernel_spec_grad,
        (sums, *others),
        (),
        [shape(weight.shape, F32)],
        [pltpu.VMEM((4, 128, 128), F32)] * 2 + [lines],
        8,
        "spectral_gradient",
    )
    kernel_out_shape = shape((3, 3, C, C), F32)
    field_grad, point_total, one_total, two_total = pl.pallas_call(
        kernel_f,
        grid=(LEV,),
        in_specs=[
            whole_spec(SP, 32, 128),
            whole_spec(SP * 32, 256),
            whole_spec(SP * 32, 256),
            whole_spec(128, NC),
            level_spec(C * RL, NC),
        ],
        out_specs=[level_spec(C * RL, NC), whole_spec(C, C), whole_spec(3, 3, C, C), whole_spec(3, 3, C, C)],
        out_shape=[natural, shape((C, C), F32), kernel_out_shape, kernel_out_shape],
        scratch_shapes=[
            pltpu.VMEM((LEV, C * RL, 128), F32),
            pltpu.VMEM((SP, 32, 128), F32),
            pltpu.VMEM((SP * SHARE, 128), F32),
        ],
        compiler_params=params(56),
        name="field_gradient",
    )(gathered, high, low, jnp.asarray(BACK), back)
    spec_total = jnp.transpose(spec_grad.reshape(C, QN, 2, C), (2, 0, 3, 1))
    return (
        out.reshape(field.shape),
        field_grad.reshape(field.shape),
        spec_total,
        point_total,
        one_total,
        two_total,
    )


def solution(mesh):
    specs = (
        P("rep", None, None, "sp", None),
        P("rep", None, None, "sp", None),
        P(None, None, None, "sp"),
        P(),
        P(),
        P(),
    )
    return jax.shard_map(local, mesh=mesh, in_specs=specs, out_specs=specs, check_vma=False)
```

```python
import math

import jax
import jax.numpy as jnp
import numpy as np
import ml_dtypes
from jax import lax
from jax.experimental import pallas as pl
from jax.experimental.pallas import tpu as pltpu
from jax.sharding import PartitionSpec as P

M = 12
C = 36
CP = 48
CO = 40
LEV = 2
RL = 8
NC = 1024
NR = 256
SP = 32
QN = 9
GR = 3 * CP
SHARE = 14

ROOT_HALF = 0.7071067811865476
INV_ROOT_TAU = 0.3989422804014327
BF = jnp.bfloat16
F32 = jnp.float32


def split_np(values):
    high = values.astype(np.float32).astype(ml_dtypes.bfloat16)
    low = (values - high.astype(np.float64)).astype(np.float32).astype(ml_dtypes.bfloat16)
    return high, low


def make_tables():
    n = np.arange(NC)[:, None]
    k = np.arange(M)[None, :]
    t = 2.0 * np.pi * ((n * k) % NC) / NC
    forward = np.concatenate([np.cos(t), -np.sin(t)], axis=1)
    doubled = np.where(np.arange(M) == 0, 1.0, 2.0)
    doubled = np.concatenate([doubled, doubled]) / (NR * NC)
    table = np.zeros((NC, 128), np.float32)
    table[:, :24] = forward
    table = table.astype(ml_dtypes.bfloat16)

    def inverse(matrix):
        high, low = split_np(matrix.T)
        out = np.zeros((128, NC), ml_dtypes.bfloat16)
        out[0:24], out[24:48], out[48:72] = high, low, high
        return out

    rows, turned = np.zeros((SP, 32, 256)), np.zeros((SP, 32, 256))
    freq = np.where(np.arange(24) < M, np.arange(24), NR - 24 + np.arange(24))
    mode_row = np.zeros((SP, 32, 32))
    for owner in range(SP):
        for q in range(QN):
            mode = owner * QN + q
            j, kk = mode // M, mode % M
            for r in range(RL):
                p = 2.0 * np.pi * ((freq[j] * r) % NR) / NR
                for x, line, sign in ((rows, q, 1.0), (turned, QN + q, -1.0)):
                    x[owner, line, r * 24 + kk] = sign * np.cos(p)
                    x[owner, line, r * 24 + 12 + kk] = sign * np.sin(p)
                for x, line in ((rows, QN + q), (turned, q)):
                    x[owner, line, r * 24 + kk] = -np.sin(p)
                    x[owner, line, r * 24 + 12 + kk] = np.cos(p)
            mode_row[owner, q, j] = mode_row[owner, QN + q, j] = 1.0
    rows, turned = split_np(rows.reshape(SP * 32, 256)), split_np(turned.reshape(SP * 32, 256))
    scale = np.zeros((1, 256), np.float32)
    scale[0, :192] = np.tile(doubled, RL)
    return (
        table,
        inverse(forward * doubled[None, :]),
        inverse(forward),
        rows,
        turned,
        mode_row.reshape(SP * 32, 32).astype(ml_dtypes.bfloat16),
        scale,
    )


TABLE, INVERSE, BACK, ROWS, ROWS_TURNED, MODE_ROW, SCALE = make_tables()


def dot(a, b):
    return lax.dot_general(a, b, (((1,), (0,)), ((), ())), preferred_element_type=F32)


def dot_nt(a, b):
    return lax.dot_general(a, b, (((1,), (1,)), ((), ())), preferred_element_type=F32)


def dot_tn(a, b):
    return lax.dot_general(a, b, (((0,), (0,)), ((), ())), preferred_element_type=F32)


def split(values):
    high = values.astype(BF)
    return high, (values - high.astype(F32)).astype(BF)


def gelu_parts(v):
    cdf = 0.5 * (1.0 + lax.erf(v * ROOT_HALF))
    return v * cdf, cdf + v * jnp.exp(-0.5 * v * v) * INV_ROOT_TAU


def store_taps(taps, i, x):
    col = lax.broadcasted_iota(jnp.int32, (CP, NC), 1)
    taps[i, 0:CP] = jnp.where(col == 0, 0.0, pltpu.roll(x, 1, 1)).astype(BF)
    taps[i, CP : 2 * CP] = x.astype(BF)
    taps[i, 2 * CP : 3 * CP] = jnp.where(col == NC - 1, 0.0, pltpu.roll(x, NC - 1, 1)).astype(BF)


def row_transform(cols, matrix):
    both = dot_nt(matrix, jnp.concatenate(split(cols), axis=0))
    return (both[:, 0:128] + both[:, 128:256]).astype(BF)


def row_expand(modes, matrix):
    return dot_tn(modes, matrix)


def strip_pair(even, top, bottom):
    top, bottom = [jnp.concatenate([x[0:CO].astype(F32) for x in rows], axis=0) for rows in (top, bottom)]
    return jnp.where(even, bottom, top).astype(BF), jnp.where(even, top, bottom).astype(BF)


def halo_rows(even, first, second):
    first, second = first[0].astype(F32), second[0].astype(F32)
    above, below = jnp.where(even, second, first), jnp.where(even, first, second)
    rest = jnp.zeros((CP - CO, NC), F32)
    return [jnp.concatenate([x[i * CO : (i + 1) * CO], rest], axis=0) for x in (above, below) for i in range(2)]


def place_rows(rows, left):
    high, low = split(rows)
    high, low = high.astype(F32), low.astype(F32)
    left[...] = jnp.zeros_like(left)
    for lev in range(LEV):
        for r in range(RL):
            at = (lev * RL + r) * CO
            h = high[lev * 64 : lev * 64 + CO, r * 24 : r * 24 + 24]
            w = low[lev * 64 : lev * 64 + CO, r * 24 : r * 24 + 24]
            left[at : at + CO, 0:72] = jnp.concatenate([h, h, w], axis=1)


def kernel_a(place, field, table, high, low, turned_high, turned_low, mode_row, message, matrix, flat, cols):
    j = lax.broadcasted_iota(jnp.int32, (32, 128), 0)
    turn = ((j + jnp.where(j < M, 0, NR - 24)) * place[0]) % SP
    angle = turn.astype(F32) * (2.0 * math.pi / SP)
    t_high, t_low = split(jnp.concatenate([jnp.cos(angle), jnp.sin(angle)], axis=1))
    phase = dot(mode_row[...], t_high) + dot(mode_row[...], t_low)
    cosine, sine = phase[:, 0:128], phase[:, 128:256]
    cosine, sine = jnp.concatenate([cosine, cosine], axis=1), jnp.concatenate([sine, sine], axis=1)
    first = high[...].astype(F32) + low[...].astype(F32)
    turned = turned_high[...].astype(F32) + turned_low[...].astype(F32)
    turned = (first * cosine + turned * sine).astype(BF)
    matrix[...] = turned
    flat[...] = dot(field[...], table[...])
    cols[...] = jnp.zeros_like(cols)
    for lev in range(LEV):
        for r in range(RL):
            part = flat[pl.ds(lev * C * RL + r, C, stride=RL), :]
            cols[lev * 64 : lev * 64 + C, r * 24 : r * 24 + 24] = part[:, 0:24]
    message[...] = row_transform(cols[...], turned)


def prepare(one, two, point, w_one, w_two, w_two_back, w_one_back, w_point, w_point_back, base, wide):
    def spread(target, rows):
        wide[...] = jnp.zeros_like(wide)
        for t in range(4):
            wide[t * CP : (t + 1) * CP, t * rows : t * rows + base.shape[1]] = base[...]
        target[...] = wide[:, 0 : target.shape[1]].astype(BF)

    for kernel, forward, backward in ((one, w_one, w_one_back), (two, w_two, w_two_back)):
        base[...] = jnp.zeros_like(base)
        for a in range(3):
            for b in range(3):
                at = (a * 3 + b) * CP
                base[0:C, at : at + C] = jnp.transpose(kernel[a, b].astype(F32))
        spread(forward, GR)
        for a in range(3):
            for b in range(3):
                at = ((2 - a) * 3 + 2 - b) * CP
                base[0:C, at : at + C] = kernel[a, b].astype(F32)
        spread(backward, GR)
    for target, matrix in ((w_point, jnp.transpose(point[...].astype(F32))), (w_point_back, point[...].astype(F32))):
        wide[...] = jnp.zeros_like(wide)
        for t in range(4):
            wide[t * CP : t * CP + C, t * CP : t * CP + C] = matrix
        target[...] = wide[:, 0 : 4 * CP].astype(BF)


def kernel_rows(place, field, cot, one, two, point, after, rows, strip_one, strip_two, cot_rows, w_one, w_two, w_two_back, w_one_back, w_point, w_point_back, wide, base, spread):
    even = place[0] % 2 == 0

    @pl.when(pl.program_id(0) == 0)
    def _():
        prepare(one, two, point, w_one, w_two, w_two_back, w_one_back, w_point, w_point_back, base, spread)

    for k, (source, target) in enumerate(((field, rows), (cot, cot_rows))):
        for n in range(0, NC, 128):
            wide[k, n // 128, 0 : C * RL, :] = source[0, :, n : n + 128].astype(F32)
            wide[k, n // 128, C * RL :, :] = jnp.zeros((12 * RL, 128), F32)
        for n in range(0, NC, 128):
            found = [wide[k, n // 128, pl.ds(r, CP, stride=RL), :] for r in range(RL)]
            for r in range(RL):
                target[0, r, :, n : n + 128] = found[r].astype(BF)
            if k == 0:
                x, y = strip_pair(even, found[0:2], found[RL - 2 :])
                strip_one[0, :, n : n + 128], strip_two[0, :, n : n + 128] = x, y


def window(ref, i, count):
    return ref[i : i + count].reshape(count * GR, NC)


def kernel_b(place, rows, first, second, w_one, w_two, w_point, middle, slope, pre, taps, mid_taps):
    index = place[0]
    halo = halo_rows(index % 2 == 0, first, second)
    for i, x in enumerate(halo[0:2] + [rows[0, r].astype(F32) for r in range(RL)] + halo[2:4]):
        store_taps(taps, i, x)
    rest = jnp.zeros((CP - CO, NC), F32)
    for start, count in ((0, 4), (4, 3), (7, 3)):
        d = dot(w_one[0 : CP * count, 0 : GR * (count + 2)], window(taps, start, count + 2))
        for t in range(count):
            i = start + t
            value, gradient = gelu_parts(d[t * CP : t * CP + CO])
            if i in (0, RL + 1):
                keep = jnp.where(index == (0 if i == 0 else SP - 1), 0.0, 1.0).astype(F32)
                value, gradient = value * keep, gradient * keep
            slope[0, i] = jnp.concatenate([gradient, rest], axis=0).astype(BF)
            value = jnp.concatenate([value, rest], axis=0)
            middle[0, i] = value.astype(BF)
            store_taps(mid_taps, i, value)
    for r in (0, 4):
        d = dot(w_two[...], window(mid_taps, r, 6))
        d = d + dot(w_point[...], rows[0, r : r + 4].reshape(4 * CP, NC))
        for t in range(4):
            pre[0, r + t] = d[t * CP : t * CP + CO]


def own_modes(received):
    return jnp.sum(received.astype(F32), axis=0)


def by_channel(own, real, imag):
    rest = jnp.zeros((96, 128), F32)
    real[...] = jnp.transpose(jnp.concatenate([own, rest], axis=0))
    imag[...] = jnp.transpose(jnp.concatenate([pltpu.roll(own, 32 - QN, 0), rest], axis=0))


def weight_rows(weight, lines):
    lines[...] = jnp.zeros_like(lines)
    lines[:, 0:C] = weight[...]


def mode_line(lines, q, part):
    return lines[pl.ds(2 * q + part, C, stride=2 * QN), :]


def kernel_mix(received, weight, message, kept, real, imag, mixed, lines):
    own = own_modes(received[...])
    kept[...] = own
    by_channel(own, real, imag)
    weight_rows(weight, lines)
    mixed[...] = jnp.zeros_like(mixed)
    for q in range(QN):
        w_re, w_im = mode_line(lines, q, 0), mode_line(lines, q, 1)
        re, im = [], []
        for lev in range(LEV):
            s_re = real[lev * 64 : lev * 64 + C, q : q + 1]
            s_im = imag[lev * 64 : lev * 64 + C, q : q + 1]
            re.append(jnp.sum(w_re * s_re - w_im * s_im, axis=0, keepdims=True))
            im.append(jnp.sum(w_im * s_re + w_re * s_im, axis=0, keepdims=True))
        mixed[q : q + 1] = re[0] + pltpu.roll(re[1], 64, 1)
        mixed[QN + q : QN + q + 1] = im[0] + pltpu.roll(im[1], 64, 1)
    message[...] = jnp.broadcast_to(mixed[0:32].astype(BF)[None], (SP, 32, 128))


def mix_back(own, lines, mixed):
    other = pltpu.roll(own, 64, 1)
    mixed[...] = jnp.zeros_like(mixed)
    for q in range(QN):
        w_re, w_im = mode_line(lines, q, 0), mode_line(lines, q, 1)
        for lev, z in enumerate((own, other)):
            z_re, z_im = z[q : q + 1], z[QN + q : QN + q + 1]
            at = lev * 64
            mixed[at : at + C, q : q + 1] = jnp.sum(w_re * z_re + w_im * z_im, axis=1, keepdims=True)
            mixed[at : at + C, QN + q : QN + q + 1] = jnp.sum(w_re * z_im - w_im * z_re, axis=1, keepdims=True)
    return jnp.transpose(mixed[...])[0:32].astype(BF)


def kernel_spec_grad(p0, p1, p2, p3, grad, s_re, s_im, lines):
    pairs = (p0, p1, p2, p3)
    co = []
    for i, pair in enumerate(pairs):
        by_channel(pair[0:32], s_re.at[i], s_im.at[i])
        co.append((pair[32:64], pltpu.roll(pair[32:64], 64, 1)))
    for q in range(QN):
        res, ims = [], []
        for i in range(4):
            re, im = jnp.zeros((C, 128), F32), jnp.zeros((C, 128), F32)
            for lev in range(LEV):
                at = lev * 64
                a, b = s_re[i, at : at + C, q : q + 1], s_im[i, at : at + C, q : q + 1]
                x, y = co[i][lev][q : q + 1], co[i][lev][QN + q : QN + q + 1]
                re = re + (a * x + b * y)
                im = im + (a * y - b * x)
            res.append(re)
            ims.append(im)
        lines[pl.ds(2 * q, C, stride=2 * QN), :] = (res[0] + res[1]) + (res[2] + res[3])
        lines[pl.ds(2 * q + 1, C, stride=2 * QN), :] = (ims[0] + ims[1]) + (ims[2] + ims[3])
    grad[...] = lines[:, 0:C]


def kernel_d(place, received, matrix, inverse, pre, cot, table, scale, values, slopes, strip_one, strip_two, message, left, spec, kept, cols):
    lev = pl.program_id(0)

    @pl.when(lev == 0)
    def _():
        place_rows(row_expand(received[...], matrix[...]), left)
        spec[...] = dot(left[...].astype(BF), inverse[...]).reshape(LEV * RL, CO, NC)
        cols[...] = jnp.zeros_like(cols)

    rest = jnp.zeros((CP - CO, NC), F32)
    edges = {}
    for r in range(RL):
        value, gradient = gelu_parts(pre[0, r] + spec[lev * RL + r])
        values[0, r] = jnp.concatenate([value, rest], axis=0).astype(BF)
        s = jnp.concatenate([gradient, rest], axis=0) * cot[0, r].astype(F32)
        slopes[0, r] = s.astype(BF)
        edges[r] = s
    x, y = strip_pair(place[0] % 2 == 0, [edges[0], edges[1]], [edges[RL - 2], edges[RL - 1]])
    strip_one[0], strip_two[0] = x, y
    kept[lev] = dot(slopes[0].reshape(RL * CP, NC), table[...])

    @pl.when(lev == LEV - 1)
    def _():
        for at in range(LEV):
            for r in range(RL):
                cols[at * 64 : at * 64 + CO, r * 24 : r * 24 + 24] = kept[at, r * CP : r * CP + CO, 0:24]
        message[...] = row_transform(cols[...] * scale[...], matrix[...])


def kernel_out(values, after, out, wide):
    for lev in range(LEV):
        for r in range(RL):
            for n in range(0, NC, 128):
                x = values[lev, r, :, n : n + 128].astype(F32)
                wide[n // 128, pl.ds(lev * C * RL + r, C, stride=RL), :] = x[0:C]
    for n in range(0, NC, 128):
        for lev in range(LEV):
            out[lev, :, n : n + 128] = wide[n // 128, lev * C * RL : (lev + 1) * C * RL].astype(BF)


def kernel_own(received, kept, sums):
    sums[0:32] = kept[...]
    sums[32:64] = own_modes(received[...])


def kernel_mix_back(sums, weight, cofield, mixed, lines):
    weight_rows(weight, lines)
    cofield[...] = mix_back(sums[32:64], lines, mixed)


def kernel_send_back(cofield, p0, p1, p2, p3, message):
    total = (p0[32:64] + p1[32:64]) + (p2[32:64] + p3[32:64])
    row = lax.broadcasted_iota(jnp.int32, (32, 128), 0)
    total = jnp.where(row < 2 * QN, cofield[...].astype(F32), total).astype(BF)
    message[...] = jnp.broadcast_to(total[None], (SP, 32, 128))


def kernel_e_zero(slopes, middle, rows, slope, w_two, grad_two, inner, taps):
    left, right = [], []
    for r in range(RL):
        store_taps(taps, r, slopes[0, r].astype(F32))
        left.append(jnp.concatenate([middle[0, r], middle[0, r + 1], middle[0, r + 2], rows[0, r]], axis=0))
        right.append(taps[r])
    for start in (0, 3):
        d = dot(w_two[0 : 3 * CP, 0 : 5 * GR], window(taps, start, 5))
        for t in range(3):
            value = d[t * CP : (t + 1) * CP] * slope[0, start + t + 2].astype(F32)
            inner[0, start + t] = value.astype(BF)
    part = dot_nt(jnp.concatenate(left, axis=1), jnp.concatenate(right, axis=1))

    @pl.when(pl.program_id(0) == 0)
    def _():
        grad_two[...] = part

    @pl.when(pl.program_id(0) > 0)
    def _():
        grad_two[...] += part


def kernel_e(place, slopes, first, second, rows, f_first, f_second, slope, w_two, modes, grad_two, inner, outer, message, taps, pre_taps, grad_one, sums, packed):
    index = place[0]
    lev = pl.program_id(0)
    even = index % 2 == 0
    halo = halo_rows(even, first, second)
    near = [slopes[0, r].astype(F32) for r in (0, 1, RL - 2, RL - 1)]
    for i, x in enumerate(halo[0:2] + near + halo[2:4]):
        store_taps(taps, i, x)
    for i in range(6):
        store_taps(pre_taps, i + 1, inner[0, i].astype(F32))
    for k in range(2):
        d = dot(w_two[0 : 2 * CP, 0 : 4 * GR], window(taps, 4 * k, 4))
        for t in range(2):
            i = RL * k + t
            value = d[t * CP : (t + 1) * CP] * slope[0, i].astype(F32)
            if i in (0, RL + 1):
                value = value * jnp.where(index == (0 if i == 0 else SP - 1), 0.0, 1.0).astype(F32)
            else:
                store_taps(pre_taps, i - 1, value)
            outer[0, 2 * k + t] = value.astype(BF)
    halo = halo_rows(even, f_first, f_second)
    field = [halo[1].astype(BF)] + [rows[0, r] for r in range(RL)] + [halo[2].astype(BF)]
    left = jnp.concatenate([jnp.concatenate(field[r : r + 3], axis=0) for r in range(RL)], axis=1)
    right = jnp.concatenate([pre_taps[r] for r in range(RL)], axis=1)
    part_one = dot_nt(left, right)

    @pl.when(lev == 0)
    def _():
        grad_one[...] = part_one

    @pl.when(lev == LEV - 1)
    def _():
        sums[...] = jnp.zeros_like(sums)
        two, one = grad_two[...], grad_one[...] + part_one
        for b in range(3):
            at = b * CP
            sums[b * GR : (b + 1) * GR, 0:C] = two[0:GR, at : at + C]
            sums[b * GR : (b + 1) * GR, C : 2 * C] = one[:, at : at + C]
        sums[0:CP, 2 * C : 3 * C] = two[GR : GR + CP, CP : CP + C]
        packed[...] = modes[...].astype(F32)
        for owner in range(SP):
            packed[owner, 2 * QN : 32] = sums[owner * SHARE : (owner + 1) * SHARE]
        message[...] = packed[...].astype(BF)


def kernel_e_two(inner, outer, slopes, w_one, w_point, after, back, taps, wide):
    lines = [outer[0, 0], outer[0, 1]] + [inner[0, i] for i in range(6)] + [outer[0, 2], outer[0, 3]]
    for i, x in enumerate(lines):
        store_taps(taps, i, x.astype(F32))
    for r in (0, 4):
        d = dot(w_one[...], window(taps, r, 6))
        d = d + dot(w_point[...], slopes[0, r : r + 4].reshape(4 * CP, NC))
        for t in range(4):
            for n in range(0, NC, 128):
                wide[n // 128, pl.ds(r + t, C, stride=RL), :] = d[t * CP : t * CP + C, n : n + 128]
    for n in range(0, NC, 128):
        back[0, :, n : n + 128] = wide[n // 128]


def kernel_f(received, matrix, inverse, back, out, point, one, two, left, packed, sums):
    lev = pl.program_id(0)

    @pl.when(lev == 0)
    def _():
        modes = received[...].reshape(SP * 32, 128)
        r_high, r_low = split(row_expand(modes, matrix[...]))
        r_high, r_low = r_high.astype(F32), r_low.astype(F32)
        rest = jnp.zeros((C, 56), F32)
        for at in range(LEV):
            for r in range(RL):
                h = r_high[at * 64 : at * 64 + C, r * 24 : r * 24 + 24]
                w = r_low[at * 64 : at * 64 + C, r * 24 : r * 24 + 24]
                left[at, pl.ds(r, C, stride=RL), :] = jnp.concatenate([h, h, w, rest], axis=1)
        packed[...] = received[...].astype(F32)
        for owner in range(SP):
            sums[owner * SHARE : (owner + 1) * SHARE] = packed[owner, 2 * QN : 32]
        scaled = sums[...] * (1.0 / math.sqrt(NR * NC * LEV * 4))
        for a in range(3):
            for b in range(3):
                at = (2 - b) * GR + a * CP
                two[a, b] = scaled[at : at + C, 0:C]
                one[a, b] = scaled[at : at + C, C : 2 * C]
        point[...] = scaled[0:C, 2 * C : 3 * C]

    out[0] = (back[0] + dot(left[lev].astype(BF), inverse[...])).astype(BF)


def shape(dims, kind):
    return jax.ShapeDtypeStruct(dims, kind)


def params(mib):
    return pltpu.CompilerParams(vmem_limit_bytes=mib * 1024 * 1024)


def estimate(us):
    if us is None:
        return None
    return pl.CostEstimate(flops=us * 10**9, bytes_accessed=us * 3 * 10**6, transcendentals=0)


def level_spec(*dims):
    return pl.BlockSpec((1,) + dims, lambda lev: (lev,) + (0,) * len(dims))


def whole_spec(*dims):
    return pl.BlockSpec(dims, lambda lev: (0,) * len(dims))


def partners(first, second):
    pairs = [(i, i ^ 1) for i in range(SP)]
    others = [(i, i + 1) for i in range(1, SP - 1, 2)] + [(i + 1, i) for i in range(1, SP - 1, 2)]
    return lax.ppermute(first, "sp", pairs), lax.ppermute(second, "sp", others)


def exchange(x):
    return lax.all_to_all(x, "sp", 0, 0, tiled=True)


def anywhere():
    return pl.BlockSpec(memory_space=pl.ANY)


def plain_call(kernel, operands, after, outs, scratch, mib, name, place=(), cost=None):
    vmem = pl.BlockSpec(memory_space=pltpu.VMEM)
    return pl.pallas_call(
        kernel,
        in_specs=[pl.BlockSpec(memory_space=pltpu.SMEM)] * len(place) + [vmem] * len(operands) + [anywhere()] * len(after),
        out_specs=[vmem] * len(outs),
        out_shape=outs,
        scratch_shapes=scratch,
        compiler_params=params(mib),
        cost_estimate=estimate(cost),
        name=name,
    )(*place, *operands, *after)


def local(field, cotangent, spec_weight, point_weight, kernel_one, kernel_two):
    place = lax.axis_index("sp").astype(jnp.int32).reshape(1)
    inputs = field.reshape(LEV * C * RL, NC)
    table = jnp.asarray(TABLE)
    weight = jnp.transpose(spec_weight, (1, 3, 0, 2)).reshape(C * QN * 2, C)
    strip = shape((LEV, 2 * CO, NC), BF)
    grid_rows = shape((LEV, RL, CP, NC), BF)
    natural = shape((LEV, C * RL, NC), BF)
    flat, cols = pltpu.VMEM((LEV * C * RL, 128), F32), pltpu.VMEM((128, 256), F32)
    row_matrix = shape((SP * 32, 256), BF)
    message, matrix = plain_call(
        kernel_a,
        (inputs, table, *map(jnp.asarray, ROWS + ROWS_TURNED), jnp.asarray(MODE_ROW)),
        (),
        [shape((SP * 32, 128), BF), row_matrix],
        [flat, cols],
        56,
        "field_modes",
        (place,),
    )
    arrived = exchange(message.reshape(SP, 32, 128))
    toeplitz, blocks = shape((4 * CP, 6 * GR), BF), shape((4 * CP, 4 * CP), BF)
    weights_out = [toeplitz] * 4 + [blocks] * 2
    rows, f_first, f_second, cot_rows, w_one, w_two, w_two_back, w_one_back, w_point, w_point_back = pl.pallas_call(
        kernel_rows,
        grid=(LEV,),
        in_specs=[
            pl.BlockSpec(memory_space=pltpu.SMEM),
            level_spec(C * RL, NC),
            level_spec(C * RL, NC),
            whole_spec(3, 3, C, C),
            whole_spec(3, 3, C, C),
            whole_spec(C, C),
            anywhere(),
        ],
        out_specs=[level_spec(RL, CP, NC), level_spec(2 * CO, NC), level_spec(2 * CO, NC), level_spec(RL, CP, NC)]
        + [whole_spec(*x.shape) for x in weights_out],
        out_shape=[grid_rows, strip, strip, grid_rows] + weights_out,
        scratch_shapes=[
            pltpu.VMEM((2, NC // 128, (C + 12) * RL, 128), F32),
            pltpu.VMEM((CP, 9 * CP), F32),
            pltpu.VMEM((4 * CP, 6 * GR), F32),
        ],
        compiler_params=params(56),
        name="row_layout",
    )(place, field.reshape(natural.shape), cotangent.reshape(natural.shape), kernel_one, kernel_two, point_weight, message)
    f_first, f_second = partners(f_first, f_second)

    square, lines = pltpu.VMEM((128, 128), F32), pltpu.VMEM((C * QN * 2, 128), F32)
    mixed, kept = plain_call(
        kernel_mix,
        (arrived, weight),
        (),
        [shape((SP, 32, 128), BF), shape((32, 128), F32)],
        [square, square, square, lines],
        8,
        "mode_mix",
    )
    gathered = exchange(mixed).reshape(SP * 32, 128)

    middle, slope, pre = pl.pallas_call(
        kernel_b,
        grid=(LEV,),
        in_specs=[
            pl.BlockSpec(memory_space=pltpu.SMEM),
            level_spec(RL, CP, NC),
            level_spec(2 * CO, NC),
            level_spec(2 * CO, NC),
            whole_spec(4 * CP, 6 * GR),
            whole_spec(4 * CP, 6 * GR),
            whole_spec(4 * CP, 4 * CP),
        ],
        out_specs=[
            level_spec(RL + 2, CP, NC),
            level_spec(RL + 2, CP, NC),
            level_spec(RL, CO, NC),
        ],
        out_shape=[
            shape((LEV, RL + 2, CP, NC), BF),
            shape((LEV, RL + 2, CP, NC), BF),
            shape((LEV, RL, CO, NC), F32),
        ],
        scratch_shapes=[pltpu.VMEM((RL + 4, GR, NC), BF), pltpu.VMEM((RL + 2, GR, NC), BF)],
        compiler_params=params(56),
        name="two_convolutions",
    )(place, rows, f_first, f_second, w_one, w_two, w_point)

    left, spec = pltpu.VMEM((LEV * RL * CO, 128), F32), pltpu.VMEM((LEV * RL * CO, NC), F32)
    values, slopes, s_first, s_second, message = pl.pallas_call(
        kernel_d,
        grid=(LEV,),
        in_specs=[
            pl.BlockSpec(memory_space=pltpu.SMEM),
            whole_spec(SP * 32, 128),
            whole_spec(SP * 32, 256),
            whole_spec(128, NC),
            level_spec(RL, CO, NC),
            level_spec(RL, CP, NC),
            whole_spec(NC, 128),
            whole_spec(1, 256),
        ],
        out_specs=[level_spec(RL, CP, NC)] * 2 + [level_spec(2 * CO, NC)] * 2 + [whole_spec(SP * 32, 128)],
        out_shape=[grid_rows, grid_rows, strip, strip, shape((SP * 32, 128), BF)],
        scratch_shapes=[
            left,
            pltpu.VMEM((LEV * RL, CO, NC), F32),
            pltpu.VMEM((LEV, RL * CP, 128), F32),
            cols,
        ],
        compiler_params=params(56),
        name="output_and_slope",
    )(place, gathered, matrix, jnp.asarray(INVERSE), pre, cot_rows, table, jnp.asarray(SCALE))
    s_first, s_second = partners(s_first, s_second)

    grad_two, inner = pl.pallas_call(
        kernel_e_zero,
        grid=(LEV,),
        in_specs=[
            level_spec(RL, CP, NC),
            level_spec(RL + 2, CP, NC),
            level_spec(RL, CP, NC),
            level_spec(RL + 2, CP, NC),
            whole_spec(4 * CP, 6 * GR),
        ],
        out_specs=[whole_spec(GR + CP, GR), level_spec(6, CP, NC)],
        out_shape=[shape((GR + CP, GR), F32), shape((LEV, 6, CP, NC), BF)],
        scratch_shapes=[pltpu.VMEM((RL, GR, NC), BF)],
        compiler_params=params(56),
        name="inner_slopes_and_gradients",
    )(slopes, middle, rows, slope, w_two_back)
    outer, message = pl.pallas_call(
        kernel_e,
        grid=(LEV,),
        in_specs=[
            pl.BlockSpec(memory_space=pltpu.SMEM),
            level_spec(RL, CP, NC),
            level_spec(2 * CO, NC),
            level_spec(2 * CO, NC),
            level_spec(RL, CP, NC),
            level_spec(2 * CO, NC),
            level_spec(2 * CO, NC),
            level_spec(RL + 2, CP, NC),
            whole_spec(4 * CP, 6 * GR),
            whole_spec(SP, 32, 128),
            whole_spec(GR + CP, GR),
            level_spec(6, CP, NC),
        ],
        out_specs=[level_spec(4, CP, NC), whole_spec(SP, 32, 128)],
        out_shape=[shape((LEV, 4, CP, NC), BF), shape((SP, 32, 128), BF)],
        scratch_shapes=[
            pltpu.VMEM((RL, GR, NC), BF),
            pltpu.VMEM((RL, GR, NC), BF),
            pltpu.VMEM((GR, GR), F32),
            pltpu.VMEM((SP * SHARE, 128), F32),
            pltpu.VMEM((SP, 32, 128), F32),
        ],
        compiler_params=params(56),
        name="outer_slopes_and_gradients",
    )(place, slopes, s_first, s_second, rows, f_first, f_second, slope, w_two_back, message.reshape(SP, 32, 128), grad_two, inner)
    arrived = exchange(message)
    back = pl.pallas_call(
        kernel_e_two,
        grid=(LEV,),
        in_specs=[
            level_spec(6, CP, NC),
            level_spec(4, CP, NC),
            level_spec(RL, CP, NC),
            whole_spec(4 * CP, 6 * GR),
            whole_spec(4 * CP, 4 * CP),
            anywhere(),
        ],
        out_specs=level_spec(C * RL, NC),
        out_shape=shape(natural.shape, F32),
        scratch_shapes=[pltpu.VMEM((RL + 2, GR, NC), BF), pltpu.VMEM((NC // 128, C * RL, 128), F32)],
        compiler_params=params(56),
        name="backward_convolution",
    )(inner, outer, slopes, w_one_back, w_point_back, message)
    (out,) = plain_call(
        kernel_out,
        (values,),
        (message,),
        [natural],
        [pltpu.VMEM((NC // 128, LEV * C * RL, 128), F32)],
        56,
        "output_layout",
    )
    (sums,) = plain_call(
        kernel_own, (arrived, kept), (), [shape((64, 128), F32)], [], 8, "own_sums"
    )
    others = [lax.ppermute(sums, "rep", [(i, i ^ k) for i in range(4)]) for k in (1, 2, 3)]
    (cofield,) = plain_call(
        kernel_mix_back, (sums, weight), (), [shape((32, 128), BF)], [square, lines], 8, "mode_mix_back"
    )
    (message,) = plain_call(
        kernel_send_back, (cofield, sums, *others), (), [shape((SP, 32, 128), BF)], [], 8, "gradient_modes"
    )
    gathered = exchange(message)
    (spec_grad,) = plain_call(
        kernel_spec_grad,
        (sums, *others),
        (),
        [shape(weight.shape, F32)],
        [pltpu.VMEM((4, 128, 128), F32)] * 2 + [lines],
        8,
        "spectral_gradient",
    )
    kernel_out_shape = shape((3, 3, C, C), F32)
    field_grad, point_total, one_total, two_total = pl.pallas_call(
        kernel_f,
        grid=(LEV,),
        in_specs=[
            whole_spec(SP, 32, 128),
            whole_spec(SP * 32, 256),
            whole_spec(128, NC),
            level_spec(C * RL, NC),
        ],
        out_specs=[level_spec(C * RL, NC), whole_spec(C, C), whole_spec(3, 3, C, C), whole_spec(3, 3, C, C)],
        out_shape=[natural, shape((C, C), F32), kernel_out_shape, kernel_out_shape],
        scratch_shapes=[
            pltpu.VMEM((LEV, C * RL, 128), F32),
            pltpu.VMEM((SP, 32, 128), F32),
            pltpu.VMEM((SP * SHARE, 128), F32),
        ],
        compiler_params=params(56),
        name="field_gradient",
    )(gathered, matrix, jnp.asarray(BACK), back)
    spec_total = jnp.transpose(spec_grad.reshape(C, QN, 2, C), (2, 0, 3, 1))
    return (
        out.reshape(field.shape),
        field_grad.reshape(field.shape),
        spec_total,
        point_total,
        one_total,
        two_total,
    )


def solution(mesh):
    specs = (
        P("rep", None, None, "sp", None),
        P("rep", None, None, "sp", None),
        P(None, None, None, "sp"),
        P(),
        P(),
        P(),
    )
    return jax.shard_map(local, mesh=mesh, in_specs=specs, out_specs=specs, check_vma=False)
```

```python
import math

import jax
import jax.numpy as jnp
import numpy as np
import ml_dtypes
from jax import lax
from jax.experimental import pallas as pl
from jax.experimental.pallas import tpu as pltpu
from jax.sharding import PartitionSpec as P

M = 12
C = 36
CP = 48
CO = 40
LEV = 2
RL = 8
NC = 1024
NR = 256
SP = 32
QN = 9
GR = 3 * CP
SHARE = 14

ROOT_HALF = 0.7071067811865476
INV_ROOT_TAU = 0.3989422804014327
BF = jnp.bfloat16
F32 = jnp.float32


def split_np(values):
    high = values.astype(np.float32).astype(ml_dtypes.bfloat16)
    low = (values - high.astype(np.float64)).astype(np.float32).astype(ml_dtypes.bfloat16)
    return high, low


def make_tables():
    n = np.arange(NC)[:, None]
    k = np.arange(M)[None, :]
    t = 2.0 * np.pi * ((n * k) % NC) / NC
    forward = np.concatenate([np.cos(t), -np.sin(t)], axis=1)
    doubled = np.where(np.arange(M) == 0, 1.0, 2.0)
    doubled = np.concatenate([doubled, doubled]) / (NR * NC)
    table = np.zeros((NC, 128), np.float32)
    table[:, :24] = forward
    table = table.astype(ml_dtypes.bfloat16)

    def inverse(matrix):
        high, low = split_np(matrix.T)
        out = np.zeros((128, NC), ml_dtypes.bfloat16)
        out[0:24], out[24:48], out[48:72] = high, low, high
        return out

    rows, turned = np.zeros((SP, 32, 256)), np.zeros((SP, 32, 256))
    freq = np.where(np.arange(24) < M, np.arange(24), NR - 24 + np.arange(24))
    mode_row = np.zeros((SP, 32, 32))
    for owner in range(SP):
        for q in range(QN):
            mode = owner * QN + q
            j, kk = mode // M, mode % M
            for r in range(RL):
                p = 2.0 * np.pi * ((freq[j] * r) % NR) / NR
                for x, line, sign in ((rows, q, 1.0), (turned, QN + q, -1.0)):
                    x[owner, line, r * 24 + kk] = sign * np.cos(p)
                    x[owner, line, r * 24 + 12 + kk] = sign * np.sin(p)
                for x, line in ((rows, QN + q), (turned, q)):
                    x[owner, line, r * 24 + kk] = -np.sin(p)
                    x[owner, line, r * 24 + 12 + kk] = np.cos(p)
            mode_row[owner, q, j] = mode_row[owner, QN + q, j] = 1.0
    rows, turned = split_np(rows.reshape(SP * 32, 256)), split_np(turned.reshape(SP * 32, 256))
    scale = np.zeros((1, 256), np.float32)
    scale[0, :192] = np.tile(doubled, RL)
    return (
        table,
        inverse(forward * doubled[None, :]),
        inverse(forward),
        rows,
        turned,
        mode_row.reshape(SP * 32, 32).astype(ml_dtypes.bfloat16),
        scale,
    )


TABLE, INVERSE, BACK, ROWS, ROWS_TURNED, MODE_ROW, SCALE = make_tables()


def dot(a, b):
    return lax.dot_general(a, b, (((1,), (0,)), ((), ())), preferred_element_type=F32)


def dot_nt(a, b):
    return lax.dot_general(a, b, (((1,), (1,)), ((), ())), preferred_element_type=F32)


def dot_tn(a, b):
    return lax.dot_general(a, b, (((0,), (0,)), ((), ())), preferred_element_type=F32)


def split(values):
    high = values.astype(BF)
    return high, (values - high.astype(F32)).astype(BF)


def gelu_parts(v):
    cdf = 0.5 * (1.0 + lax.erf(v * ROOT_HALF))
    return v * cdf, cdf + v * jnp.exp(-0.5 * v * v) * INV_ROOT_TAU


def store_taps(taps, i, x):
    col = lax.broadcasted_iota(jnp.int32, (CP, NC), 1)
    taps[i, 0:CP] = jnp.where(col == 0, 0.0, pltpu.roll(x, 1, 1)).astype(BF)
    taps[i, CP : 2 * CP] = x.astype(BF)
    taps[i, 2 * CP : 3 * CP] = jnp.where(col == NC - 1, 0.0, pltpu.roll(x, NC - 1, 1)).astype(BF)


def row_transform(cols, matrix):
    both = dot_nt(matrix, jnp.concatenate(split(cols), axis=0))
    return (both[:, 0:128] + both[:, 128:256]).astype(BF)


def row_expand(modes, matrix):
    return dot_tn(modes, matrix)


def strip_pair(even, top, bottom):
    top, bottom = [jnp.concatenate([x[0:CO].astype(F32) for x in rows], axis=0) for rows in (top, bottom)]
    return jnp.where(even, bottom, top).astype(BF), jnp.where(even, top, bottom).astype(BF)


def halo_rows(even, first, second):
    first, second = first[0].astype(F32), second[0].astype(F32)
    above, below = jnp.where(even, second, first), jnp.where(even, first, second)
    rest = jnp.zeros((CP - CO, NC), F32)
    return [jnp.concatenate([x[i * CO : (i + 1) * CO], rest], axis=0) for x in (above, below) for i in range(2)]


def place_rows(rows, left):
    high, low = split(rows)
    high, low = high.astype(F32), low.astype(F32)
    left[...] = jnp.zeros_like(left)
    for lev in range(LEV):
        for r in range(RL):
            at = (lev * RL + r) * CO
            h = high[lev * 64 : lev * 64 + CO, r * 24 : r * 24 + 24]
            w = low[lev * 64 : lev * 64 + CO, r * 24 : r * 24 + 24]
            left[at : at + CO, 0:72] = jnp.concatenate([h, h, w], axis=1)


def kernel_a(place, field, table, high, low, turned_high, turned_low, mode_row, message, matrix, flat, cols):
    j = lax.broadcasted_iota(jnp.int32, (32, 128), 0)
    turn = ((j + jnp.where(j < M, 0, NR - 24)) * place[0]) % SP
    angle = turn.astype(F32) * (2.0 * math.pi / SP)
    t_high, t_low = split(jnp.concatenate([jnp.cos(angle), jnp.sin(angle)], axis=1))
    phase = dot(mode_row[...], t_high) + dot(mode_row[...], t_low)
    cosine, sine = phase[:, 0:128], phase[:, 128:256]
    cosine, sine = jnp.concatenate([cosine, cosine], axis=1), jnp.concatenate([sine, sine], axis=1)
    first = high[...].astype(F32) + low[...].astype(F32)
    turned = turned_high[...].astype(F32) + turned_low[...].astype(F32)
    turned = (first * cosine + turned * sine).astype(BF)
    matrix[...] = turned
    flat[...] = dot(field[...], table[...])
    cols[...] = jnp.zeros_like(cols)
    for lev in range(LEV):
        for r in range(RL):
            part = flat[pl.ds(lev * C * RL + r, C, stride=RL), :]
            cols[lev * 64 : lev * 64 + C, r * 24 : r * 24 + 24] = part[:, 0:24]
    message[...] = row_transform(cols[...], turned)


def prepare(one, two, point, w_one, w_two, w_two_back, w_one_back, w_point, w_point_back, base, wide):
    def spread(target, rows):
        wide[...] = jnp.zeros_like(wide)
        for t in range(4):
            wide[t * CP : (t + 1) * CP, t * rows : t * rows + base.shape[1]] = base[...]
        target[...] = wide[:, 0 : target.shape[1]].astype(BF)

    for kernel, forward, backward in ((one, w_one, w_one_back), (two, w_two, w_two_back)):
        base[...] = jnp.zeros_like(base)
        for a in range(3):
            for b in range(3):
                at = (a * 3 + b) * CP
                base[0:C, at : at + C] = jnp.transpose(kernel[a, b].astype(F32))
        spread(forward, GR)
        for a in range(3):
            for b in range(3):
                at = ((2 - a) * 3 + 2 - b) * CP
                base[0:C, at : at + C] = kernel[a, b].astype(F32)
        spread(backward, GR)
    for target, matrix in ((w_point, jnp.transpose(point[...].astype(F32))), (w_point_back, point[...].astype(F32))):
        wide[...] = jnp.zeros_like(wide)
        for t in range(4):
            wide[t * CP : t * CP + C, t * CP : t * CP + C] = matrix
        target[...] = wide[:, 0 : 4 * CP].astype(BF)


def kernel_rows(place, field, cot, one, two, point, after, rows, strip_one, strip_two, cot_rows, w_one, w_two, w_two_back, w_one_back, w_point, w_point_back, wide, base, spread):
    even = place[0] % 2 == 0

    @pl.when(pl.program_id(0) == 0)
    def _():
        prepare(one, two, point, w_one, w_two, w_two_back, w_one_back, w_point, w_point_back, base, spread)

    for k, (source, target) in enumerate(((field, rows), (cot, cot_rows))):
        for n in range(0, NC, 128):
            wide[k, n // 128, 0 : C * RL, :] = source[0, :, n : n + 128].astype(F32)
            wide[k, n // 128, C * RL :, :] = jnp.zeros((12 * RL, 128), F32)
        for n in range(0, NC, 128):
            found = [wide[k, n // 128, pl.ds(r, CP, stride=RL), :] for r in range(RL)]
            for r in range(RL):
                target[0, r, :, n : n + 128] = found[r].astype(BF)
            if k == 0:
                x, y = strip_pair(even, found[0:2], found[RL - 2 :])
                strip_one[0, :, n : n + 128], strip_two[0, :, n : n + 128] = x, y


def window(ref, i, count):
    return ref[i : i + count].reshape(count * GR, NC)


def kernel_b(place, rows, first, second, w_one, w_two, w_point, middle, slope, pre, taps, mid_taps):
    index = place[0]
    halo = halo_rows(index % 2 == 0, first, second)
    for i, x in enumerate(halo[0:2] + [rows[0, r].astype(F32) for r in range(RL)] + halo[2:4]):
        store_taps(taps, i, x)
    rest = jnp.zeros((CP - CO, NC), F32)
    for start, count in ((0, 4), (4, 3), (7, 3)):
        d = dot(w_one[0 : CP * count, 0 : GR * (count + 2)], window(taps, start, count + 2))
        for t in range(count):
            i = start + t
            value, gradient = gelu_parts(d[t * CP : t * CP + CO])
            if i in (0, RL + 1):
                keep = jnp.where(index == (0 if i == 0 else SP - 1), 0.0, 1.0).astype(F32)
                value, gradient = value * keep, gradient * keep
            slope[0, i] = jnp.concatenate([gradient, rest], axis=0).astype(BF)
            value = jnp.concatenate([value, rest], axis=0)
            middle[0, i] = value.astype(BF)
            store_taps(mid_taps, i, value)
    for r in (0, 4):
        d = dot(w_two[...], window(mid_taps, r, 6))
        d = d + dot(w_point[...], rows[0, r : r + 4].reshape(4 * CP, NC))
        for t in range(4):
            pre[0, r + t] = d[t * CP : t * CP + CO]


def own_modes(received):
    return jnp.sum(received.astype(F32), axis=0)


def by_channel(own, real, imag):
    rest = jnp.zeros((96, 128), F32)
    real[...] = jnp.transpose(jnp.concatenate([own, rest], axis=0))
    imag[...] = jnp.transpose(jnp.concatenate([pltpu.roll(own, 32 - QN, 0), rest], axis=0))


def weight_rows(weight, lines):
    lines[...] = jnp.zeros_like(lines)
    lines[:, 0:C] = weight[...]


def mode_line(lines, q, part):
    return lines[pl.ds(2 * q + part, C, stride=2 * QN), :]


def kernel_mix(received, weight, message, kept, real, imag, mixed, lines):
    own = own_modes(received[...])
    kept[...] = own
    by_channel(own, real, imag)
    weight_rows(weight, lines)
    mixed[...] = jnp.zeros_like(mixed)
    for q in range(QN):
        w_re, w_im = mode_line(lines, q, 0), mode_line(lines, q, 1)
        re, im = [], []
        for lev in range(LEV):
            s_re = real[lev * 64 : lev * 64 + C, q : q + 1]
            s_im = imag[lev * 64 : lev * 64 + C, q : q + 1]
            re.append(jnp.sum(w_re * s_re - w_im * s_im, axis=0, keepdims=True))
            im.append(jnp.sum(w_im * s_re + w_re * s_im, axis=0, keepdims=True))
        mixed[q : q + 1] = re[0] + pltpu.roll(re[1], 64, 1)
        mixed[QN + q : QN + q + 1] = im[0] + pltpu.roll(im[1], 64, 1)
    message[...] = jnp.broadcast_to(mixed[0:32].astype(BF)[None], (SP, 32, 128))


def mix_back(own, lines, mixed):
    other = pltpu.roll(own, 64, 1)
    mixed[...] = jnp.zeros_like(mixed)
    for q in range(QN):
        w_re, w_im = mode_line(lines, q, 0), mode_line(lines, q, 1)
        for lev, z in enumerate((own, other)):
            z_re, z_im = z[q : q + 1], z[QN + q : QN + q + 1]
            at = lev * 64
            mixed[at : at + C, q : q + 1] = jnp.sum(w_re * z_re + w_im * z_im, axis=1, keepdims=True)
            mixed[at : at + C, QN + q : QN + q + 1] = jnp.sum(w_re * z_im - w_im * z_re, axis=1, keepdims=True)
    return jnp.transpose(mixed[...])[0:32].astype(BF)


def kernel_spec_grad(p0, p1, p2, p3, grad, s_re, s_im, lines):
    pairs = (p0, p1, p2, p3)
    co = []
    for i, pair in enumerate(pairs):
        by_channel(pair[0:32], s_re.at[i], s_im.at[i])
        co.append((pair[32:64], pltpu.roll(pair[32:64], 64, 1)))
    for q in range(QN):
        res, ims = [], []
        for i in range(4):
            re, im = jnp.zeros((C, 128), F32), jnp.zeros((C, 128), F32)
            for lev in range(LEV):
                at = lev * 64
                a, b = s_re[i, at : at + C, q : q + 1], s_im[i, at : at + C, q : q + 1]
                x, y = co[i][lev][q : q + 1], co[i][lev][QN + q : QN + q + 1]
                re = re + (a * x + b * y)
                im = im + (a * y - b * x)
            res.append(re)
            ims.append(im)
        lines[pl.ds(2 * q, C, stride=2 * QN), :] = (res[0] + res[1]) + (res[2] + res[3])
        lines[pl.ds(2 * q + 1, C, stride=2 * QN), :] = (ims[0] + ims[1]) + (ims[2] + ims[3])
    grad[...] = lines[:, 0:C]


def kernel_d(place, received, matrix, inverse, pre, cot, table, scale, values, slopes, strip_one, strip_two, message, left, spec, kept, cols):
    lev = pl.program_id(0)

    @pl.when(lev == 0)
    def _():
        place_rows(row_expand(received[...], matrix[...]), left)
        spec[...] = dot(left[...].astype(BF), inverse[...]).reshape(LEV * RL, CO, NC)
        cols[...] = jnp.zeros_like(cols)

    rest = jnp.zeros((CP - CO, NC), F32)
    edges = {}
    for r in range(RL):
        value, gradient = gelu_parts(pre[0, r] + spec[lev * RL + r])
        values[0, r] = jnp.concatenate([value, rest], axis=0).astype(BF)
        s = jnp.concatenate([gradient, rest], axis=0) * cot[0, r].astype(F32)
        slopes[0, r] = s.astype(BF)
        edges[r] = s
    x, y = strip_pair(place[0] % 2 == 0, [edges[0], edges[1]], [edges[RL - 2], edges[RL - 1]])
    strip_one[0], strip_two[0] = x, y
    kept[lev] = dot(slopes[0].reshape(RL * CP, NC), table[...])

    @pl.when(lev == LEV - 1)
    def _():
        for at in range(LEV):
            for r in range(RL):
                cols[at * 64 : at * 64 + CO, r * 24 : r * 24 + 24] = kept[at, r * CP : r * CP + CO, 0:24]
        message[...] = row_transform(cols[...] * scale[...], matrix[...])


def kernel_out(values, after, out, wide):
    for lev in range(LEV):
        for r in range(RL):
            for n in range(0, NC, 128):
                x = values[lev, r, :, n : n + 128].astype(F32)
                wide[n // 128, pl.ds(lev * C * RL + r, C, stride=RL), :] = x[0:C]
    for n in range(0, NC, 128):
        for lev in range(LEV):
            out[lev, :, n : n + 128] = wide[n // 128, lev * C * RL : (lev + 1) * C * RL].astype(BF)


def kernel_own(received, kept, sums):
    sums[0:32] = kept[...]
    sums[32:64] = own_modes(received[...])


def kernel_mix_back(sums, weight, cofield, mixed, lines):
    weight_rows(weight, lines)
    cofield[...] = mix_back(sums[32:64], lines, mixed)


def kernel_send_back(cofield, p0, p1, p2, p3, message):
    total = (p0[32:64] + p1[32:64]) + (p2[32:64] + p3[32:64])
    row = lax.broadcasted_iota(jnp.int32, (32, 128), 0)
    total = jnp.where(row < 2 * QN, cofield[...].astype(F32), total).astype(BF)
    message[...] = jnp.broadcast_to(total[None], (SP, 32, 128))


def kernel_e_zero(slopes, middle, rows, slope, w_two, grad_two, inner, taps):
    left, right = [], []
    for r in range(RL):
        store_taps(taps, r, slopes[0, r].astype(F32))
        left.append(jnp.concatenate([middle[0, r], middle[0, r + 1], middle[0, r + 2], rows[0, r]], axis=0))
        right.append(taps[r])
    for start in (0, 3):
        d = dot(w_two[0 : 3 * CP, 0 : 5 * GR], window(taps, start, 5))
        for t in range(3):
            value = d[t * CP : (t + 1) * CP] * slope[0, start + t + 2].astype(F32)
            inner[0, start + t] = value.astype(BF)
    part = dot_nt(jnp.concatenate(left, axis=1), jnp.concatenate(right, axis=1))

    @pl.when(pl.program_id(0) == 0)
    def _():
        grad_two[...] = part

    @pl.when(pl.program_id(0) > 0)
    def _():
        grad_two[...] += part


def kernel_e(place, slopes, first, second, rows, f_first, f_second, slope, w_two, modes, grad_two, inner, outer, message, taps, pre_taps, grad_one, sums, packed):
    index = place[0]
    lev = pl.program_id(0)
    even = index % 2 == 0
    halo = halo_rows(even, first, second)
    near = [slopes[0, r].astype(F32) for r in (0, 1, RL - 2, RL - 1)]
    for i, x in enumerate(halo[0:2] + near + halo[2:4]):
        store_taps(taps, i, x)
    for i in range(6):
        store_taps(pre_taps, i + 1, inner[0, i].astype(F32))
    for k in range(2):
        d = dot(w_two[0 : 2 * CP, 0 : 4 * GR], window(taps, 4 * k, 4))
        for t in range(2):
            i = RL * k + t
            value = d[t * CP : (t + 1) * CP] * slope[0, i].astype(F32)
            if i in (0, RL + 1):
                value = value * jnp.where(index == (0 if i == 0 else SP - 1), 0.0, 1.0).astype(F32)
            else:
                store_taps(pre_taps, i - 1, value)
            outer[0, 2 * k + t] = value.astype(BF)
    halo = halo_rows(even, f_first, f_second)
    field = [halo[1].astype(BF)] + [rows[0, r] for r in range(RL)] + [halo[2].astype(BF)]
    left = jnp.concatenate([jnp.concatenate(field[r : r + 3], axis=0) for r in range(RL)], axis=1)
    right = jnp.concatenate([pre_taps[r] for r in range(RL)], axis=1)
    part_one = dot_nt(left, right)

    @pl.when(lev == 0)
    def _():
        grad_one[...] = part_one

    @pl.when(lev == LEV - 1)
    def _():
        sums[...] = jnp.zeros_like(sums)
        two, one = grad_two[...], grad_one[...] + part_one
        for b in range(3):
            at = b * CP
            sums[b * GR : (b + 1) * GR, 0:C] = two[0:GR, at : at + C]
            sums[b * GR : (b + 1) * GR, C : 2 * C] = one[:, at : at + C]
        sums[0:CP, 2 * C : 3 * C] = two[GR : GR + CP, CP : CP + C]
        packed[...] = modes[...].astype(F32)
        for owner in range(SP):
            packed[owner, 2 * QN : 32] = sums[owner * SHARE : (owner + 1) * SHARE]
        message[...] = packed[...].astype(BF)


def kernel_e_two(inner, outer, slopes, w_one, w_point, after, back, taps, wide):
    lines = [outer[0, 0], outer[0, 1]] + [inner[0, i] for i in range(6)] + [outer[0, 2], outer[0, 3]]
    for i, x in enumerate(lines):
        store_taps(taps, i, x.astype(F32))
    for r in (0, 4):
        d = dot(w_one[...], window(taps, r, 6))
        d = d + dot(w_point[...], slopes[0, r : r + 4].reshape(4 * CP, NC))
        for t in range(4):
            for n in range(0, NC, 128):
                wide[n // 128, pl.ds(r + t, C, stride=RL), :] = d[t * CP : t * CP + C, n : n + 128]
    for n in range(0, NC, 128):
        back[0, :, n : n + 128] = wide[n // 128]


def kernel_f(received, matrix, inverse, back, out, point, one, two, left, packed, sums):
    lev = pl.program_id(0)

    @pl.when(lev == 0)
    def _():
        modes = received[...].reshape(SP * 32, 128)
        r_high, r_low = split(row_expand(modes, matrix[...]))
        r_high, r_low = r_high.astype(F32), r_low.astype(F32)
        rest = jnp.zeros((C, 56), F32)
        for at in range(LEV):
            for r in range(RL):
                h = r_high[at * 64 : at * 64 + C, r * 24 : r * 24 + 24]
                w = r_low[at * 64 : at * 64 + C, r * 24 : r * 24 + 24]
                left[at, pl.ds(r, C, stride=RL), :] = jnp.concatenate([h, h, w, rest], axis=1)
        packed[...] = received[...].astype(F32)
        for owner in range(SP):
            sums[owner * SHARE : (owner + 1) * SHARE] = packed[owner, 2 * QN : 32]
        scaled = sums[...] * (1.0 / math.sqrt(NR * NC * LEV * 4))
        for a in range(3):
            for b in range(3):
                at = (2 - b) * GR + a * CP
                two[a, b] = scaled[at : at + C, 0:C]
                one[a, b] = scaled[at : at + C, C : 2 * C]
        point[...] = scaled[0:C, 2 * C : 3 * C]

    out[0] = (back[0] + dot(left[lev].astype(BF), inverse[...])).astype(BF)


def shape(dims, kind):
    return jax.ShapeDtypeStruct(dims, kind)


def params(mib):
    return pltpu.CompilerParams(vmem_limit_bytes=mib * 1024 * 1024)


def estimate(us):
    if us is None:
        return None
    return pl.CostEstimate(flops=us * 10**9, bytes_accessed=us * 3 * 10**6, transcendentals=0)


def level_spec(*dims):
    return pl.BlockSpec((1,) + dims, lambda lev: (lev,) + (0,) * len(dims))


def whole_spec(*dims):
    return pl.BlockSpec(dims, lambda lev: (0,) * len(dims))


def partners(first, second):
    pairs = [(i, i ^ 1) for i in range(SP)]
    others = [(i, i + 1) for i in range(1, SP - 1, 2)] + [(i + 1, i) for i in range(1, SP - 1, 2)]
    return lax.ppermute(first, "sp", pairs), lax.ppermute(second, "sp", others)


def exchange(x):
    return lax.all_to_all(x, "sp", 0, 0, tiled=True)


def anywhere():
    return pl.BlockSpec(memory_space=pl.ANY)


def plain_call(kernel, operands, after, outs, scratch, mib, name, place=(), cost=None):
    vmem = pl.BlockSpec(memory_space=pltpu.VMEM)
    return pl.pallas_call(
        kernel,
        in_specs=[pl.BlockSpec(memory_space=pltpu.SMEM)] * len(place) + [vmem] * len(operands) + [anywhere()] * len(after),
        out_specs=[vmem] * len(outs),
        out_shape=outs,
        scratch_shapes=scratch,
        compiler_params=params(mib),
        cost_estimate=estimate(cost),
        name=name,
    )(*place, *operands, *after)


def local(field, cotangent, spec_weight, point_weight, kernel_one, kernel_two):
    place = lax.axis_index("sp").astype(jnp.int32).reshape(1)
    inputs = field.reshape(LEV * C * RL, NC)
    table = jnp.asarray(TABLE)
    weight = jnp.transpose(spec_weight, (1, 3, 0, 2)).reshape(C * QN * 2, C)
    strip = shape((LEV, 2 * CO, NC), BF)
    grid_rows = shape((LEV, RL, CP, NC), BF)
    natural = shape((LEV, C * RL, NC), BF)
    flat, cols = pltpu.VMEM((LEV * C * RL, 128), F32), pltpu.VMEM((128, 256), F32)
    row_matrix = shape((SP * 32, 256), BF)
    message, matrix = plain_call(
        kernel_a,
        (inputs, table, *map(jnp.asarray, ROWS + ROWS_TURNED), jnp.asarray(MODE_ROW)),
        (),
        [shape((SP * 32, 128), BF), row_matrix],
        [flat, cols],
        56,
        "field_modes",
        (place,),
    )
    arrived = exchange(message.reshape(SP, 32, 128))
    toeplitz, blocks = shape((4 * CP, 6 * GR), BF), shape((4 * CP, 4 * CP), BF)
    weights_out = [toeplitz] * 4 + [blocks] * 2
    rows, f_first, f_second, cot_rows, w_one, w_two, w_two_back, w_one_back, w_point, w_point_back = pl.pallas_call(
        kernel_rows,
        grid=(LEV,),
        in_specs=[
            pl.BlockSpec(memory_space=pltpu.SMEM),
            level_spec(C * RL, NC),
            level_spec(C * RL, NC),
            whole_spec(3, 3, C, C),
            whole_spec(3, 3, C, C),
            whole_spec(C, C),
            anywhere(),
        ],
        out_specs=[level_spec(RL, CP, NC), level_spec(2 * CO, NC), level_spec(2 * CO, NC), level_spec(RL, CP, NC)]
        + [whole_spec(*x.shape) for x in weights_out],
        out_shape=[grid_rows, strip, strip, grid_rows] + weights_out,
        scratch_shapes=[
            pltpu.VMEM((2, NC // 128, (C + 12) * RL, 128), F32),
            pltpu.VMEM((CP, 9 * CP), F32),
            pltpu.VMEM((4 * CP, 6 * GR), F32),
        ],
        compiler_params=params(56),
        name="row_layout",
    )(place, field.reshape(natural.shape), cotangent.reshape(natural.shape), kernel_one, kernel_two, point_weight, message)
    f_first, f_second = partners(f_first, f_second)

    square, lines = pltpu.VMEM((128, 128), F32), pltpu.VMEM((C * QN * 2, 128), F32)
    mixed, kept = plain_call(
        kernel_mix,
        (arrived, weight),
        (),
        [shape((SP, 32, 128), BF), shape((32, 128), F32)],
        [square, square, square, lines],
        8,
        "mode_mix",
    )
    gathered = exchange(mixed).reshape(SP * 32, 128)

    middle, slope, pre = pl.pallas_call(
        kernel_b,
        grid=(LEV,),
        in_specs=[
            pl.BlockSpec(memory_space=pltpu.SMEM),
            level_spec(RL, CP, NC),
            level_spec(2 * CO, NC),
            level_spec(2 * CO, NC),
            whole_spec(4 * CP, 6 * GR),
            whole_spec(4 * CP, 6 * GR),
            whole_spec(4 * CP, 4 * CP),
        ],
        out_specs=[
            level_spec(RL + 2, CP, NC),
            level_spec(RL + 2, CP, NC),
            level_spec(RL, CO, NC),
        ],
        out_shape=[
            shape((LEV, RL + 2, CP, NC), BF),
            shape((LEV, RL + 2, CP, NC), BF),
            shape((LEV, RL, CO, NC), F32),
        ],
        scratch_shapes=[pltpu.VMEM((RL + 4, GR, NC), BF), pltpu.VMEM((RL + 2, GR, NC), BF)],
        compiler_params=params(56),
        name="two_convolutions",
    )(place, rows, f_first, f_second, w_one, w_two, w_point)

    left, spec = pltpu.VMEM((LEV * RL * CO, 128), F32), pltpu.VMEM((LEV * RL * CO, NC), F32)
    values, slopes, s_first, s_second, message = pl.pallas_call(
        kernel_d,
        grid=(LEV,),
        in_specs=[
            pl.BlockSpec(memory_space=pltpu.SMEM),
            whole_spec(SP * 32, 128),
            whole_spec(SP * 32, 256),
            whole_spec(128, NC),
            level_spec(RL, CO, NC),
            level_spec(RL, CP, NC),
            whole_spec(NC, 128),
            whole_spec(1, 256),
        ],
        out_specs=[level_spec(RL, CP, NC)] * 2 + [level_spec(2 * CO, NC)] * 2 + [whole_spec(SP * 32, 128)],
        out_shape=[grid_rows, grid_rows, strip, strip, shape((SP * 32, 128), BF)],
        scratch_shapes=[
            left,
            pltpu.VMEM((LEV * RL, CO, NC), F32),
            pltpu.VMEM((LEV, RL * CP, 128), F32),
            cols,
        ],
        compiler_params=params(52),
        name="output_and_slope",
    )(place, gathered, matrix, jnp.asarray(INVERSE), pre, cot_rows, table, jnp.asarray(SCALE))
    s_first, s_second = partners(s_first, s_second)

    grad_two, inner = pl.pallas_call(
        kernel_e_zero,
        grid=(LEV,),
        in_specs=[
            level_spec(RL, CP, NC),
            level_spec(RL + 2, CP, NC),
            level_spec(RL, CP, NC),
            level_spec(RL + 2, CP, NC),
            whole_spec(4 * CP, 6 * GR),
        ],
        out_specs=[whole_spec(GR + CP, GR), level_spec(6, CP, NC)],
        out_shape=[shape((GR + CP, GR), F32), shape((LEV, 6, CP, NC), BF)],
        scratch_shapes=[pltpu.VMEM((RL, GR, NC), BF)],
        compiler_params=params(56),
        name="inner_slopes_and_gradients",
    )(slopes, middle, rows, slope, w_two_back)
    outer, message = pl.pallas_call(
        kernel_e,
        grid=(LEV,),
        in_specs=[
            pl.BlockSpec(memory_space=pltpu.SMEM),
            level_spec(RL, CP, NC),
            level_spec(2 * CO, NC),
            level_spec(2 * CO, NC),
            level_spec(RL, CP, NC),
            level_spec(2 * CO, NC),
            level_spec(2 * CO, NC),
            level_spec(RL + 2, CP, NC),
            whole_spec(4 * CP, 6 * GR),
            whole_spec(SP, 32, 128),
            whole_spec(GR + CP, GR),
            level_spec(6, CP, NC),
        ],
        out_specs=[level_spec(4, CP, NC), whole_spec(SP, 32, 128)],
        out_shape=[shape((LEV, 4, CP, NC), BF), shape((SP, 32, 128), BF)],
        scratch_shapes=[
            pltpu.VMEM((RL, GR, NC), BF),
            pltpu.VMEM((RL, GR, NC), BF),
            pltpu.VMEM((GR, GR), F32),
            pltpu.VMEM((SP * SHARE, 128), F32),
            pltpu.VMEM((SP, 32, 128), F32),
        ],
        compiler_params=params(56),
        name="outer_slopes_and_gradients",
    )(place, slopes, s_first, s_second, rows, f_first, f_second, slope, w_two_back, message.reshape(SP, 32, 128), grad_two, inner)
    arrived = exchange(message)
    back = pl.pallas_call(
        kernel_e_two,
        grid=(LEV,),
        in_specs=[
            level_spec(6, CP, NC),
            level_spec(4, CP, NC),
            level_spec(RL, CP, NC),
            whole_spec(4 * CP, 6 * GR),
            whole_spec(4 * CP, 4 * CP),
            anywhere(),
        ],
        out_specs=level_spec(C * RL, NC),
        out_shape=shape(natural.shape, F32),
        scratch_shapes=[pltpu.VMEM((RL + 2, GR, NC), BF), pltpu.VMEM((NC // 128, C * RL, 128), F32)],
        compiler_params=params(56),
        name="backward_convolution",
    )(inner, outer, slopes, w_one_back, w_point_back, message)
    (out,) = plain_call(
        kernel_out,
        (values,),
        (message,),
        [natural],
        [pltpu.VMEM((NC // 128, LEV * C * RL, 128), F32)],
        56,
        "output_layout",
    )
    (sums,) = plain_call(
        kernel_own, (arrived, kept), (), [shape((64, 128), F32)], [], 8, "own_sums"
    )
    others = [lax.ppermute(sums, "rep", [(i, i ^ k) for i in range(4)]) for k in (1, 2, 3)]
    (cofield,) = plain_call(
        kernel_mix_back, (sums, weight), (), [shape((32, 128), BF)], [square, lines], 8, "mode_mix_back"
    )
    (message,) = plain_call(
        kernel_send_back, (cofield, sums, *others), (), [shape((SP, 32, 128), BF)], [], 8, "gradient_modes"
    )
    gathered = exchange(message)
    (spec_grad,) = plain_call(
        kernel_spec_grad,
        (sums, *others),
        (),
        [shape(weight.shape, F32)],
        [pltpu.VMEM((4, 128, 128), F32)] * 2 + [lines],
        8,
        "spectral_gradient",
    )
    kernel_out_shape = shape((3, 3, C, C), F32)
    field_grad, point_total, one_total, two_total = pl.pallas_call(
        kernel_f,
        grid=(LEV,),
        in_specs=[
            whole_spec(SP, 32, 128),
            whole_spec(SP * 32, 256),
            whole_spec(128, NC),
            level_spec(C * RL, NC),
        ],
        out_specs=[level_spec(C * RL, NC), whole_spec(C, C), whole_spec(3, 3, C, C), whole_spec(3, 3, C, C)],
        out_shape=[natural, shape((C, C), F32), kernel_out_shape, kernel_out_shape],
        scratch_shapes=[
            pltpu.VMEM((LEV, C * RL, 128), F32),
            pltpu.VMEM((SP, 32, 128), F32),
            pltpu.VMEM((SP * SHARE, 128), F32),
        ],
        compiler_params=params(52),
        name="field_gradient",
    )(gathered, matrix, jnp.asarray(BACK), back)
    spec_total = jnp.transpose(spec_grad.reshape(C, QN, 2, C), (2, 0, 3, 1))
    return (
        out.reshape(field.shape),
        field_grad.reshape(field.shape),
        spec_total,
        point_total,
        one_total,
        two_total,
    )


def solution(mesh):
    specs = (
        P("rep", None, None, "sp", None),
        P("rep", None, None, "sp", None),
        P(None, None, None, "sp"),
        P(),
        P(),
        P(),
    )
    return jax.shard_map(local, mesh=mesh, in_specs=specs, out_specs=specs, check_vma=False)
```

```python
import math

import jax
import jax.numpy as jnp
import numpy as np
import ml_dtypes
from jax import lax
from jax.experimental import pallas as pl
from jax.experimental.pallas import tpu as pltpu
from jax.sharding import PartitionSpec as P

M = 12
C = 36
CP = 48
CO = 40
LEV = 2
RL = 8
NC = 1024
NR = 256
SP = 32
QN = 9
GR = 3 * CP
SHARE = 14

ROOT_HALF = 0.7071067811865476
INV_ROOT_TAU = 0.3989422804014327
BF = jnp.bfloat16
F32 = jnp.float32


def split_np(values):
    high = values.astype(np.float32).astype(ml_dtypes.bfloat16)
    low = (values - high.astype(np.float64)).astype(np.float32).astype(ml_dtypes.bfloat16)
    return high, low


def make_tables():
    n = np.arange(NC)[:, None]
    k = np.arange(M)[None, :]
    t = 2.0 * np.pi * ((n * k) % NC) / NC
    forward = np.concatenate([np.cos(t), -np.sin(t)], axis=1)
    doubled = np.where(np.arange(M) == 0, 1.0, 2.0)
    doubled = np.concatenate([doubled, doubled]) / (NR * NC)
    table = np.zeros((NC, 128), np.float32)
    table[:, :24] = forward
    table = table.astype(ml_dtypes.bfloat16)

    def inverse(matrix):
        high, low = split_np(matrix.T)
        out = np.zeros((128, NC), ml_dtypes.bfloat16)
        out[0:24], out[24:48], out[48:72] = high, low, high
        return out

    rows, turned = np.zeros((SP, 32, 256)), np.zeros((SP, 32, 256))
    freq = np.where(np.arange(24) < M, np.arange(24), NR - 24 + np.arange(24))
    mode_row = np.zeros((SP, 32, 32))
    for owner in range(SP):
        for q in range(QN):
            mode = owner * QN + q
            j, kk = mode // M, mode % M
            for r in range(RL):
                p = 2.0 * np.pi * ((freq[j] * r) % NR) / NR
                for x, line, sign in ((rows, q, 1.0), (turned, QN + q, -1.0)):
                    x[owner, line, r * 24 + kk] = sign * np.cos(p)
                    x[owner, line, r * 24 + 12 + kk] = sign * np.sin(p)
                for x, line in ((rows, QN + q), (turned, q)):
                    x[owner, line, r * 24 + kk] = -np.sin(p)
                    x[owner, line, r * 24 + 12 + kk] = np.cos(p)
            mode_row[owner, q, j] = mode_row[owner, QN + q, j] = 1.0
    rows, turned = split_np(rows.reshape(SP * 32, 256)), split_np(turned.reshape(SP * 32, 256))
    scale = np.zeros((1, 256), np.float32)
    scale[0, :192] = np.tile(doubled, RL)
    return (
        table,
        inverse(forward * doubled[None, :]),
        inverse(forward),
        rows,
        turned,
        mode_row.reshape(SP * 32, 32).astype(ml_dtypes.bfloat16),
        scale,
    )


TABLE, INVERSE, BACK, ROWS, ROWS_TURNED, MODE_ROW, SCALE = make_tables()


def dot(a, b):
    return lax.dot_general(a, b, (((1,), (0,)), ((), ())), preferred_element_type=F32)


def dot_nt(a, b):
    return lax.dot_general(a, b, (((1,), (1,)), ((), ())), preferred_element_type=F32)


def dot_tn(a, b):
    return lax.dot_general(a, b, (((0,), (0,)), ((), ())), preferred_element_type=F32)


def split(values):
    high = values.astype(BF)
    return high, (values - high.astype(F32)).astype(BF)


def gelu_parts(v):
    cdf = 0.5 * (1.0 + lax.erf(v * ROOT_HALF))
    return v * cdf, cdf + v * jnp.exp(-0.5 * v * v) * INV_ROOT_TAU


def store_taps(taps, i, x):
    col = lax.broadcasted_iota(jnp.int32, (CP, NC), 1)
    taps[i, 0:CP] = jnp.where(col == 0, 0.0, pltpu.roll(x, 1, 1)).astype(BF)
    taps[i, CP : 2 * CP] = x.astype(BF)
    taps[i, 2 * CP : 3 * CP] = jnp.where(col == NC - 1, 0.0, pltpu.roll(x, NC - 1, 1)).astype(BF)


def row_transform(cols, matrix):
    both = dot_nt(matrix, jnp.concatenate(split(cols), axis=0))
    return (both[:, 0:128] + both[:, 128:256]).astype(BF)


def row_expand(modes, matrix):
    return dot_tn(modes, matrix)


def strip_pair(even, top, bottom):
    top, bottom = [jnp.concatenate([x[0:CO].astype(F32) for x in rows], axis=0) for rows in (top, bottom)]
    return jnp.where(even, bottom, top).astype(BF), jnp.where(even, top, bottom).astype(BF)


def halo_rows(even, first, second):
    first, second = first[0].astype(F32), second[0].astype(F32)
    above, below = jnp.where(even, second, first), jnp.where(even, first, second)
    rest = jnp.zeros((CP - CO, NC), F32)
    return [jnp.concatenate([x[i * CO : (i + 1) * CO], rest], axis=0) for x in (above, below) for i in range(2)]


def place_rows(rows, left):
    high, low = split(rows)
    high, low = high.astype(F32), low.astype(F32)
    left[...] = jnp.zeros_like(left)
    for lev in range(LEV):
        for r in range(RL):
            at = (lev * RL + r) * CO
            h = high[lev * 64 : lev * 64 + CO, r * 24 : r * 24 + 24]
            w = low[lev * 64 : lev * 64 + CO, r * 24 : r * 24 + 24]
            left[at : at + CO, 0:72] = jnp.concatenate([h, h, w], axis=1)


def kernel_a(place, field, table, high, low, turned_high, turned_low, mode_row, message, matrix, flat, cols):
    j = lax.broadcasted_iota(jnp.int32, (32, 128), 0)
    turn = ((j + jnp.where(j < M, 0, NR - 24)) * place[0]) % SP
    angle = turn.astype(F32) * (2.0 * math.pi / SP)
    t_high, t_low = split(jnp.concatenate([jnp.cos(angle), jnp.sin(angle)], axis=1))
    phase = dot(mode_row[...], t_high) + dot(mode_row[...], t_low)
    cosine, sine = phase[:, 0:128], phase[:, 128:256]
    cosine, sine = jnp.concatenate([cosine, cosine], axis=1), jnp.concatenate([sine, sine], axis=1)
    first = high[...].astype(F32) + low[...].astype(F32)
    turned = turned_high[...].astype(F32) + turned_low[...].astype(F32)
    turned = (first * cosine + turned * sine).astype(BF)
    matrix[...] = turned
    flat[...] = dot(field[...], table[...])
    cols[...] = jnp.zeros_like(cols)
    for lev in range(LEV):
        for r in range(RL):
            part = flat[pl.ds(lev * C * RL + r, C, stride=RL), :]
            cols[lev * 64 : lev * 64 + C, r * 24 : r * 24 + 24] = part[:, 0:24]
    message[...] = row_transform(cols[...], turned)


def prepare(one, two, point, w_one, w_two, w_two_back, w_one_back, w_point, w_point_back, base, wide):
    def spread(target, rows):
        wide[...] = jnp.zeros_like(wide)
        for t in range(4):
            wide[t * CP : (t + 1) * CP, t * rows : t * rows + base.shape[1]] = base[...]
        target[...] = wide[:, 0 : target.shape[1]].astype(BF)

    for kernel, forward, backward in ((one, w_one, w_one_back), (two, w_two, w_two_back)):
        base[...] = jnp.zeros_like(base)
        for a in range(3):
            for b in range(3):
                at = (a * 3 + b) * CP
                base[0:C, at : at + C] = jnp.transpose(kernel[a, b].astype(F32))
        spread(forward, GR)
        for a in range(3):
            for b in range(3):
                at = ((2 - a) * 3 + 2 - b) * CP
                base[0:C, at : at + C] = kernel[a, b].astype(F32)
        spread(backward, GR)
    for target, matrix in ((w_point, jnp.transpose(point[...].astype(F32))), (w_point_back, point[...].astype(F32))):
        wide[...] = jnp.zeros_like(wide)
        for t in range(4):
            wide[t * CP : t * CP + C, t * CP : t * CP + C] = matrix
        target[...] = wide[:, 0 : 4 * CP].astype(BF)


def kernel_rows(place, field, cot, one, two, point, after, rows, strip_one, strip_two, cot_rows, w_one, w_two, w_two_back, w_one_back, w_point, w_point_back, wide, base, spread):
    even = place[0] % 2 == 0

    @pl.when(pl.program_id(0) == 0)
    def _():
        prepare(one, two, point, w_one, w_two, w_two_back, w_one_back, w_point, w_point_back, base, spread)

    for k, (source, target) in enumerate(((field, rows), (cot, cot_rows))):
        for n in range(0, NC, 128):
            wide[k, n // 128, 0 : C * RL, :] = source[0, :, n : n + 128].astype(F32)
            wide[k, n // 128, C * RL :, :] = jnp.zeros((12 * RL, 128), F32)
        for n in range(0, NC, 128):
            found = [wide[k, n // 128, pl.ds(r, CP, stride=RL), :] for r in range(RL)]
            for r in range(RL):
                target[0, r, :, n : n + 128] = found[r].astype(BF)
            if k == 0:
                x, y = strip_pair(even, found[0:2], found[RL - 2 :])
                strip_one[0, :, n : n + 128], strip_two[0, :, n : n + 128] = x, y


def window(ref, i, count):
    return ref[i : i + count].reshape(count * GR, NC)


def kernel_b(place, rows, first, second, w_one, w_two, w_point, middle, slope, pre, taps, mid_taps):
    index = place[0]
    halo = halo_rows(index % 2 == 0, first, second)
    for i, x in enumerate(halo[0:2] + [rows[0, r].astype(F32) for r in range(RL)] + halo[2:4]):
        store_taps(taps, i, x)
    rest = jnp.zeros((CP - CO, NC), F32)
    for start, count in ((0, 4), (4, 3), (7, 3)):
        d = dot(w_one[0 : CP * count, 0 : GR * (count + 2)], window(taps, start, count + 2))
        for t in range(count):
            i = start + t
            value, gradient = gelu_parts(d[t * CP : t * CP + CO])
            if i in (0, RL + 1):
                keep = jnp.where(index == (0 if i == 0 else SP - 1), 0.0, 1.0).astype(F32)
                value, gradient = value * keep, gradient * keep
            slope[0, i] = jnp.concatenate([gradient, rest], axis=0).astype(BF)
            value = jnp.concatenate([value, rest], axis=0)
            middle[0, i] = value.astype(BF)
            store_taps(mid_taps, i, value)
    for r in (0, 4):
        d = dot(w_two[...], window(mid_taps, r, 6))
        d = d + dot(w_point[...], rows[0, r : r + 4].reshape(4 * CP, NC))
        for t in range(4):
            pre[0, r + t] = d[t * CP : t * CP + CO]


def own_modes(received):
    return jnp.sum(received.astype(F32), axis=0)


def by_channel(own, real, imag):
    rest = jnp.zeros((96, 128), F32)
    real[...] = jnp.transpose(jnp.concatenate([own, rest], axis=0))
    imag[...] = jnp.transpose(jnp.concatenate([pltpu.roll(own, 32 - QN, 0), rest], axis=0))


def weight_rows(weight, lines):
    lines[...] = jnp.zeros_like(lines)
    lines[:, 0:C] = weight[...]


def mode_line(lines, q, part):
    return lines[pl.ds(2 * q + part, C, stride=2 * QN), :]


def kernel_mix(received, weight, message, kept, real, imag, mixed, lines):
    own = own_modes(received[...])
    kept[...] = own
    by_channel(own, real, imag)
    weight_rows(weight, lines)
    mixed[...] = jnp.zeros_like(mixed)
    for q in range(QN):
        w_re, w_im = mode_line(lines, q, 0), mode_line(lines, q, 1)
        re, im = [], []
        for lev in range(LEV):
            s_re = real[lev * 64 : lev * 64 + C, q : q + 1]
            s_im = imag[lev * 64 : lev * 64 + C, q : q + 1]
            re.append(jnp.sum(w_re * s_re - w_im * s_im, axis=0, keepdims=True))
            im.append(jnp.sum(w_im * s_re + w_re * s_im, axis=0, keepdims=True))
        mixed[q : q + 1] = re[0] + pltpu.roll(re[1], 64, 1)
        mixed[QN + q : QN + q + 1] = im[0] + pltpu.roll(im[1], 64, 1)
    message[...] = jnp.broadcast_to(mixed[0:32].astype(BF)[None], (SP, 32, 128))


def mix_back(own, lines, mixed):
    other = pltpu.roll(own, 64, 1)
    mixed[...] = jnp.zeros_like(mixed)
    for q in range(QN):
        w_re, w_im = mode_line(lines, q, 0), mode_line(lines, q, 1)
        for lev, z in enumerate((own, other)):
            z_re, z_im = z[q : q + 1], z[QN + q : QN + q + 1]
            at = lev * 64
            mixed[at : at + C, q : q + 1] = jnp.sum(w_re * z_re + w_im * z_im, axis=1, keepdims=True)
            mixed[at : at + C, QN + q : QN + q + 1] = jnp.sum(w_re * z_im - w_im * z_re, axis=1, keepdims=True)
    return jnp.transpose(mixed[...])[0:32].astype(BF)


def kernel_spec_grad(p0, p1, p2, p3, grad, s_re, s_im, lines):
    pairs = (p0, p1, p2, p3)
    co = []
    for i, pair in enumerate(pairs):
        by_channel(pair[0:32], s_re.at[i], s_im.at[i])
        co.append((pair[32:64], pltpu.roll(pair[32:64], 64, 1)))
    for q in range(QN):
        res, ims = [], []
        for i in range(4):
            re, im = jnp.zeros((C, 128), F32), jnp.zeros((C, 128), F32)
            for lev in range(LEV):
                at = lev * 64
                a, b = s_re[i, at : at + C, q : q + 1], s_im[i, at : at + C, q : q + 1]
                x, y = co[i][lev][q : q + 1], co[i][lev][QN + q : QN + q + 1]
                re = re + (a * x + b * y)
                im = im + (a * y - b * x)
            res.append(re)
            ims.append(im)
        lines[pl.ds(2 * q, C, stride=2 * QN), :] = (res[0] + res[1]) + (res[2] + res[3])
        lines[pl.ds(2 * q + 1, C, stride=2 * QN), :] = (ims[0] + ims[1]) + (ims[2] + ims[3])
    grad[...] = lines[:, 0:C]


def kernel_d(place, received, matrix, inverse, pre, cot, table, scale, values, slopes, strip_one, strip_two, message, left, spec, kept, cols):
    lev = pl.program_id(0)

    @pl.when(lev == 0)
    def _():
        place_rows(row_expand(received[...], matrix[...]), left)
        spec[...] = dot(left[...].astype(BF), inverse[...]).reshape(LEV * RL, CO, NC)
        cols[...] = jnp.zeros_like(cols)

    rest = jnp.zeros((CP - CO, NC), F32)
    edges = {}
    for r in range(RL):
        value, gradient = gelu_parts(pre[0, r] + spec[lev * RL + r])
        values[0, r] = jnp.concatenate([value, rest], axis=0).astype(BF)
        s = jnp.concatenate([gradient, rest], axis=0) * cot[0, r].astype(F32)
        slopes[0, r] = s.astype(BF)
        edges[r] = s
    x, y = strip_pair(place[0] % 2 == 0, [edges[0], edges[1]], [edges[RL - 2], edges[RL - 1]])
    strip_one[0], strip_two[0] = x, y
    kept[lev] = dot(slopes[0].reshape(RL * CP, NC), table[...])

    @pl.when(lev == LEV - 1)
    def _():
        for at in range(LEV):
            for r in range(RL):
                cols[at * 64 : at * 64 + CO, r * 24 : r * 24 + 24] = kept[at, r * CP : r * CP + CO, 0:24]
        message[...] = row_transform(cols[...] * scale[...], matrix[...])


def kernel_out(values, after, out, wide):
    for lev in range(LEV):
        for r in range(RL):
            for n in range(0, NC, 128):
                x = values[lev, r, :, n : n + 128].astype(F32)
                wide[n // 128, pl.ds(lev * C * RL + r, C, stride=RL), :] = x[0:C]
    for n in range(0, NC, 128):
        for lev in range(LEV):
            out[lev, :, n : n + 128] = wide[n // 128, lev * C * RL : (lev + 1) * C * RL].astype(BF)


def kernel_own(received, kept, sums):
    sums[0:32] = kept[...]
    sums[32:64] = own_modes(received[...])


def kernel_mix_back(sums, weight, cofield, mixed, lines):
    weight_rows(weight, lines)
    cofield[...] = mix_back(sums[32:64], lines, mixed)


def kernel_send_back(cofield, p0, p1, p2, p3, message):
    total = (p0[32:64] + p1[32:64]) + (p2[32:64] + p3[32:64])
    row = lax.broadcasted_iota(jnp.int32, (32, 128), 0)
    total = jnp.where(row < 2 * QN, cofield[...].astype(F32), total).astype(BF)
    message[...] = jnp.broadcast_to(total[None], (SP, 32, 128))


def kernel_e_zero(slopes, middle, rows, slope, w_two, grad_two, inner, taps):
    left, right = [], []
    for r in range(RL):
        store_taps(taps, r, slopes[0, r].astype(F32))
        left.append(jnp.concatenate([middle[0, r], middle[0, r + 1], middle[0, r + 2], rows[0, r]], axis=0))
        right.append(taps[r])
    for start in (0, 3):
        d = dot(w_two[0 : 3 * CP, 0 : 5 * GR], window(taps, start, 5))
        for t in range(3):
            value = d[t * CP : (t + 1) * CP] * slope[0, start + t + 2].astype(F32)
            inner[0, start + t] = value.astype(BF)
    part = dot_nt(jnp.concatenate(left, axis=1), jnp.concatenate(right, axis=1))

    @pl.when(pl.program_id(0) == 0)
    def _():
        grad_two[...] = part

    @pl.when(pl.program_id(0) > 0)
    def _():
        grad_two[...] += part


def kernel_e(place, slopes, first, second, rows, f_first, f_second, slope, w_two, modes, grad_two, inner, outer, message, taps, pre_taps, grad_one, sums, packed):
    index = place[0]
    lev = pl.program_id(0)
    even = index % 2 == 0
    halo = halo_rows(even, first, second)
    near = [slopes[0, r].astype(F32) for r in (0, 1, RL - 2, RL - 1)]
    for i, x in enumerate(halo[0:2] + near + halo[2:4]):
        store_taps(taps, i, x)
    for i in range(6):
        store_taps(pre_taps, i + 1, inner[0, i].astype(F32))
    for k in range(2):
        d = dot(w_two[0 : 2 * CP, 0 : 4 * GR], window(taps, 4 * k, 4))
        for t in range(2):
            i = RL * k + t
            value = d[t * CP : (t + 1) * CP] * slope[0, i].astype(F32)
            if i in (0, RL + 1):
                value = value * jnp.where(index == (0 if i == 0 else SP - 1), 0.0, 1.0).astype(F32)
            else:
                store_taps(pre_taps, i - 1, value)
            outer[0, 2 * k + t] = value.astype(BF)
    halo = halo_rows(even, f_first, f_second)
    field = [halo[1].astype(BF)] + [rows[0, r] for r in range(RL)] + [halo[2].astype(BF)]
    left = jnp.concatenate([jnp.concatenate(field[r : r + 3], axis=0) for r in range(RL)], axis=1)
    right = jnp.concatenate([pre_taps[r] for r in range(RL)], axis=1)
    part_one = dot_nt(left, right)

    @pl.when(lev == 0)
    def _():
        grad_one[...] = part_one

    @pl.when(lev == LEV - 1)
    def _():
        sums[...] = jnp.zeros_like(sums)
        two, one = grad_two[...], grad_one[...] + part_one
        for b in range(3):
            at = b * CP
            sums[b * GR : (b + 1) * GR, 0:C] = two[0:GR, at : at + C]
            sums[b * GR : (b + 1) * GR, C : 2 * C] = one[:, at : at + C]
        sums[0:CP, 2 * C : 3 * C] = two[GR : GR + CP, CP : CP + C]
        packed[...] = modes[...].astype(F32)
        for owner in range(SP):
            packed[owner, 2 * QN : 32] = sums[owner * SHARE : (owner + 1) * SHARE]
        message[...] = packed[...].astype(BF)


def kernel_e_two(inner, outer, slopes, w_one, w_point, after, back, taps, wide):
    lines = [outer[0, 0], outer[0, 1]] + [inner[0, i] for i in range(6)] + [outer[0, 2], outer[0, 3]]
    for i, x in enumerate(lines):
        store_taps(taps, i, x.astype(F32))
    for r in (0, 4):
        d = dot(w_one[...], window(taps, r, 6))
        d = d + dot(w_point[...], slopes[0, r : r + 4].reshape(4 * CP, NC))
        for t in range(4):
            for n in range(0, NC, 128):
                wide[n // 128, pl.ds(r + t, C, stride=RL), :] = d[t * CP : t * CP + C, n : n + 128]
    for n in range(0, NC, 128):
        back[0, :, n : n + 128] = wide[n // 128]


def kernel_f(received, matrix, inverse, back, out, point, one, two, left, packed, sums):
    lev = pl.program_id(0)

    @pl.when(lev == 0)
    def _():
        modes = received[...].reshape(SP * 32, 128)
        r_high, r_low = split(row_expand(modes, matrix[...]))
        r_high, r_low = r_high.astype(F32), r_low.astype(F32)
        rest = jnp.zeros((C, 56), F32)
        for at in range(LEV):
            for r in range(RL):
                h = r_high[at * 64 : at * 64 + C, r * 24 : r * 24 + 24]
                w = r_low[at * 64 : at * 64 + C, r * 24 : r * 24 + 24]
                left[at, pl.ds(r, C, stride=RL), :] = jnp.concatenate([h, h, w, rest], axis=1)
        packed[...] = received[...].astype(F32)
        for owner in range(SP):
            sums[owner * SHARE : (owner + 1) * SHARE] = packed[owner, 2 * QN : 32]
        scaled = sums[...] * (1.0 / math.sqrt(NR * NC * LEV * 4))
        for a in range(3):
            for b in range(3):
                at = (2 - b) * GR + a * CP
                two[a, b] = scaled[at : at + C, 0:C]
                one[a, b] = scaled[at : at + C, C : 2 * C]
        point[...] = scaled[0:C, 2 * C : 3 * C]

    out[0] = (back[0] + dot(left[lev].astype(BF), inverse[...])).astype(BF)


def shape(dims, kind):
    return jax.ShapeDtypeStruct(dims, kind)


def params(mib):
    return pltpu.CompilerParams(vmem_limit_bytes=mib * 1024 * 1024)


def estimate(us):
    if us is None:
        return None
    return pl.CostEstimate(flops=us * 10**9, bytes_accessed=us * 3 * 10**6, transcendentals=0)


def level_spec(*dims):
    return pl.BlockSpec((1,) + dims, lambda lev: (lev,) + (0,) * len(dims))


def whole_spec(*dims):
    return pl.BlockSpec(dims, lambda lev: (0,) * len(dims))


def partners(first, second):
    pairs = [(i, i ^ 1) for i in range(SP)]
    others = [(i, i + 1) for i in range(1, SP - 1, 2)] + [(i + 1, i) for i in range(1, SP - 1, 2)]
    return lax.ppermute(first, "sp", pairs), lax.ppermute(second, "sp", others)


def exchange(x):
    return lax.all_to_all(x, "sp", 0, 0, tiled=True)


def anywhere():
    return pl.BlockSpec(memory_space=pl.ANY)


def plain_call(kernel, operands, after, outs, scratch, mib, name, place=(), cost=None):
    vmem = pl.BlockSpec(memory_space=pltpu.VMEM)
    return pl.pallas_call(
        kernel,
        in_specs=[pl.BlockSpec(memory_space=pltpu.SMEM)] * len(place) + [vmem] * len(operands) + [anywhere()] * len(after),
        out_specs=[vmem] * len(outs),
        out_shape=outs,
        scratch_shapes=scratch,
        compiler_params=params(mib),
        cost_estimate=estimate(cost),
        name=name,
    )(*place, *operands, *after)


def local(field, cotangent, spec_weight, point_weight, kernel_one, kernel_two):
    place = lax.axis_index("sp").astype(jnp.int32).reshape(1)
    inputs = field.reshape(LEV * C * RL, NC)
    table = jnp.asarray(TABLE)
    weight = jnp.transpose(spec_weight, (1, 3, 0, 2)).reshape(C * QN * 2, C)
    strip = shape((LEV, 2 * CO, NC), BF)
    grid_rows = shape((LEV, RL, CP, NC), BF)
    natural = shape((LEV, C * RL, NC), BF)
    flat, cols = pltpu.VMEM((LEV * C * RL, 128), F32), pltpu.VMEM((128, 256), F32)
    row_matrix = shape((SP * 32, 256), BF)
    message, matrix = plain_call(
        kernel_a,
        (inputs, table, *map(jnp.asarray, ROWS + ROWS_TURNED), jnp.asarray(MODE_ROW)),
        (),
        [shape((SP * 32, 128), BF), row_matrix],
        [flat, cols],
        56,
        "field_modes",
        (place,),
    )
    arrived = exchange(message.reshape(SP, 32, 128))
    toeplitz, blocks = shape((4 * CP, 6 * GR), BF), shape((4 * CP, 4 * CP), BF)
    weights_out = [toeplitz] * 4 + [blocks] * 2
    rows, f_first, f_second, cot_rows, w_one, w_two, w_two_back, w_one_back, w_point, w_point_back = pl.pallas_call(
        kernel_rows,
        grid=(LEV,),
        in_specs=[
            pl.BlockSpec(memory_space=pltpu.SMEM),
            level_spec(C * RL, NC),
            level_spec(C * RL, NC),
            whole_spec(3, 3, C, C),
            whole_spec(3, 3, C, C),
            whole_spec(C, C),
            anywhere(),
        ],
        out_specs=[level_spec(RL, CP, NC), level_spec(2 * CO, NC), level_spec(2 * CO, NC), level_spec(RL, CP, NC)]
        + [whole_spec(*x.shape) for x in weights_out],
        out_shape=[grid_rows, strip, strip, grid_rows] + weights_out,
        scratch_shapes=[
            pltpu.VMEM((2, NC // 128, (C + 12) * RL, 128), F32),
            pltpu.VMEM((CP, 9 * CP), F32),
            pltpu.VMEM((4 * CP, 6 * GR), F32),
        ],
        compiler_params=params(56),
        name="row_layout",
    )(place, field.reshape(natural.shape), cotangent.reshape(natural.shape), kernel_one, kernel_two, point_weight, message)
    f_first, f_second = partners(f_first, f_second)

    square, lines = pltpu.VMEM((128, 128), F32), pltpu.VMEM((C * QN * 2, 128), F32)
    mixed, kept = plain_call(
        kernel_mix,
        (arrived, weight),
        (),
        [shape((SP, 32, 128), BF), shape((32, 128), F32)],
        [square, square, square, lines],
        8,
        "mode_mix",
    )
    gathered = exchange(mixed).reshape(SP * 32, 128)

    middle, slope, pre = pl.pallas_call(
        kernel_b,
        grid=(LEV,),
        in_specs=[
            pl.BlockSpec(memory_space=pltpu.SMEM),
            level_spec(RL, CP, NC),
            level_spec(2 * CO, NC),
            level_spec(2 * CO, NC),
            whole_spec(4 * CP, 6 * GR),
            whole_spec(4 * CP, 6 * GR),
            whole_spec(4 * CP, 4 * CP),
        ],
        out_specs=[
            level_spec(RL + 2, CP, NC),
            level_spec(RL + 2, CP, NC),
            level_spec(RL, CO, NC),
        ],
        out_shape=[
            shape((LEV, RL + 2, CP, NC), BF),
            shape((LEV, RL + 2, CP, NC), BF),
            shape((LEV, RL, CO, NC), F32),
        ],
        scratch_shapes=[pltpu.VMEM((RL + 4, GR, NC), BF), pltpu.VMEM((RL + 2, GR, NC), BF)],
        compiler_params=params(56),
        name="two_convolutions",
    )(place, rows, f_first, f_second, w_one, w_two, w_point)

    left, spec = pltpu.VMEM((LEV * RL * CO, 128), F32), pltpu.VMEM((LEV * RL * CO, NC), F32)
    values, slopes, s_first, s_second, message = pl.pallas_call(
        kernel_d,
        grid=(LEV,),
        in_specs=[
            pl.BlockSpec(memory_space=pltpu.SMEM),
            whole_spec(SP * 32, 128),
            whole_spec(SP * 32, 256),
            whole_spec(128, NC),
            level_spec(RL, CO, NC),
            level_spec(RL, CP, NC),
            whole_spec(NC, 128),
            whole_spec(1, 256),
        ],
        out_specs=[level_spec(RL, CP, NC)] * 2 + [level_spec(2 * CO, NC)] * 2 + [whole_spec(SP * 32, 128)],
        out_shape=[grid_rows, grid_rows, strip, strip, shape((SP * 32, 128), BF)],
        scratch_shapes=[
            left,
            pltpu.VMEM((LEV * RL, CO, NC), F32),
            pltpu.VMEM((LEV, RL * CP, 128), F32),
            cols,
        ],
        compiler_params=params(52),
        name="output_and_slope",
    )(place, gathered, matrix, jnp.asarray(INVERSE), pre, cot_rows, table, jnp.asarray(SCALE))
    s_first, s_second = partners(s_first, s_second)

    grad_two, inner = pl.pallas_call(
        kernel_e_zero,
        grid=(LEV,),
        in_specs=[
            level_spec(RL, CP, NC),
            level_spec(RL + 2, CP, NC),
            level_spec(RL, CP, NC),
            level_spec(RL + 2, CP, NC),
            whole_spec(4 * CP, 6 * GR),
        ],
        out_specs=[whole_spec(GR + CP, GR), level_spec(6, CP, NC)],
        out_shape=[shape((GR + CP, GR), F32), shape((LEV, 6, CP, NC), BF)],
        scratch_shapes=[pltpu.VMEM((RL, GR, NC), BF)],
        compiler_params=params(56),
        name="inner_slopes_and_gradients",
    )(slopes, middle, rows, slope, w_two_back)
    outer, message = pl.pallas_call(
        kernel_e,
        grid=(LEV,),
        in_specs=[
            pl.BlockSpec(memory_space=pltpu.SMEM),
            level_spec(RL, CP, NC),
            level_spec(2 * CO, NC),
            level_spec(2 * CO, NC),
            level_spec(RL, CP, NC),
            level_spec(2 * CO, NC),
            level_spec(2 * CO, NC),
            level_spec(RL + 2, CP, NC),
            whole_spec(4 * CP, 6 * GR),
            whole_spec(SP, 32, 128),
            whole_spec(GR + CP, GR),
            level_spec(6, CP, NC),
        ],
        out_specs=[level_spec(4, CP, NC), whole_spec(SP, 32, 128)],
        out_shape=[shape((LEV, 4, CP, NC), BF), shape((SP, 32, 128), BF)],
        scratch_shapes=[
            pltpu.VMEM((RL, GR, NC), BF),
            pltpu.VMEM((RL, GR, NC), BF),
            pltpu.VMEM((GR, GR), F32),
            pltpu.VMEM((SP * SHARE, 128), F32),
            pltpu.VMEM((SP, 32, 128), F32),
        ],
        compiler_params=params(52),
        name="outer_slopes_and_gradients",
    )(place, slopes, s_first, s_second, rows, f_first, f_second, slope, w_two_back, message.reshape(SP, 32, 128), grad_two, inner)
    arrived = exchange(message)
    back = pl.pallas_call(
        kernel_e_two,
        grid=(LEV,),
        in_specs=[
            level_spec(6, CP, NC),
            level_spec(4, CP, NC),
            level_spec(RL, CP, NC),
            whole_spec(4 * CP, 6 * GR),
            whole_spec(4 * CP, 4 * CP),
            anywhere(),
        ],
        out_specs=level_spec(C * RL, NC),
        out_shape=shape(natural.shape, F32),
        scratch_shapes=[pltpu.VMEM((RL + 2, GR, NC), BF), pltpu.VMEM((NC // 128, C * RL, 128), F32)],
        compiler_params=params(56),
        name="backward_convolution",
    )(inner, outer, slopes, w_one_back, w_point_back, message)
    (out,) = plain_call(
        kernel_out,
        (values,),
        (message,),
        [natural],
        [pltpu.VMEM((NC // 128, LEV * C * RL, 128), F32)],
        56,
        "output_layout",
    )
    (sums,) = plain_call(
        kernel_own, (arrived, kept), (), [shape((64, 128), F32)], [], 8, "own_sums"
    )
    others = [lax.ppermute(sums, "rep", [(i, i ^ k) for i in range(4)]) for k in (1, 2, 3)]
    (cofield,) = plain_call(
        kernel_mix_back, (sums, weight), (), [shape((32, 128), BF)], [square, lines], 8, "mode_mix_back"
    )
    (message,) = plain_call(
        kernel_send_back, (cofield, sums, *others), (), [shape((SP, 32, 128), BF)], [], 8, "gradient_modes"
    )
    gathered = exchange(message)
    (spec_grad,) = plain_call(
        kernel_spec_grad,
        (sums, *others),
        (),
        [shape(weight.shape, F32)],
        [pltpu.VMEM((4, 128, 128), F32)] * 2 + [lines],
        8,
        "spectral_gradient",
    )
    kernel_out_shape = shape((3, 3, C, C), F32)
    field_grad, point_total, one_total, two_total = pl.pallas_call(
        kernel_f,
        grid=(LEV,),
        in_specs=[
            whole_spec(SP, 32, 128),
            whole_spec(SP * 32, 256),
            whole_spec(128, NC),
            level_spec(C * RL, NC),
        ],
        out_specs=[level_spec(C * RL, NC), whole_spec(C, C), whole_spec(3, 3, C, C), whole_spec(3, 3, C, C)],
        out_shape=[natural, shape((C, C), F32), kernel_out_shape, kernel_out_shape],
        scratch_shapes=[
            pltpu.VMEM((LEV, C * RL, 128), F32),
            pltpu.VMEM((SP, 32, 128), F32),
            pltpu.VMEM((SP * SHARE, 128), F32),
        ],
        compiler_params=params(52),
        name="field_gradient",
    )(gathered, matrix, jnp.asarray(BACK), back)
    spec_total = jnp.transpose(spec_grad.reshape(C, QN, 2, C), (2, 0, 3, 1))
    return (
        out.reshape(field.shape),
        field_grad.reshape(field.shape),
        spec_total,
        point_total,
        one_total,
        two_total,
    )


def solution(mesh):
    specs = (
        P("rep", None, None, "sp", None),
        P("rep", None, None, "sp", None),
        P(None, None, None, "sp"),
        P(),
        P(),
        P(),
    )
    return jax.shard_map(local, mesh=mesh, in_specs=specs, out_specs=specs, check_vma=False)
```
